32 devices in a mesh: ctx: 8 (over y, x, core), head: 4 (over z).
Axes of the slice: x: 2, y: 2, z: 4, core: 2. Of those that a mesh axis runs over, the one named last changes fastest.
Arguments:
- queries: bfloat16 [4, 8, 8192], P(None, 'ctx', 'head')
- kv_cache: bfloat16 [8, 64, 2, 64, 1024], P(None, 'ctx', None, None, 'head'), may hold values from -6 to 6
- new_kv: bfloat16 [4, 8, 2, 1024], P(None, 'ctx', None, 'head'), may hold values from -6 to 6
- selected: int32 [4, 8, 8, 8], P(None, None, 'head'), may hold values from 0 to 63, as said below
- out_weight: bfloat16 [8192, 8192], P('head', 'ctx'), may hold values from -0.0625 to 0.0625
Outputs:
- mixed: bfloat16 [8, 4, 8192], P('head', None, 'ctx')
The draws below stay inside these ranges and needn't reach their ends.
Inputs may be any that keep to these rules, and one draw needn't show every extreme that they name: Each list selected[s, b, k] names 8 distinct pages; at most 4 of them lie in one aligned block of pages 8 * i to 8 * i + 8 - 1 (the pages of one index of ctx), and exactly 4 in some such block of every list.
All inputs are finite; a program needn't handle non-finite values.
Results may differ from the reference program's by a relative error of at most 0.022.
Values may be sent and summed in bfloat16 or wider, within the bound.
No kernel may reach another device: no remote copies, remote signals or barrier semaphores. Data moves between devices by JAX's collectives and lax.ppermute only.
A program may use at most 128 MiB of HBM per device.

```python
import jax
import jax.numpy as jnp
from jax import lax

HQ = 64
KVH = 8
HD = 128
D = 8192
PAGE = 64
S = 4
P_DEV = 8
CAP = 4
BATCH = 8
PAGES = 64
SEL = 8
N_CTX = 8


def draw_queries(key, part):
    key = jax.random.fold_in(key, 1)
    key_base = jax.random.fold_in(key, 0)
    base = jax.random.normal(key_base, (S, BATCH, HQ * HD), jnp.float32)
    base = jnp.clip(base, -6.0, 6.0)
    return base.astype(jnp.bfloat16)


def draw_selected(key, part):
    key = jax.random.fold_in(key, 2)
    keys = jax.random.split(key, S * BATCH * KVH)

    def one_list(single):
        key_a, key_b, key_c, key_d, key_e = jax.random.split(single, 5)
        hottest = jax.random.randint(key_a, (), 0, N_CTX)
        hot_pages = hottest * P_DEV + jax.random.permutation(key_b, P_DEV)[:CAP]
        others = jax.random.permutation(key_c, N_CTX - 1)[:N_CTX // 2]
        others = jnp.where(others >= hottest, others + 1, others)
        spread = others * P_DEV + jax.random.randint(key_d, (N_CTX // 2,), 0, P_DEV)
        listed = jnp.concatenate([hot_pages, spread]).astype(jnp.int32)
        return jnp.take(listed, jax.random.permutation(key_e, SEL))
    return jax.vmap(one_list)(keys).reshape(S, BATCH, KVH, SEL).astype(jnp.int32)


def block_scale(own_key, shape, shards, smallest, top_value):
    loudness = 1.0
    for position, parts in shards:
        draws = jax.random.uniform(jax.random.fold_in(jax.random.fold_in(own_key, 6), position), (parts,), jnp.float32, smallest / len(shards), top_value / len(shards))
        loudness = loudness * jnp.repeat(jnp.exp(draws), shape[position] // parts).reshape((-1,) + (1,) * (len(shape) - 1 - position))
    return loudness


def centred(stream_key, dims, scale, bound, cuts=(), held_as=jnp.bfloat16):
    drawn = jax.random.normal(stream_key, dims, jnp.float32) * scale
    if len(cuts) > 0:
        drawn = block_scale(stream_key, dims, cuts, -0.22, 0.18) * drawn
    return jnp.clip(drawn, min=-bound, max=bound).astype(held_as)


def setup_inputs(seed: int = 0) -> dict:
    arg_keys = jax.random.split(jax.random.key(seed), 6)
    return {
        "queries": draw_queries(jax.random.fold_in(arg_keys[5], 71), 0),
        "kv_cache": centred(arg_keys[1], (BATCH, PAGES, 2, PAGE, KVH * HD), 1.0, 6.0, ((1, 8), (4, 4))),
        "new_kv": centred(arg_keys[2], (S, BATCH, 2, KVH * HD), 1.0, 6.0, ((1, 8), (3, 4))),
        "selected": draw_selected(jax.random.fold_in(arg_keys[5], 71), 0),
        "out_weight": centred(arg_keys[4], (HQ * HD, D), (HQ * HD) ** -0.5, 0.0625, ((0, 4), (1, 8))),
    }


NEG = -1.0e30


def reference(queries, kv_cache, new_kv, selected, out_weight):
    steps = queries.shape[0]
    batch = queries.shape[1]
    groups = HQ // KVH
    scale = HD ** -0.5
    q_all = queries.reshape(steps, batch, KVH, groups, HD)
    cache = kv_cache.reshape(batch, PAGES, 2, PAGE, KVH, HD)
    new_all = new_kv.reshape(steps, batch, 2, KVH, HD)
    causal = jnp.arange(steps)[None, :] <= jnp.arange(steps)[:, None]

    def one_head(cache_head, chosen, q_head, new_head):
        got = cache_head[chosen]
        keys = got[:, :, 0].reshape(steps, SEL * PAGE, HD).astype(jnp.float32)
        vals = got[:, :, 1].reshape(steps, SEL * PAGE, HD).astype(jnp.float32)
        q_float = q_head.astype(jnp.float32)
        new_float = new_head.astype(jnp.float32)
        old_scores = jnp.einsum('sgd,std->sgt', q_float, keys) * scale
        new_scores = jnp.einsum('sgd,rd->sgr', q_float, new_float[:, 0]) * scale
        new_scores = jnp.where(causal[:, None, :], new_scores, NEG)
        scores = jnp.concatenate([old_scores, new_scores], axis=-1)
        top_score = jnp.max(scores, axis=-1, keepdims=True)
        expo = jnp.exp(scores - top_score)
        total = jnp.sum(expo, axis=-1)
        rounded = expo.astype(jnp.bfloat16).astype(jnp.float32)
        weighted = jnp.einsum('sgt,std->sgd', rounded[..., :SEL * PAGE], vals)
        weighted = weighted + jnp.einsum('sgr,rd->sgd', rounded[..., SEL * PAGE:], new_float[:, 1])
        return weighted / total[..., None]

    def one_seq(index):
        cache_seq = jnp.moveaxis(cache[index], 3, 0)
        chosen = jnp.moveaxis(selected[:, index], 1, 0)
        q_seq = jnp.moveaxis(q_all[:, index], 1, 0)
        new_seq = jnp.moveaxis(new_all[:, index], 2, 0)
        result = jax.vmap(one_head)(cache_seq, chosen, q_seq, new_seq)
        return jnp.moveaxis(result, 0, 1).reshape(steps, HQ * HD).astype(jnp.bfloat16)

    attention = lax.map(one_seq, jnp.arange(batch))
    mixed = jnp.einsum('bsf,fd->bsd', attention.astype(jnp.float32), out_weight.astype(jnp.float32))
    return mixed.astype(jnp.bfloat16)
```

```python
import functools

import jax
import jax.numpy as jnp
from jax import lax
from jax.experimental import pallas as pl
from jax.experimental.pallas import tpu as pltpu
from jax.sharding import PartitionSpec as P

HQ = 64
KVH = 8
HD = 128
PAGE = 64
GROUPS = HQ // KVH
STAT_ROWS = 16
NEG = -1e30
WEIGHT_PIECES = 4
VMEM_LIMIT = 24 * 1024 * 1024

VMEM = pl.BlockSpec(memory_space=pltpu.VMEM)
ANY = pl.BlockSpec(memory_space=pl.ANY)
HBM = pl.BlockSpec(memory_space=pltpu.HBM)
NT = (((1,), (1,)), ((), ()))


def query_rows(q_ref, slot, turned):
    steps, width = q_ref.shape[1:]
    for j in range(width // HD):
        piece = q_ref[slot, :, j * HD : (j + 1) * HD]
        turned[j * steps : (j + 1) * steps, :] = piece.astype(jnp.float32)
    return turned[...].astype(jnp.bfloat16)


def spread_heads(query, heads):
    rows = query.shape[0]
    row_head = lax.broadcasted_iota(jnp.int32, (rows, heads * HD), 0) // (rows // heads)
    lane_head = lax.broadcasted_iota(jnp.int32, (rows, heads * HD), 1) // HD
    wide = jnp.concatenate([query] * heads, axis=1)
    return jnp.where(row_head == lane_head, wide, jnp.zeros_like(wide))


def own_heads(weighted, heads):
    span = weighted.shape[0] // heads
    return jnp.concatenate(
        [weighted[h * span : (h + 1) * span, h * HD : (h + 1) * HD] for h in range(heads)], axis=0
    )


def three_parts(x):
    high = x.astype(jnp.bfloat16).astype(jnp.float32)
    rest = x - high
    middle = rest.astype(jnp.bfloat16).astype(jnp.float32)
    return high, middle, rest - middle


def stat_rows(slots):
    return -(-3 * slots // STAT_ROWS) * STAT_ROWS


def columns_to_rows(columns):
    rows = columns[0].shape[0]
    lane = lax.broadcasted_iota(jnp.int32, (rows, 128), 1)
    sheet = jnp.zeros((rows, 128), jnp.float32)
    for i, column in enumerate(columns):
        sheet = jnp.where(lane == i, column, sheet)
    sheet = jnp.concatenate([sheet, jnp.zeros((128 - rows, 128), jnp.float32)], axis=0)
    turned = jnp.transpose(sheet)
    return [turned[i : i + 1] for i in range(len(columns))]


def rows_to_columns(listed, rows):
    columns = []
    for first in range(0, len(listed), 128):
        some = listed[first : first + 128]
        blank = [jnp.zeros((128 - len(some), 128), jnp.float32)] if len(some) < 128 else []
        turned = jnp.transpose(jnp.concatenate(some + blank, axis=0))
        columns += [turned[:rows, i : i + 1] for i in range(len(some))]
    return columns


def page_masks(bits_ref, seq, steps, page_bit):
    masks = []
    for h in range(bits_ref.shape[1]):
        bits = jnp.concatenate([bits_ref[seq, h]] * (page_bit.shape[1] // 128), axis=1)
        masks += [(page_bit & bits) != 0] * steps
    return jnp.concatenate(masks, axis=0)


def own_kernel(
    q_in, kv_in, selected_in, new_in, q_out, kv_out, bits_out, new_out, selected_ref, new_ref, sems
):
    steps, _, heads, _ = selected_ref.shape
    m, pages = kv_out.shape[:2]
    me = lax.axis_index("ctx")
    pairs = [(selected_in, selected_ref), (new_in, new_ref), (q_in, q_out)]
    pairs += [(kv_in.at[me ^ (2 * i)], kv_out.at[i]) for i in range(m)]
    copies = [pltpu.make_async_copy(*pair, sems.at[i]) for i, pair in enumerate(pairs)]
    for copy in copies:
        copy.start()
    for copy in copies[:2]:
        copy.wait()
    by_step = []
    for s in range(steps):
        lists = jnp.concatenate([selected_ref[s, me ^ (2 * i)] for i in range(m)], axis=0)
        for core in range(2):
            page = lists - (me ^ core) * pages
            here = (page >= 0) & (page < pages)
            bit = jnp.where(here, jnp.left_shift(1, page & 31), 0).astype(jnp.float32)
            total = jnp.sum(bit, axis=1, keepdims=True).astype(jnp.int32)
            by_step.append(jnp.broadcast_to(total, (m * heads, 128)))
    step_of = lax.broadcasted_iota(jnp.int32, (8, 128), 0) % steps
    for core in range(2):
        for i in range(m):
            for h in range(heads):
                row = i * heads + h
                bits = jnp.zeros((8, 128), jnp.int32)
                for s in range(steps):
                    bits = jnp.where(step_of == s, by_step[2 * s + core][row : row + 1], bits)
                bits_out[core, i, h] = bits
    for part in range(2):
        tokens = [new_ref[s, part : part + 1].astype(jnp.float32) for s in range(steps)]
        blank = jnp.zeros((16 - steps, new_ref.shape[2]), jnp.float32)
        new_out[part] = jnp.concatenate(tokens + [blank], axis=0).astype(jnp.bfloat16)
    for copy in copies[2:]:
        copy.wait()


def own_side(queries, kv_cache, selected, new_kv):
    batch, heads = selected.shape[1:3]
    m = batch // 2
    operands = (queries, kv_cache, selected, new_kv)
    return pl.pallas_call(
        own_kernel,
        out_shape=[
            jax.ShapeDtypeStruct(queries.shape, queries.dtype),
            jax.ShapeDtypeStruct((m,) + kv_cache.shape[1:], kv_cache.dtype),
            jax.ShapeDtypeStruct((2, m, heads, 8, 128), jnp.int32),
            jax.ShapeDtypeStruct((2, 16, new_kv.shape[2]), jnp.bfloat16),
        ],
        in_specs=[HBM] * 4,
        out_specs=[VMEM] * 4,
        scratch_shapes=[
            pltpu.VMEM(selected.shape, selected.dtype),
            pltpu.VMEM(new_kv.shape, new_kv.dtype),
            pltpu.SemaphoreType.DMA((3 + m,)),
        ],
        compiler_params=pltpu.CompilerParams(vmem_limit_bytes=VMEM_LIMIT),
        cost_estimate=pl.CostEstimate(
            flops=2**20, bytes_accessed=kv_cache.size * 2, transcendentals=0
        ),
    )(*[pltpu.with_memory_space_constraint(x, pltpu.HBM) for x in operands])


def page_masks(bits_ref, core, i, steps, page_bit):
    masks = []
    for h in range(bits_ref.shape[2]):
        bits = jnp.concatenate([bits_ref[core, i, h]] * (page_bit.shape[1] // 128), axis=1)
        masks += [(page_bit & bits) != 0] * steps
    return jnp.concatenate(masks, axis=0)


def attend(spread, pieces):
    found = []
    for keys, values, allowed in pieces:
        scores = lax.dot_general(spread, keys, NT, preferred_element_type=jnp.float32)
        found.append((allowed, jnp.where(allowed, scores * HD ** (-0.5), NEG), values))

    def finish():
        top = functools.reduce(
            jnp.maximum, [jnp.max(scores, axis=1, keepdims=True) for _, scores, _ in found]
        )
        total, weighted = 0.0, 0.0
        for allowed, scores, values in found:
            expo = jnp.where(allowed, jnp.exp(scores - top), 0.0)
            total = total + jnp.sum(expo, axis=1, keepdims=True)
            weighted = weighted + jnp.dot(
                expo.astype(jnp.bfloat16), values, preferred_element_type=jnp.float32
            )
        return top, total, weighted

    return finish


def page_pieces(kv_ref, where, bits_ref, core, i, steps, heads):
    tokens = kv_ref.shape[1] * PAGE
    page_bit = jnp.left_shift(1, lax.broadcasted_iota(jnp.int32, (8, tokens), 1) // PAGE)
    keys = kv_ref[where, :, 0].reshape(tokens, heads * HD)
    values = kv_ref[where, :, 1].reshape(tokens, heads * HD)
    return keys, values, page_masks(bits_ref, core, i, steps, page_bit)


def staged(count, ahead, begin, end):
    begun = [begin(i) for i in range(min(ahead, count))]
    for i in range(count):
        if i + ahead < count:
            begun.append(begin(i + ahead))
        end(i, begun[i]())


def first_kernel(heads, bits_ref, new_ref, own_ref, *refs):
    *q_refs, spread_ref, sum_ref, stat_ref, turned = refs
    steps = q_refs[0].shape[1]
    rows = turned.shape[1]

    def begin(i):
        spread = spread_heads(query_rows(q_refs[i], 0, turned.at[i]), heads)
        spread_ref[i] = spread
        pieces = [page_pieces(own_ref, i, bits_ref, 0, i, steps, heads)]
        if i == 0:
            step_of = lax.broadcasted_iota(jnp.int32, (rows, 16), 0) % steps
            causal = lax.broadcasted_iota(jnp.int32, (rows, 16), 1) <= step_of
            pieces.append((new_ref[0], new_ref[1], causal))
        return attend(spread, pieces)

    def end(i, state):
        top, total, weighted = state
        lane = lax.broadcasted_iota(jnp.int32, (rows, 128), 1)
        stat_ref[i] = jnp.where(lane == 0, top, total)
        sum_ref[i] = own_heads(weighted, heads)

    staged(len(q_refs), 1, begin, end)


def second_kernel(steps, heads, bits_ref, spread_ref, sum_ref, stat_ref, other_ref, out_ref):
    m, rows = spread_ref.shape[:2]
    me = lax.axis_index("ctx")
    columns = []

    def begin(i):
        pieces = [page_pieces(other_ref, me ^ (2 * i), bits_ref, 1, i, steps, heads)]
        return attend(spread_ref[i], pieces)

    def end(i, state):
        top, total, weighted = state
        stats = stat_ref[i]
        first_top, first_total = stats[:, 0:1], stats[:, 1:2]
        both = jnp.maximum(top, first_top)
        factor, first_factor = jnp.exp(top - both), jnp.exp(first_top - both)
        total = total * factor + first_total * first_factor
        total = jnp.where(total > 0.0, total, 1.0)
        joined = own_heads(weighted, heads) * (factor / total)
        joined = joined + sum_ref[i] * (first_factor / total)
        out_ref[i * rows : (i + 1) * rows, :] = joined.astype(jnp.bfloat16)
        columns.append(both + jnp.log(total))

    staged(m, m if m <= 4 else 2, begin, end)
    count = stat_rows(m)
    stat_row = lax.broadcasted_iota(jnp.int32, (count, 128), 0)
    block = jnp.zeros((count, 128), jnp.float32)
    for i, row in enumerate(columns_to_rows(columns)):
        for j, part in enumerate(three_parts(row)):
            block = jnp.where(stat_row == 3 * i + j, part, block)
    out_ref[m * rows :, :] = block.astype(jnp.bfloat16)


def partials(bits, new_pairs, own_kv, other_kv, queries, rows, heads):
    m, pages = own_kv.shape[:2]
    tokens, width = pages * PAGE, own_kv.shape[4]
    steps = queries[0].shape[1]
    options = dict(
        compiler_params=pltpu.CompilerParams(vmem_limit_bytes=VMEM_LIMIT),
        cost_estimate=pl.CostEstimate(
            flops=4 * m * rows * tokens * width,
            bytes_accessed=2**20,
            transcendentals=m * rows * tokens,
        ),
    )
    state = pl.pallas_call(
        functools.partial(first_kernel, heads),
        out_shape=[
            jax.ShapeDtypeStruct((m, rows, width), jnp.bfloat16),
            jax.ShapeDtypeStruct((m, rows, HD), jnp.float32),
            jax.ShapeDtypeStruct((m, rows, 128), jnp.float32),
        ],
        in_specs=[VMEM] * (3 + m),
        out_specs=[VMEM] * 3,
        scratch_shapes=[pltpu.VMEM((m, rows, HD), jnp.float32)],
        **options,
    )(bits, new_pairs, own_kv, *queries)
    return pl.pallas_call(
        functools.partial(second_kernel, steps, heads),
        out_shape=jax.ShapeDtypeStruct((m * rows + stat_rows(m), HD), jnp.bfloat16),
        in_specs=[VMEM] * 5,
        out_specs=VMEM,
        **options,
    )(bits, *state, other_kv)


def last_merge_kernel(rows, steps, *refs):
    *part_refs, _, out_ref = refs
    m = len(part_refs)
    stats = [ref[m * rows :, :].astype(jnp.float32) for ref in part_refs]
    factors = []
    for i in range(m):
        logs = []
        for j in range(m):
            k = 3 * (i ^ j)
            logs.append(stats[j][k : k + 1] + stats[j][k + 1 : k + 2] + stats[j][k + 2 : k + 3])
        top = functools.reduce(jnp.maximum, logs)
        some = [jnp.exp(x - top) for x in logs]
        total = functools.reduce(jnp.add, some)
        factors += [f / total for f in some]
    columns = rows_to_columns(factors, rows)
    for i in range(m):
        joined = jnp.zeros((rows, HD), jnp.float32)
        for j, ref in enumerate(part_refs):
            span = slice((i ^ j) * rows, ((i ^ j) + 1) * rows)
            joined = joined + columns[i * m + j] * ref[span, :].astype(jnp.float32)
        for j in range(rows // steps):
            piece = joined[j * steps : (j + 1) * steps]
            out_ref[i, :, j * HD : (j + 1) * HD] = piece.astype(jnp.bfloat16)


def last_merge(parts, weight, rows, steps):
    m = len(parts)
    return pl.pallas_call(
        functools.partial(last_merge_kernel, rows, steps),
        out_shape=jax.ShapeDtypeStruct((m, steps, rows // steps * HD), jnp.bfloat16),
        in_specs=[VMEM] * m + [ANY],
        out_specs=VMEM,
        compiler_params=pltpu.CompilerParams(vmem_limit_bytes=VMEM_LIMIT),
        cost_estimate=pl.CostEstimate(
            flops=2 * m * m * rows * HD, bytes_accessed=2**18, transcendentals=0
        ),
    )(*parts, weight)


def load_kernel(weight_ref, _, out_ref, sems):
    piece = out_ref.shape[0] // WEIGHT_PIECES
    copies = []
    for i in range(WEIGHT_PIECES):
        span = pl.ds(i * piece, piece)
        copy = pltpu.make_async_copy(weight_ref.at[span], out_ref.at[span], sems.at[i])
        copy.start()
        copies.append(copy)
    for copy in copies:
        copy.wait()


def load_weight(out_weight, after):
    return pl.pallas_call(
        load_kernel,
        out_shape=jax.ShapeDtypeStruct(out_weight.shape, out_weight.dtype),
        in_specs=[HBM, ANY],
        out_specs=VMEM,
        scratch_shapes=[pltpu.SemaphoreType.DMA((WEIGHT_PIECES,))],
        compiler_params=pltpu.CompilerParams(vmem_limit_bytes=VMEM_LIMIT),
        cost_estimate=pl.CostEstimate(
            flops=0, bytes_accessed=out_weight.size * 4, transcendentals=0
        ),
    )(pltpu.with_memory_space_constraint(out_weight, pltpu.HBM), after)


def project_rows(att_ref, weight_ref, lhs):
    count, _, width = lhs.shape
    steps = att_ref.shape[1]
    lhs[...] = jnp.zeros_like(lhs)
    for i in range(count):
        lhs[i, :steps, :] = att_ref[i].astype(jnp.float32)
    left = lhs[...].reshape(count * 8, width).astype(jnp.bfloat16)
    product = jnp.dot(left, weight_ref[...], preferred_element_type=jnp.float32)
    return product.reshape(count, 8, weight_ref.shape[1])


def half_kernel(att_ref, weight_ref, out_ref, lhs):
    out_ref[...] = project_rows(att_ref, weight_ref, lhs)


def project_kernel(n_head, targets, att_ref, half_ref, weight_ref, *refs):
    lhs, rows_all = refs[-2:]
    out_refs = refs[:-2]
    m, steps, _ = att_ref.shape
    seqs = 2 * m // n_head
    me = lax.axis_index("ctx")
    mine = lax.axis_index("head")
    product = project_rows(att_ref, weight_ref, lhs)
    for i in range(m):
        rows_all[2 * i] = product[i]
        rows_all[2 * i + 1] = half_ref[i]
    for k, ref in enumerate(out_refs):
        target = mine
        if k > 0:
            for core, row in enumerate(targets[k - 1]):
                for z, t in enumerate(row):
                    target = jnp.where((me % 2 == core) & (mine == z), t, target)
        for j in range(seqs):
            found = rows_all[(jnp.maximum(target, 0) * seqs + j) ^ me][:steps]
            if k > 0 and any(t < 0 for row in targets[k - 1] for t in row):
                found = jnp.where(target < 0, 0.0, found)
            ref[j] = found.astype(ref.dtype)


def project_options(att, weight):
    m, _, width = att.shape
    columns = weight.shape[1]
    return dict(
        compiler_params=pltpu.CompilerParams(vmem_limit_bytes=VMEM_LIMIT),
        cost_estimate=pl.CostEstimate(
            flops=2 * m * 8 * width * columns,
            bytes_accessed=width * columns * 2,
            transcendentals=0,
        ),
    )


def project_half(att, weight):
    m, _, width = att.shape
    return pl.pallas_call(
        half_kernel,
        out_shape=jax.ShapeDtypeStruct((m, 8, weight.shape[1]), jnp.float32),
        in_specs=[VMEM] * 2,
        out_specs=VMEM,
        scratch_shapes=[pltpu.VMEM((m, 8, width), jnp.float32)],
        **project_options(att, weight),
    )(att, weight)


def project(att, half, weight, n_head, targets):
    m, steps, width = att.shape
    n = 2 * m
    columns = weight.shape[1]
    outs = [
        jax.ShapeDtypeStruct((n // n_head, steps, columns), jnp.bfloat16 if k else jnp.float32)
        for k in range(1 + len(targets))
    ]
    return pl.pallas_call(
        functools.partial(project_kernel, n_head, targets),
        out_shape=outs,
        in_specs=[VMEM] * 3,
        out_specs=[VMEM] * len(outs),
        scratch_shapes=[
            pltpu.VMEM((m, 8, width), jnp.float32),
            pltpu.VMEM((n, 8, columns), jnp.float32),
        ],
        **project_options(att, weight),
    )(att, half, weight)


def head_plan(n_head):
    if n_head == 4:
        return [
            (((0, 1), (1, 1), (0, 3), (0, 0)), ((1, 2), (1, 3), (0, 2), (1, 0))),
            (((1, 0), (0, 2), (0, 0), (0, 1)), ((1, 1), (1, 2), (1, 3), (0, 3))),
            (((0, 3), (0, 0), (1, 2), (0, 2)), ((1, 3), (0, 1), (1, 0), (1, 1))),
            (((0, 2), (0, 3), (0, 1), (1, 3)), ((0, 0), (1, 0), (1, 1), (1, 2))),
        ]
    return [
        tuple(tuple((core, (z + t) % n_head) for z in range(n_head)) for core in range(2))
        for t in range(1, n_head)
    ]


def plan_targets(plan):
    seen = set()
    targets = []
    for permutation in plan:
        rows = []
        for core, row in enumerate(permutation):
            rows.append([])
            for z, (to_core, t) in enumerate(row):
                useful = to_core == core and (core, z, t) not in seen
                rows[core].append(t if useful else -1)
                if useful:
                    seen.add((core, z, t))
        targets.append(rows)
    return targets


def send_by(permutation, x):
    n, n_head = lax.axis_size("ctx"), lax.axis_size("head")
    pairs = []
    for c in range(n):
        for z in range(n_head):
            core, t = permutation[c % 2][z]
            pairs.append((c * n_head + z, (c - c % 2 + core) * n_head + t))
    return lax.ppermute(x, ("ctx", "head"), pairs)


def swap(x, axis, r):
    size = lax.axis_size(axis)
    return lax.ppermute(x, axis, [(i, i ^ r) for i in range(size)])


def swap_chips(x, n):
    return [swap(x, "ctx", r) for r in range(2, n, 2)]


def swap_other_cores(x, n):
    return [swap(x, "ctx", r) for r in range(1, n, 2)]


def local(queries, kv_cache, new_kv, selected, out_weight):
    steps, _, width = queries.shape
    heads = kv_cache.shape[4] // HD
    rows = steps * heads * GROUPS
    n = lax.axis_size("ctx")
    n_head = lax.axis_size("head")

    first_q = queries.reshape(1, steps, width)
    other_kv = swap(kv_cache, "ctx", 1)
    far_q = swap_chips(first_q, n)
    new_pairs = new_kv.reshape(steps, 2, heads * HD)
    own_q, own_kv, bits, new_pairs = own_side(first_q, kv_cache, selected, new_pairs)
    all_q = [own_q] + far_q
    sent = partials(bits, new_pairs, own_kv, other_kv, all_q, rows, heads)
    parts = swap_other_cores(sent, n)
    weight = load_weight(out_weight, sent)
    odd_att = last_merge(parts, weight, rows, steps)
    even_att = swap(odd_att, "ctx", 1)
    plan = head_plan(n_head)
    half = project_half(odd_att, weight)
    total, *rows_out = project(even_att, half, weight, n_head, plan_targets(plan))
    for chunk, permutation in zip(rows_out, plan):
        total = total + send_by(permutation, chunk).astype(jnp.float32)
    return total.astype(jnp.bfloat16)


def solution(mesh):
    return jax.shard_map(
        local,
        mesh=mesh,
        in_specs=(
            P(None, "ctx", "head"),
            P(None, "ctx", None, None, "head"),
            P(None, "ctx", None, "head"),
            P(None, None, "head", None),
            P("head", "ctx"),
        ),
        out_specs=P("head", None, "ctx"),
        check_vma=False,
    )
```

```python
import functools

import jax
import jax.numpy as jnp
from jax import lax
from jax.experimental import pallas as pl
from jax.experimental.pallas import tpu as pltpu
from jax.sharding import PartitionSpec as P

HQ = 64
KVH = 8
HD = 128
PAGE = 64
GROUPS = HQ // KVH
STAT_ROWS = 16
NEG = -1e30
WEIGHT_PIECES = 4
VMEM_LIMIT = 24 * 1024 * 1024

VMEM = pl.BlockSpec(memory_space=pltpu.VMEM)
ANY = pl.BlockSpec(memory_space=pl.ANY)
HBM = pl.BlockSpec(memory_space=pltpu.HBM)
NT = (((1,), (1,)), ((), ()))


def query_rows(q_ref, slot, turned):
    steps, width = q_ref.shape[1:]
    for j in range(width // HD):
        piece = q_ref[slot, :, j * HD : (j + 1) * HD]
        turned[j * steps : (j + 1) * steps, :] = piece.astype(jnp.float32)
    return turned[...].astype(jnp.bfloat16)


def spread_heads(query, heads):
    rows = query.shape[0]
    row_head = lax.broadcasted_iota(jnp.int32, (rows, heads * HD), 0) // (rows // heads)
    lane_head = lax.broadcasted_iota(jnp.int32, (rows, heads * HD), 1) // HD
    wide = jnp.concatenate([query] * heads, axis=1)
    return jnp.where(row_head == lane_head, wide, jnp.zeros_like(wide))


def own_heads(weighted, heads):
    span = weighted.shape[0] // heads
    return jnp.concatenate(
        [weighted[h * span : (h + 1) * span, h * HD : (h + 1) * HD] for h in range(heads)], axis=0
    )


def three_parts(x):
    high = x.astype(jnp.bfloat16).astype(jnp.float32)
    rest = x - high
    middle = rest.astype(jnp.bfloat16).astype(jnp.float32)
    return high, middle, rest - middle


def stat_rows(slots):
    return -(-3 * slots // STAT_ROWS) * STAT_ROWS


def columns_to_rows(columns):
    rows = columns[0].shape[0]
    lane = lax.broadcasted_iota(jnp.int32, (rows, 128), 1)
    sheet = jnp.zeros((rows, 128), jnp.float32)
    for i, column in enumerate(columns):
        sheet = jnp.where(lane == i, column, sheet)
    sheet = jnp.concatenate([sheet, jnp.zeros((128 - rows, 128), jnp.float32)], axis=0)
    turned = jnp.transpose(sheet)
    return [turned[i : i + 1] for i in range(len(columns))]


def rows_to_columns(listed, rows):
    columns = []
    for first in range(0, len(listed), 128):
        some = listed[first : first + 128]
        blank = [jnp.zeros((128 - len(some), 128), jnp.float32)] if len(some) < 128 else []
        turned = jnp.transpose(jnp.concatenate(some + blank, axis=0))
        columns += [turned[:rows, i : i + 1] for i in range(len(some))]
    return columns


def page_masks(bits_ref, seq, steps, page_bit):
    masks = []
    for h in range(bits_ref.shape[1]):
        bits = jnp.concatenate([bits_ref[seq, h]] * (page_bit.shape[1] // 128), axis=1)
        masks += [(page_bit & bits) != 0] * steps
    return jnp.concatenate(masks, axis=0)


def own_kernel(
    q_in, kv_in, selected_in, new_in, q_out, kv_out, bits_out, new_out, selected_ref, new_ref, sems
):
    steps, _, heads, _ = selected_ref.shape
    m, pages = kv_out.shape[:2]
    me = lax.axis_index("ctx")
    pairs = [(selected_in, selected_ref), (new_in, new_ref), (q_in, q_out)]
    pairs += [(kv_in.at[me ^ (2 * i)], kv_out.at[i]) for i in range(m)]
    copies = [pltpu.make_async_copy(*pair, sems.at[i]) for i, pair in enumerate(pairs)]
    for copy in copies:
        copy.start()
    for copy in copies[:2]:
        copy.wait()
    by_step = []
    for s in range(steps):
        lists = jnp.concatenate([selected_ref[s, me ^ (2 * i)] for i in range(m)], axis=0)
        for core in range(2):
            page = lists - (me ^ core) * pages
            here = (page >= 0) & (page < pages)
            bit = jnp.where(here, jnp.left_shift(1, page & 31), 0).astype(jnp.float32)
            total = jnp.sum(bit, axis=1, keepdims=True).astype(jnp.int32)
            by_step.append(jnp.broadcast_to(total, (m * heads, 128)))
    step_of = lax.broadcasted_iota(jnp.int32, (8, 128), 0) % steps
    for core in range(2):
        for i in range(m):
            for h in range(heads):
                row = i * heads + h
                bits = jnp.zeros((8, 128), jnp.int32)
                for s in range(steps):
                    bits = jnp.where(step_of == s, by_step[2 * s + core][row : row + 1], bits)
                bits_out[core, i, h] = bits
    for part in range(2):
        tokens = [new_ref[s, part : part + 1].astype(jnp.float32) for s in range(steps)]
        blank = jnp.zeros((16 - steps, new_ref.shape[2]), jnp.float32)
        new_out[part] = jnp.concatenate(tokens + [blank], axis=0).astype(jnp.bfloat16)
    for copy in copies[2:]:
        copy.wait()


def own_side(queries, kv_cache, selected, new_kv):
    batch, heads = selected.shape[1:3]
    m = batch // 2
    operands = (queries, kv_cache, selected, new_kv)
    return pl.pallas_call(
        own_kernel,
        out_shape=[
            jax.ShapeDtypeStruct(queries.shape, queries.dtype),
            jax.ShapeDtypeStruct((m,) + kv_cache.shape[1:], kv_cache.dtype),
            jax.ShapeDtypeStruct((2, m, heads, 8, 128), jnp.int32),
            jax.ShapeDtypeStruct((2, 16, new_kv.shape[2]), jnp.bfloat16),
        ],
        in_specs=[HBM] * 4,
        out_specs=[VMEM] * 4,
        scratch_shapes=[
            pltpu.VMEM(selected.shape, selected.dtype),
            pltpu.VMEM(new_kv.shape, new_kv.dtype),
            pltpu.SemaphoreType.DMA((3 + m,)),
        ],
        compiler_params=pltpu.CompilerParams(vmem_limit_bytes=VMEM_LIMIT),
        cost_estimate=pl.CostEstimate(
            flops=2**20, bytes_accessed=kv_cache.size * 2, transcendentals=0
        ),
    )(*[pltpu.with_memory_space_constraint(x, pltpu.HBM) for x in operands])


def page_masks(bits_ref, core, i, steps, page_bit):
    masks = []
    for h in range(bits_ref.shape[2]):
        bits = jnp.concatenate([bits_ref[core, i, h]] * (page_bit.shape[1] // 128), axis=1)
        masks += [(page_bit & bits) != 0] * steps
    return jnp.concatenate(masks, axis=0)


def attend(spread, pieces):
    found = []
    for keys, values, allowed in pieces:
        scores = lax.dot_general(spread, keys, NT, preferred_element_type=jnp.float32)
        found.append((allowed, jnp.where(allowed, scores * HD ** (-0.5), NEG), values))

    def finish():
        top = functools.reduce(
            jnp.maximum, [jnp.max(scores, axis=1, keepdims=True) for _, scores, _ in found]
        )
        total, weighted = 0.0, 0.0
        for allowed, scores, values in found:
            expo = jnp.where(allowed, jnp.exp(scores - top), 0.0)
            total = total + jnp.sum(expo, axis=1, keepdims=True)
            weighted = weighted + jnp.dot(
                expo.astype(jnp.bfloat16), values, preferred_element_type=jnp.float32
            )
        return top, total, weighted

    return finish


def page_pieces(kv_ref, where, bits_ref, core, i, steps, heads):
    tokens = kv_ref.shape[1] * PAGE
    page_bit = jnp.left_shift(1, lax.broadcasted_iota(jnp.int32, (8, tokens), 1) // PAGE)
    keys = kv_ref[where, :, 0].reshape(tokens, heads * HD)
    values = kv_ref[where, :, 1].reshape(tokens, heads * HD)
    return keys, values, page_masks(bits_ref, core, i, steps, page_bit)


def staged(count, ahead, begin, end):
    begun = [begin(i) for i in range(min(ahead, count))]
    for i in range(count):
        if i + ahead < count:
            begun.append(begin(i + ahead))
        end(i, begun[i]())


def first_kernel(heads, bits_ref, new_ref, own_ref, *refs):
    *q_refs, spread_ref, sum_ref, stat_ref, turned = refs
    steps = q_refs[0].shape[1]
    rows = turned.shape[1]

    def begin(i):
        spread = spread_heads(query_rows(q_refs[i], 0, turned.at[i]), heads)
        spread_ref[i] = spread
        pieces = [page_pieces(own_ref, i, bits_ref, 0, i, steps, heads)]
        if i == 0:
            step_of = lax.broadcasted_iota(jnp.int32, (rows, 16), 0) % steps
            causal = lax.broadcasted_iota(jnp.int32, (rows, 16), 1) <= step_of
            pieces.append((new_ref[0], new_ref[1], causal))
        return attend(spread, pieces)

    def end(i, state):
        top, total, weighted = state
        lane = lax.broadcasted_iota(jnp.int32, (rows, 128), 1)
        stat_ref[i] = jnp.where(lane == 0, top, total)
        sum_ref[i] = own_heads(weighted, heads)

    staged(len(q_refs), 1, begin, end)


def second_kernel(steps, heads, bits_ref, spread_ref, sum_ref, stat_ref, other_ref, out_ref):
    m, rows = spread_ref.shape[:2]
    me = lax.axis_index("ctx")
    columns = []

    def begin(i):
        pieces = [page_pieces(other_ref, me ^ (2 * i), bits_ref, 1, i, steps, heads)]
        return attend(spread_ref[i], pieces)

    def end(i, state):
        top, total, weighted = state
        stats = stat_ref[i]
        first_top, first_total = stats[:, 0:1], stats[:, 1:2]
        both = jnp.maximum(top, first_top)
        factor, first_factor = jnp.exp(top - both), jnp.exp(first_top - both)
        total = total * factor + first_total * first_factor
        total = jnp.where(total > 0.0, total, 1.0)
        joined = own_heads(weighted, heads) * (factor / total)
        joined = joined + sum_ref[i] * (first_factor / total)
        out_ref[i * rows : (i + 1) * rows, :] = joined.astype(jnp.bfloat16)
        columns.append(both + jnp.log(total))

    staged(m, m if m <= 4 else 2, begin, end)
    count = stat_rows(m)
    stat_row = lax.broadcasted_iota(jnp.int32, (count, 128), 0)
    block = jnp.zeros((count, 128), jnp.float32)
    for i, row in enumerate(columns_to_rows(columns)):
        for j, part in enumerate(three_parts(row)):
            block = jnp.where(stat_row == 3 * i + j, part, block)
    out_ref[m * rows :, :] = block.astype(jnp.bfloat16)


def partials(bits, new_pairs, own_kv, other_kv, queries, rows, heads):
    m, pages = own_kv.shape[:2]
    tokens, width = pages * PAGE, own_kv.shape[4]
    steps = queries[0].shape[1]
    options = dict(
        compiler_params=pltpu.CompilerParams(vmem_limit_bytes=VMEM_LIMIT),
        cost_estimate=pl.CostEstimate(
            flops=4 * m * rows * tokens * width,
            bytes_accessed=2**20,
            transcendentals=m * rows * tokens,
        ),
    )
    state = pl.pallas_call(
        functools.partial(first_kernel, heads),
        out_shape=[
            jax.ShapeDtypeStruct((m, rows, width), jnp.bfloat16),
            jax.ShapeDtypeStruct((m, rows, HD), jnp.float32),
            jax.ShapeDtypeStruct((m, rows, 128), jnp.float32),
        ],
        in_specs=[VMEM] * (3 + m),
        out_specs=[VMEM] * 3,
        scratch_shapes=[pltpu.VMEM((m, rows, HD), jnp.float32)],
        **options,
    )(bits, new_pairs, own_kv, *queries)
    return pl.pallas_call(
        functools.partial(second_kernel, steps, heads),
        out_shape=jax.ShapeDtypeStruct((m * rows + stat_rows(m), HD), jnp.bfloat16),
        in_specs=[VMEM] * 5,
        out_specs=VMEM,
        **options,
    )(bits, *state, other_kv)


def last_merge_kernel(rows, steps, chips, *refs):
    *part_refs, _, out_ref = refs
    m = len(part_refs)
    stats = [ref[m * rows :, :].astype(jnp.float32) for ref in part_refs]
    core = lax.axis_index("ctx") % 2

    def stat_of(k, slot):
        return stats[k][3 * slot : 3 * slot + 1] + stats[k][3 * slot + 1 : 3 * slot + 2] + (
            stats[k][3 * slot + 2 : 3 * slot + 3]
        )

    factors = []
    for i in range(m):
        logs = []
        for k in range(m):
            even, odd = i ^ chips[0][k], i ^ chips[1][k]
            log = stat_of(k, even)
            logs.append(log if even == odd else jnp.where(core == 0, log, stat_of(k, odd)))
        top = functools.reduce(jnp.maximum, logs)
        some = [jnp.exp(x - top) for x in logs]
        total = functools.reduce(jnp.add, some)
        factors += [f / total for f in some]
    columns = rows_to_columns(factors, rows)
    for i in range(m):
        joined = jnp.zeros((rows, HD), jnp.float32)
        for k, ref in enumerate(part_refs):
            even, odd = i ^ chips[0][k], i ^ chips[1][k]
            first = even * rows
            if even != odd:
                first = pl.multiple_of(jnp.where(core == 0, even, odd) * rows, rows)
            joined = joined + columns[i * m + k] * ref[pl.ds(first, rows), :].astype(jnp.float32)
        for j in range(rows // steps):
            piece = joined[j * steps : (j + 1) * steps]
            out_ref[i, :, j * HD : (j + 1) * HD] = piece.astype(jnp.bfloat16)


def last_merge(parts, weight, rows, steps, chips):
    m = len(parts)
    return pl.pallas_call(
        functools.partial(last_merge_kernel, rows, steps, chips),
        out_shape=jax.ShapeDtypeStruct((m, steps, rows // steps * HD), jnp.bfloat16),
        in_specs=[VMEM] * m + [ANY],
        out_specs=VMEM,
        compiler_params=pltpu.CompilerParams(vmem_limit_bytes=VMEM_LIMIT),
        cost_estimate=pl.CostEstimate(
            flops=2 * m * m * rows * HD, bytes_accessed=2**18, transcendentals=0
        ),
    )(*parts, weight)


def load_kernel(weight_ref, _, out_ref, sems):
    piece = out_ref.shape[0] // WEIGHT_PIECES
    copies = []
    for i in range(WEIGHT_PIECES):
        span = pl.ds(i * piece, piece)
        copy = pltpu.make_async_copy(weight_ref.at[span], out_ref.at[span], sems.at[i])
        copy.start()
        copies.append(copy)
    for copy in copies:
        copy.wait()


def load_weight(out_weight, after):
    return pl.pallas_call(
        load_kernel,
        out_shape=jax.ShapeDtypeStruct(out_weight.shape, out_weight.dtype),
        in_specs=[HBM, ANY],
        out_specs=VMEM,
        scratch_shapes=[pltpu.SemaphoreType.DMA((WEIGHT_PIECES,))],
        compiler_params=pltpu.CompilerParams(vmem_limit_bytes=VMEM_LIMIT),
        cost_estimate=pl.CostEstimate(
            flops=0, bytes_accessed=out_weight.size * 4, transcendentals=0
        ),
    )(pltpu.with_memory_space_constraint(out_weight, pltpu.HBM), after)


def project_rows(att_ref, weight_ref, lhs):
    count, _, width = lhs.shape
    steps = att_ref.shape[1]
    lhs[...] = jnp.zeros_like(lhs)
    for i in range(count):
        lhs[i, :steps, :] = att_ref[i].astype(jnp.float32)
    left = lhs[...].reshape(count * 8, width).astype(jnp.bfloat16)
    product = jnp.dot(left, weight_ref[...], preferred_element_type=jnp.float32)
    return product.reshape(count, 8, weight_ref.shape[1])


def half_kernel(att_ref, weight_ref, out_ref, lhs):
    out_ref[...] = project_rows(att_ref, weight_ref, lhs)


def project_kernel(n_head, targets, att_ref, half_ref, weight_ref, *refs):
    lhs, rows_all = refs[-2:]
    out_refs = refs[:-2]
    m, steps, _ = att_ref.shape
    seqs = 2 * m // n_head
    me = lax.axis_index("ctx")
    mine = lax.axis_index("head")
    product = project_rows(att_ref, weight_ref, lhs)
    for i in range(m):
        rows_all[2 * i] = product[i]
        rows_all[2 * i + 1] = half_ref[i]
    for k, ref in enumerate(out_refs):
        target = mine
        if k > 0:
            for core, row in enumerate(targets[k - 1]):
                for z, t in enumerate(row):
                    target = jnp.where((me % 2 == core) & (mine == z), t, target)
        for j in range(seqs):
            found = rows_all[(jnp.maximum(target, 0) * seqs + j) ^ me][:steps]
            if k > 0 and any(t < 0 for row in targets[k - 1] for t in row):
                found = jnp.where(target < 0, 0.0, found)
            ref[j] = found.astype(ref.dtype)


def project_options(att, weight):
    m, _, width = att.shape
    columns = weight.shape[1]
    return dict(
        compiler_params=pltpu.CompilerParams(vmem_limit_bytes=VMEM_LIMIT),
        cost_estimate=pl.CostEstimate(
            flops=2 * m * 8 * width * columns,
            bytes_accessed=width * columns * 2,
            transcendentals=0,
        ),
    )


def project_half(att, weight):
    m, _, width = att.shape
    return pl.pallas_call(
        half_kernel,
        out_shape=jax.ShapeDtypeStruct((m, 8, weight.shape[1]), jnp.float32),
        in_specs=[VMEM] * 2,
        out_specs=VMEM,
        scratch_shapes=[pltpu.VMEM((m, 8, width), jnp.float32)],
        **project_options(att, weight),
    )(att, weight)


def project(att, half, weight, n_head, targets):
    m, steps, width = att.shape
    n = 2 * m
    columns = weight.shape[1]
    outs = [
        jax.ShapeDtypeStruct((n // n_head, steps, columns), jnp.bfloat16 if k else jnp.float32)
        for k in range(1 + len(targets))
    ]
    return pl.pallas_call(
        functools.partial(project_kernel, n_head, targets),
        out_shape=outs,
        in_specs=[VMEM] * 3,
        out_specs=[VMEM] * len(outs),
        scratch_shapes=[
            pltpu.VMEM((m, 8, width), jnp.float32),
            pltpu.VMEM((n, 8, columns), jnp.float32),
        ],
        **project_options(att, weight),
    )(att, half, weight)


def head_plan(n_head):
    if n_head == 4:
        return [
            (((0, 1), (1, 1), (0, 3), (0, 0)), ((1, 2), (1, 3), (0, 2), (1, 0))),
            (((1, 0), (0, 2), (0, 0), (0, 1)), ((1, 1), (1, 2), (1, 3), (0, 3))),
            (((0, 3), (0, 0), (1, 2), (0, 2)), ((1, 3), (0, 1), (1, 0), (1, 1))),
            (((0, 2), (0, 3), (0, 1), (1, 3)), ((0, 0), (1, 0), (1, 1), (1, 2))),
        ]
    return [
        tuple(tuple((core, (z + t) % n_head) for z in range(n_head)) for core in range(2))
        for t in range(1, n_head)
    ]


def plan_targets(plan):
    seen = set()
    targets = []
    for permutation in plan:
        rows = []
        for core, row in enumerate(permutation):
            rows.append([])
            for z, (to_core, t) in enumerate(row):
                useful = to_core == core and (core, z, t) not in seen
                rows[core].append(t if useful else -1)
                if useful:
                    seen.add((core, z, t))
        targets.append(rows)
    return targets


def send_by(permutation, x):
    n, n_head = lax.axis_size("ctx"), lax.axis_size("head")
    pairs = []
    for c in range(n):
        for z in range(n_head):
            core, t = permutation[c % 2][z]
            pairs.append((c * n_head + z, (c - c % 2 + core) * n_head + t))
    return lax.ppermute(x, ("ctx", "head"), pairs)


def swap(x, axis, r):
    size = lax.axis_size(axis)
    return lax.ppermute(x, axis, [(i, i ^ r) for i in range(size)])


def swap_chips(x, n):
    return [swap(x, "ctx", r) for r in range(2, n, 2)]


def swap_other_cores(x, n):
    sends = [list(range(1, n, 2))] * 2
    if n == 8:
        sends = [[1, 3, 5, 7], [1, 5, 3, 7]]
    got = []
    for even, odd in zip(*sends):
        pairs = [(i, i ^ (odd if i % 2 else even)) for i in range(n)]
        got.append(lax.ppermute(x, "ctx", pairs))
    return got, [[r // 2 for r in sends[1]], [r // 2 for r in sends[0]]]


def local(queries, kv_cache, new_kv, selected, out_weight):
    steps, _, width = queries.shape
    heads = kv_cache.shape[4] // HD
    rows = steps * heads * GROUPS
    n = lax.axis_size("ctx")
    n_head = lax.axis_size("head")

    first_q = queries.reshape(1, steps, width)
    other_kv = swap(kv_cache, "ctx", 1)
    far_q = swap_chips(first_q, n)
    new_pairs = new_kv.reshape(steps, 2, heads * HD)
    own_q, own_kv, bits, new_pairs = own_side(first_q, kv_cache, selected, new_pairs)
    all_q = [own_q] + far_q
    sent = partials(bits, new_pairs, own_kv, other_kv, all_q, rows, heads)
    parts, chips = swap_other_cores(sent, n)
    weight = load_weight(out_weight, sent)
    odd_att = last_merge(parts, weight, rows, steps, chips)
    even_att = swap(odd_att, "ctx", 1)
    plan = head_plan(n_head)
    half = project_half(odd_att, weight)
    total, *rows_out = project(even_att, half, weight, n_head, plan_targets(plan))
    for chunk, permutation in zip(rows_out, plan):
        total = total + send_by(permutation, chunk).astype(jnp.float32)
    return total.astype(jnp.bfloat16)


def solution(mesh):
    return jax.shard_map(
        local,
        mesh=mesh,
        in_specs=(
            P(None, "ctx", "head"),
            P(None, "ctx", None, None, "head"),
            P(None, "ctx", None, "head"),
            P(None, None, "head", None),
            P("head", "ctx"),
        ),
        out_specs=P("head", None, "ctx"),
        check_vma=False,
    )
```

```python
import functools

import jax
import jax.numpy as jnp
from jax import lax
from jax.experimental import pallas as pl
from jax.experimental.pallas import tpu as pltpu
from jax.sharding import PartitionSpec as P

HQ = 64
KVH = 8
HD = 128
PAGE = 64
GROUPS = HQ // KVH
STAT_ROWS = 16
MASKED = -3e38
FLOOR = -1.5e38
WEIGHT_PIECES = 4
VMEM_LIMIT = 24 * 1024 * 1024

VMEM = pl.BlockSpec(memory_space=pltpu.VMEM)
ANY = pl.BlockSpec(memory_space=pl.ANY)
HBM = pl.BlockSpec(memory_space=pltpu.HBM)
NT = (((1,), (1,)), ((), ()))


def query_rows(q_ref, slot, turned):
    steps, width = q_ref.shape[1:]
    for j in range(width // HD):
        piece = q_ref[slot, :, j * HD : (j + 1) * HD]
        turned[j * steps : (j + 1) * steps, :] = piece.astype(jnp.float32)
    return turned[...].astype(jnp.bfloat16)


def spread_heads(query, heads):
    rows = query.shape[0]
    row_head = lax.broadcasted_iota(jnp.int32, (rows, heads * HD), 0) // (rows // heads)
    lane_head = lax.broadcasted_iota(jnp.int32, (rows, heads * HD), 1) // HD
    wide = jnp.concatenate([query] * heads, axis=1)
    return jnp.where(row_head == lane_head, wide, jnp.zeros_like(wide))


def own_heads(weighted, heads):
    span = weighted.shape[0] // heads
    return jnp.concatenate(
        [weighted[h * span : (h + 1) * span, h * HD : (h + 1) * HD] for h in range(heads)], axis=0
    )


def three_parts(x):
    high = x.astype(jnp.bfloat16).astype(jnp.float32)
    rest = x - high
    middle = rest.astype(jnp.bfloat16).astype(jnp.float32)
    return high, middle, rest - middle


def stat_rows(slots):
    return -(-3 * slots // STAT_ROWS) * STAT_ROWS


def stat_block(columns):
    rows = columns[0].shape[0]
    lane = lax.broadcasted_iota(jnp.int32, (rows, 128), 1)
    sheet = jnp.zeros((rows, 128), jnp.float32)
    for i, column in enumerate(columns):
        sheet = jnp.where(lane == i, column, sheet)
    sheet = jnp.concatenate([sheet, jnp.zeros((128 - rows, 128), jnp.float32)], axis=0)
    count = len(columns)
    parts = list(three_parts(jnp.transpose(sheet)[:count]))
    spare = stat_rows(count) - 3 * count
    if spare:
        parts.append(jnp.zeros((spare, 128), jnp.float32))
    return jnp.concatenate(parts, axis=0).astype(jnp.bfloat16)


def own_kernel(
    q_in, kv_in, selected_in, new_in, q_out, kv_out, bits_out, new_out, selected_ref, new_ref, sems
):
    steps, _, heads, _ = selected_ref.shape
    m, pages = kv_out.shape[:2]
    me = lax.axis_index("ctx")
    pairs = [(selected_in, selected_ref), (new_in, new_ref), (q_in, q_out)]
    pairs += [(kv_in.at[me ^ (2 * i)], kv_out.at[i]) for i in range(m)]
    copies = [pltpu.make_async_copy(*pair, sems.at[i]) for i, pair in enumerate(pairs)]
    for copy in copies:
        copy.start()
    for copy in copies[:2]:
        copy.wait()
    by_step = []
    for s in range(steps):
        lists = jnp.concatenate([selected_ref[s, me ^ (2 * i)] for i in range(m)], axis=0)
        for core in range(2):
            page = lists - (me ^ core) * pages
            here = (page >= 0) & (page < pages)
            bit = jnp.where(here, jnp.left_shift(1, page & 31), 0).astype(jnp.float32)
            total = jnp.sum(bit, axis=1, keepdims=True).astype(jnp.int32)
            by_step.append(jnp.broadcast_to(total, (m * heads, 128)))
    step_of = lax.broadcasted_iota(jnp.int32, (8, 128), 0) % steps
    for core in range(2):
        for i in range(m):
            for h in range(heads):
                row = i * heads + h
                bits = jnp.zeros((8, 128), jnp.int32)
                for s in range(steps):
                    bits = jnp.where(step_of == s, by_step[2 * s + core][row : row + 1], bits)
                bits_out[core, i, h] = bits
    for part in range(2):
        tokens = [new_ref[s, part : part + 1].astype(jnp.float32) for s in range(steps)]
        blank = jnp.zeros((16 - steps, new_ref.shape[2]), jnp.float32)
        new_out[part] = jnp.concatenate(tokens + [blank], axis=0).astype(jnp.bfloat16)
    for copy in copies[2:]:
        copy.wait()


def own_side(queries, kv_cache, selected, new_kv):
    batch, heads = selected.shape[1:3]
    m = batch // 2
    operands = (queries, kv_cache, selected, new_kv)
    return pl.pallas_call(
        own_kernel,
        out_shape=[
            jax.ShapeDtypeStruct(queries.shape, queries.dtype),
            jax.ShapeDtypeStruct((m,) + kv_cache.shape[1:], kv_cache.dtype),
            jax.ShapeDtypeStruct((2, m, heads, 8, 128), jnp.int32),
            jax.ShapeDtypeStruct((2, 16, new_kv.shape[2]), jnp.bfloat16),
        ],
        in_specs=[HBM] * 4,
        out_specs=[VMEM] * 4,
        scratch_shapes=[
            pltpu.VMEM(selected.shape, selected.dtype),
            pltpu.VMEM(new_kv.shape, new_kv.dtype),
            pltpu.SemaphoreType.DMA((3 + m,)),
        ],
        compiler_params=pltpu.CompilerParams(vmem_limit_bytes=VMEM_LIMIT),
        cost_estimate=pl.CostEstimate(
            flops=2**20, bytes_accessed=kv_cache.size * 2, transcendentals=0
        ),
    )(*[pltpu.with_memory_space_constraint(x, pltpu.HBM) for x in operands])


def page_masks(bits_ref, core, i, steps, page_bit):
    masks = []
    for h in range(bits_ref.shape[2]):
        bits = jnp.concatenate([bits_ref[core, i, h]] * (page_bit.shape[1] // 128), axis=1)
        masks += [(page_bit & bits) != 0] * steps
    return jnp.concatenate(masks, axis=0)


def attend(spread, pieces):
    found = []
    for keys, values, allowed in pieces:
        scores = lax.dot_general(spread, keys, NT, preferred_element_type=jnp.float32)
        found.append((jnp.where(allowed, scores * HD ** (-0.5), MASKED), values))

    def finish():
        tops = [jnp.max(scores, axis=1, keepdims=True) for scores, _ in found]
        top = jnp.maximum(functools.reduce(jnp.maximum, tops), FLOOR)
        total, weighted = 0.0, 0.0
        for scores, values in found:
            expo = jnp.exp(scores - top)
            total = total + jnp.sum(expo, axis=1, keepdims=True)
            weighted = weighted + jnp.dot(
                expo.astype(jnp.bfloat16), values, preferred_element_type=jnp.float32
            )
        return top, total, weighted

    return finish


def page_pieces(kv_ref, where, bits_ref, core, i, steps, heads):
    tokens = kv_ref.shape[1] * PAGE
    page_bit = jnp.left_shift(1, lax.broadcasted_iota(jnp.int32, (8, tokens), 1) // PAGE)
    keys = kv_ref[where, :, 0].reshape(tokens, heads * HD)
    values = kv_ref[where, :, 1].reshape(tokens, heads * HD)
    return keys, values, page_masks(bits_ref, core, i, steps, page_bit)


def staged(count, ahead, begin, end):
    begun = [begin(i) for i in range(min(ahead, count))]
    for i in range(count):
        if i + ahead < count:
            begun.append(begin(i + ahead))
        end(i, begun[i])


def first_kernel(heads, bits_ref, new_ref, own_ref, *refs):
    *q_refs, spread_ref, sum_ref, top_ref, total_ref, turned = refs
    steps = q_refs[0].shape[1]
    rows = turned.shape[1]

    def begin(i):
        spread = spread_heads(query_rows(q_refs[i], 0, turned.at[i]), heads)
        spread_ref[i] = spread
        pieces = [page_pieces(own_ref, i, bits_ref, 0, i, steps, heads)]
        if i == 0:
            step_of = lax.broadcasted_iota(jnp.int32, (rows, 16), 0) % steps
            causal = lax.broadcasted_iota(jnp.int32, (rows, 16), 1) <= step_of
            pieces.append((new_ref[0], new_ref[1], causal))
        return attend(spread, pieces)

    def end(i, finish):
        top, total, weighted = finish()
        top_ref[i] = jnp.broadcast_to(top, (rows, 128))
        total_ref[i] = jnp.broadcast_to(total, (rows, 128))
        sum_ref[i] = own_heads(weighted, heads)

    staged(len(q_refs), 1, begin, end)


def second_kernel(
    steps, heads, bits_ref, spread_ref, sum_ref, top_ref, total_ref, other_ref, out_ref
):
    m, rows = spread_ref.shape[:2]
    me = lax.axis_index("ctx")
    columns = []

    def begin(i):
        pieces = [page_pieces(other_ref, me ^ (2 * i), bits_ref, 1, i, steps, heads)]
        return attend(spread_ref[i], pieces)

    def end(i, finish):
        first_top, first_total = top_ref[i], total_ref[i]
        top, total, weighted = finish()
        top = jnp.broadcast_to(top, (rows, 128))
        both = jnp.maximum(top, first_top)
        factor, first_factor = jnp.exp(top - both), jnp.exp(first_top - both)
        total = jnp.broadcast_to(total, (rows, 128)) * factor + first_total * first_factor
        total = jnp.where(total > 0.0, total, 1.0)
        share = 1.0 / total
        joined = own_heads(weighted, heads) * (factor * share)
        joined = joined + sum_ref[i] * (first_factor * share)
        out_ref[i * rows : (i + 1) * rows, :] = joined.astype(jnp.bfloat16)
        columns.append(both + jnp.log(total))

    staged(m, m if m <= 4 else 2, begin, end)
    out_ref[m * rows :, :] = stat_block(columns)


def partials(bits, new_pairs, own_kv, other_kv, queries, rows, heads):
    m, pages = own_kv.shape[:2]
    tokens, width = pages * PAGE, own_kv.shape[4]
    steps = queries[0].shape[1]
    options = dict(
        compiler_params=pltpu.CompilerParams(vmem_limit_bytes=VMEM_LIMIT),
        cost_estimate=pl.CostEstimate(
            flops=4 * m * rows * tokens * width,
            bytes_accessed=2**20,
            transcendentals=m * rows * tokens,
        ),
    )
    state = pl.pallas_call(
        functools.partial(first_kernel, heads),
        out_shape=[
            jax.ShapeDtypeStruct((m, rows, width), jnp.bfloat16),
            jax.ShapeDtypeStruct((m, rows, HD), jnp.float32),
            jax.ShapeDtypeStruct((m, rows, 128), jnp.float32),
            jax.ShapeDtypeStruct((m, rows, 128), jnp.float32),
        ],
        in_specs=[VMEM] * (3 + m),
        out_specs=[VMEM] * 4,
        scratch_shapes=[pltpu.VMEM((m, rows, HD), jnp.float32)],
        **options,
    )(bits, new_pairs, own_kv, *queries)
    return pl.pallas_call(
        functools.partial(second_kernel, steps, heads),
        out_shape=jax.ShapeDtypeStruct((m * rows + stat_rows(m), HD), jnp.bfloat16),
        in_specs=[VMEM] * 6,
        out_specs=VMEM,
        **options,
    )(bits, *state, other_kv)


def last_merge_kernel(rows, steps, *refs):
    *part_refs, _, out_ref = refs
    m = len(part_refs)
    logs = []
    for j, ref in enumerate(part_refs):
        stats = ref[m * rows :, :].astype(jnp.float32)
        log = stats[:m] + stats[m : 2 * m] + stats[2 * m : 3 * m]
        if j:
            log = jnp.concatenate([log[i ^ j : (i ^ j) + 1] for i in range(m)], axis=0)
        logs.append(log)
    top = functools.reduce(jnp.maximum, logs)
    factors = [jnp.exp(log - top) for log in logs]
    share = 1.0 / functools.reduce(jnp.add, factors)
    lane = lax.broadcasted_iota(jnp.int32, (m, 128), 1) // rows
    beside = 128 // rows
    packed = []
    for first in range(0, m, beside):
        wide = jnp.zeros((m, 128), jnp.float32)
        for p in range(min(beside, m - first)):
            weight = factors[first + p] * share
            if p:
                weight = jnp.concatenate(
                    [weight[:, 128 - p * rows :], weight[:, : 128 - p * rows]], axis=1
                )
            wide = jnp.where(lane == p, weight, wide)
        packed.append(wide)
    on_row = lax.broadcasted_iota(jnp.int32, (rows, 128), 0)
    diagonal = lax.broadcasted_iota(jnp.int32, (rows, 128), 1) % rows == on_row
    for i in range(m):
        weights = jnp.concatenate(
            [jnp.where(diagonal, wide[i : i + 1], 0.0) for wide in packed], axis=1
        )
        parts = jnp.concatenate(
            [ref[(i ^ j) * rows : ((i ^ j) + 1) * rows, :] for j, ref in enumerate(part_refs)],
            axis=0,
        )
        high = weights.astype(jnp.bfloat16)
        low = (weights - high.astype(jnp.float32)).astype(jnp.bfloat16)
        joined = jnp.dot(high, parts, preferred_element_type=jnp.float32)
        joined = joined + jnp.dot(low, parts, preferred_element_type=jnp.float32)
        for j in range(rows // steps):
            piece = joined[j * steps : (j + 1) * steps]
            out_ref[i, :, j * HD : (j + 1) * HD] = piece.astype(jnp.bfloat16)


def last_merge(parts, weight, rows, steps):
    m = len(parts)
    return pl.pallas_call(
        functools.partial(last_merge_kernel, rows, steps),
        out_shape=jax.ShapeDtypeStruct((m, steps, rows // steps * HD), jnp.bfloat16),
        in_specs=[VMEM] * m + [ANY],
        out_specs=VMEM,
        compiler_params=pltpu.CompilerParams(vmem_limit_bytes=VMEM_LIMIT),
        cost_estimate=pl.CostEstimate(
            flops=2 * m * m * rows * HD, bytes_accessed=2**18, transcendentals=0
        ),
    )(*parts, weight)


def load_kernel(weight_ref, _, out_ref, sems):
    piece = out_ref.shape[0] // WEIGHT_PIECES
    copies = []
    for i in range(WEIGHT_PIECES):
        span = pl.ds(i * piece, piece)
        copy = pltpu.make_async_copy(weight_ref.at[span], out_ref.at[span], sems.at[i])
        copy.start()
        copies.append(copy)
    for copy in copies:
        copy.wait()


def load_weight(out_weight, after):
    return pl.pallas_call(
        load_kernel,
        out_shape=jax.ShapeDtypeStruct(out_weight.shape, out_weight.dtype),
        in_specs=[HBM, ANY],
        out_specs=VMEM,
        scratch_shapes=[pltpu.SemaphoreType.DMA((WEIGHT_PIECES,))],
        compiler_params=pltpu.CompilerParams(vmem_limit_bytes=VMEM_LIMIT),
        cost_estimate=pl.CostEstimate(
            flops=0, bytes_accessed=out_weight.size * 4, transcendentals=0
        ),
    )(pltpu.with_memory_space_constraint(out_weight, pltpu.HBM), after)


def project_rows(att_ref, weight_ref, lhs):
    count, _, width = lhs.shape
    steps = att_ref.shape[1]
    for i in range(count):
        lhs[i, :steps, :] = att_ref[i].astype(jnp.float32)
    left = lhs[...].reshape(count * 8, width).astype(jnp.bfloat16)
    product = jnp.dot(left, weight_ref[...], preferred_element_type=jnp.float32)
    return product.reshape(count, 8, weight_ref.shape[1])


def half_kernel(att_ref, weight_ref, out_ref, lhs):
    out_ref[...] = project_rows(att_ref, weight_ref, lhs)


def project_kernel(n_head, targets, att_ref, half_ref, weight_ref, *refs):
    lhs, rows_all = refs[-2:]
    out_refs = refs[:-2]
    m, steps, _ = att_ref.shape
    seqs = 2 * m // n_head
    me = lax.axis_index("ctx")
    mine = lax.axis_index("head")
    product = project_rows(att_ref, weight_ref, lhs)
    for i in range(m):
        rows_all[2 * i] = product[i]
        rows_all[2 * i + 1] = half_ref[i]
    for k, ref in enumerate(out_refs):
        target = mine
        if k > 0:
            for core, row in enumerate(targets[k - 1]):
                for z, t in enumerate(row):
                    target = jnp.where((me % 2 == core) & (mine == z), t, target)
        for j in range(seqs):
            found = rows_all[(jnp.maximum(target, 0) * seqs + j) ^ me][:steps]
            if k > 0 and any(t < 0 for row in targets[k - 1] for t in row):
                found = jnp.where(target < 0, 0.0, found)
            ref[j] = found.astype(ref.dtype)


def project_options(att, weight):
    m, _, width = att.shape
    columns = weight.shape[1]
    return dict(
        compiler_params=pltpu.CompilerParams(vmem_limit_bytes=VMEM_LIMIT),
        cost_estimate=pl.CostEstimate(
            flops=2 * m * 8 * width * columns,
            bytes_accessed=width * columns * 2,
            transcendentals=0,
        ),
    )


def project_half(att, weight):
    m, _, width = att.shape
    return pl.pallas_call(
        half_kernel,
        out_shape=jax.ShapeDtypeStruct((m, 8, weight.shape[1]), jnp.float32),
        in_specs=[VMEM] * 2,
        out_specs=VMEM,
        scratch_shapes=[pltpu.VMEM((m, 8, width), jnp.float32)],
        **project_options(att, weight),
    )(att, weight)


def project(att, half, weight, n_head, targets):
    m, steps, width = att.shape
    n = 2 * m
    columns = weight.shape[1]
    outs = [
        jax.ShapeDtypeStruct((n // n_head, steps, columns), jnp.bfloat16 if k else jnp.float32)
        for k in range(1 + len(targets))
    ]
    return pl.pallas_call(
        functools.partial(project_kernel, n_head, targets),
        out_shape=outs,
        in_specs=[VMEM] * 3,
        out_specs=[VMEM] * len(outs),
        scratch_shapes=[
            pltpu.VMEM((m, 8, width), jnp.float32),
            pltpu.VMEM((n, 8, columns), jnp.float32),
        ],
        **project_options(att, weight),
    )(att, half, weight)


def head_plan(n_head):
    if n_head == 4:
        return [
            (((0, 1), (1, 1), (0, 3), (0, 0)), ((1, 2), (1, 3), (0, 2), (1, 0))),
            (((1, 0), (0, 2), (0, 0), (0, 1)), ((1, 1), (1, 2), (1, 3), (0, 3))),
            (((0, 3), (0, 0), (1, 2), (0, 2)), ((1, 3), (0, 1), (1, 0), (1, 1))),
            (((0, 2), (0, 3), (0, 1), (1, 3)), ((0, 0), (1, 0), (1, 1), (1, 2))),
        ]
    return [
        tuple(tuple((core, (z + t) % n_head) for z in range(n_head)) for core in range(2))
        for t in range(1, n_head)
    ]


def plan_targets(plan):
    seen = set()
    targets = []
    for permutation in plan:
        rows = []
        for core, row in enumerate(permutation):
            rows.append([])
            for z, (to_core, t) in enumerate(row):
                useful = to_core == core and (core, z, t) not in seen
                rows[core].append(t if useful else -1)
                if useful:
                    seen.add((core, z, t))
        targets.append(rows)
    return targets


def send_by(permutation, x):
    n, n_head = lax.axis_size("ctx"), lax.axis_size("head")
    pairs = []
    for c in range(n):
        for z in range(n_head):
            core, t = permutation[c % 2][z]
            pairs.append((c * n_head + z, (c - c % 2 + core) * n_head + t))
    return lax.ppermute(x, ("ctx", "head"), pairs)


def swap(x, axis, r):
    size = lax.axis_size(axis)
    return lax.ppermute(x, axis, [(i, i ^ r) for i in range(size)])


def swap_chips(x, n):
    return [swap(x, "ctx", r) for r in range(2, n, 2)]


def swap_other_cores(x, n):
    return [swap(x, "ctx", r) for r in range(1, n, 2)]


def local(queries, kv_cache, new_kv, selected, out_weight):
    steps, _, width = queries.shape
    heads = kv_cache.shape[4] // HD
    rows = steps * heads * GROUPS
    n = lax.axis_size("ctx")
    n_head = lax.axis_size("head")

    first_q = queries.reshape(1, steps, width)
    other_kv = swap(kv_cache, "ctx", 1)
    far_q = swap_chips(first_q, n)
    new_pairs = new_kv.reshape(steps, 2, heads * HD)
    own_q, own_kv, bits, new_pairs = own_side(first_q, kv_cache, selected, new_pairs)
    all_q = [own_q] + far_q
    sent = partials(bits, new_pairs, own_kv, other_kv, all_q, rows, heads)
    parts = swap_other_cores(sent, n)
    weight = load_weight(out_weight, sent)
    odd_att = last_merge(parts, weight, rows, steps)
    even_att = swap(odd_att, "ctx", 1)
    plan = head_plan(n_head)
    half = project_half(odd_att, weight)
    total, *rows_out = project(even_att, half, weight, n_head, plan_targets(plan))
    for chunk, permutation in zip(rows_out, plan):
        total = total + send_by(permutation, chunk).astype(jnp.float32)
    return total.astype(jnp.bfloat16)


def solution(mesh):
    return jax.shard_map(
        local,
        mesh=mesh,
        in_specs=(
            P(None, "ctx", "head"),
            P(None, "ctx", None, None, "head"),
            P(None, "ctx", None, "head"),
            P(None, None, "head", None),
            P("head", "ctx"),
        ),
        out_specs=P("head", None, "ctx"),
        check_vma=False,
    )
```

```python
import functools

import jax
import jax.numpy as jnp
from jax import lax
from jax.experimental import pallas as pl
from jax.experimental.pallas import tpu as pltpu
from jax.sharding import PartitionSpec as P

HQ = 64
KVH = 8
HD = 128
PAGE = 64
GROUPS = HQ // KVH
STAT_ROWS = 16
MASKED = -3e38
FLOOR = -1.5e38
WEIGHT_PIECES = 4
VMEM_LIMIT = 24 * 1024 * 1024

VMEM = pl.BlockSpec(memory_space=pltpu.VMEM)
ANY = pl.BlockSpec(memory_space=pl.ANY)
HBM = pl.BlockSpec(memory_space=pltpu.HBM)
NT = (((1,), (1,)), ((), ()))


def query_rows(q_ref, slot, turned):
    steps, width = q_ref.shape[1:]
    for j in range(width // HD):
        piece = q_ref[slot, :, j * HD : (j + 1) * HD]
        turned[j * steps : (j + 1) * steps, :] = piece.astype(jnp.float32)
    return turned[...].astype(jnp.bfloat16)


def spread_heads(query, heads):
    rows = query.shape[0]
    row_head = lax.broadcasted_iota(jnp.int32, (rows, heads * HD), 0) // (rows // heads)
    lane_head = lax.broadcasted_iota(jnp.int32, (rows, heads * HD), 1) // HD
    wide = jnp.concatenate([query] * heads, axis=1)
    return jnp.where(row_head == lane_head, wide, jnp.zeros_like(wide))


def own_heads(weighted, heads):
    span = weighted.shape[0] // heads
    return jnp.concatenate(
        [weighted[h * span : (h + 1) * span, h * HD : (h + 1) * HD] for h in range(heads)], axis=0
    )


def three_parts(x):
    high = x.astype(jnp.bfloat16).astype(jnp.float32)
    rest = x - high
    middle = rest.astype(jnp.bfloat16).astype(jnp.float32)
    return high, middle, rest - middle


def stat_rows(slots):
    return -(-3 * slots // STAT_ROWS) * STAT_ROWS


def stat_block(columns):
    rows = columns[0].shape[0]
    lane = lax.broadcasted_iota(jnp.int32, (rows, 128), 1)
    sheet = jnp.zeros((rows, 128), jnp.float32)
    for i, column in enumerate(columns):
        sheet = jnp.where(lane == i, column, sheet)
    sheet = jnp.concatenate([sheet, jnp.zeros((128 - rows, 128), jnp.float32)], axis=0)
    count = len(columns)
    parts = list(three_parts(jnp.transpose(sheet)[:count]))
    spare = stat_rows(count) - 3 * count
    if spare:
        parts.append(jnp.zeros((spare, 128), jnp.float32))
    return jnp.concatenate(parts, axis=0).astype(jnp.bfloat16)


def own_kernel(
    q_in, kv_in, selected_in, new_in, q_out, kv_out, bits_out, new_out, selected_ref, new_ref, sems
):
    steps, _, heads, _ = selected_ref.shape
    m, pages = kv_out.shape[:2]
    me = lax.axis_index("ctx")
    pairs = [(selected_in, selected_ref), (new_in, new_ref), (q_in, q_out)]
    pairs += [(kv_in.at[me ^ (2 * i)], kv_out.at[i]) for i in range(m)]
    copies = [pltpu.make_async_copy(*pair, sems.at[i]) for i, pair in enumerate(pairs)]
    for copy in copies:
        copy.start()
    for copy in copies[:2]:
        copy.wait()
    by_step = []
    for s in range(steps):
        lists = jnp.concatenate([selected_ref[s, me ^ (2 * i)] for i in range(m)], axis=0)
        for core in range(2):
            page = lists - (me ^ core) * pages
            here = (page >= 0) & (page < pages)
            bit = jnp.where(here, jnp.left_shift(1, page & 31), 0).astype(jnp.float32)
            total = jnp.sum(bit, axis=1, keepdims=True).astype(jnp.int32)
            by_step.append(jnp.broadcast_to(total, (m * heads, 128)))
    step_of = lax.broadcasted_iota(jnp.int32, (8, 128), 0) % steps
    for core in range(2):
        for i in range(m):
            for h in range(heads):
                row = i * heads + h
                bits = jnp.zeros((8, 128), jnp.int32)
                for s in range(steps):
                    bits = jnp.where(step_of == s, by_step[2 * s + core][row : row + 1], bits)
                bits_out[core, i, h] = bits
    for part in range(2):
        tokens = [new_ref[s, part : part + 1].astype(jnp.float32) for s in range(steps)]
        blank = jnp.zeros((16 - steps, new_ref.shape[2]), jnp.float32)
        new_out[part] = jnp.concatenate(tokens + [blank], axis=0).astype(jnp.bfloat16)
    for copy in copies[2:]:
        copy.wait()


def own_side(queries, kv_cache, selected, new_kv):
    batch, heads = selected.shape[1:3]
    m = batch // 2
    operands = (queries, kv_cache, selected, new_kv)
    return pl.pallas_call(
        own_kernel,
        out_shape=[
            jax.ShapeDtypeStruct(queries.shape, queries.dtype),
            jax.ShapeDtypeStruct((m,) + kv_cache.shape[1:], kv_cache.dtype),
            jax.ShapeDtypeStruct((2, m, heads, 8, 128), jnp.int32),
            jax.ShapeDtypeStruct((2, 16, new_kv.shape[2]), jnp.bfloat16),
        ],
        in_specs=[HBM] * 4,
        out_specs=[VMEM] * 4,
        scratch_shapes=[
            pltpu.VMEM(selected.shape, selected.dtype),
            pltpu.VMEM(new_kv.shape, new_kv.dtype),
            pltpu.SemaphoreType.DMA((3 + m,)),
        ],
        compiler_params=pltpu.CompilerParams(vmem_limit_bytes=VMEM_LIMIT),
        cost_estimate=pl.CostEstimate(
            flops=2**20, bytes_accessed=kv_cache.size * 2, transcendentals=0
        ),
    )(*[pltpu.with_memory_space_constraint(x, pltpu.HBM) for x in operands])


def page_masks(bits_ref, core, i, steps, page_bit):
    masks = []
    for h in range(bits_ref.shape[2]):
        bits = jnp.concatenate([bits_ref[core, i, h]] * (page_bit.shape[1] // 128), axis=1)
        masks += [(page_bit & bits) != 0] * steps
    return jnp.concatenate(masks, axis=0)


def attend(spread, pieces):
    found = []
    for keys, values, allowed in pieces:
        scores = lax.dot_general(spread, keys, NT, preferred_element_type=jnp.float32)
        found.append((jnp.where(allowed, scores * HD ** (-0.5), MASKED), values))

    def finish():
        tops = [jnp.max(scores, axis=1, keepdims=True) for scores, _ in found]
        top = jnp.maximum(functools.reduce(jnp.maximum, tops), FLOOR)
        total, weighted = 0.0, 0.0
        for scores, values in found:
            expo = jnp.exp(scores - top)
            total = total + jnp.sum(expo, axis=1, keepdims=True)
            weighted = weighted + jnp.dot(
                expo.astype(jnp.bfloat16), values, preferred_element_type=jnp.float32
            )
        return top, total, weighted

    return finish


def page_pieces(kv_ref, where, bits_ref, core, i, steps, heads):
    tokens = kv_ref.shape[1] * PAGE
    page_bit = jnp.left_shift(1, lax.broadcasted_iota(jnp.int32, (8, tokens), 1) // PAGE)
    keys = kv_ref[where, :, 0].reshape(tokens, heads * HD)
    values = kv_ref[where, :, 1].reshape(tokens, heads * HD)
    return keys, values, page_masks(bits_ref, core, i, steps, page_bit)


def staged(count, ahead, begin, end):
    begun = [begin(i) for i in range(min(ahead, count))]
    for i in range(count):
        if i + ahead < count:
            begun.append(begin(i + ahead))
        end(i, begun[i])


def first_kernel(heads, bits_ref, new_ref, own_ref, *refs):
    *q_refs, spread_ref, sum_ref, top_ref, total_ref, turned = refs
    steps = q_refs[0].shape[1]
    rows = turned.shape[1]

    def begin(i):
        spread = spread_heads(query_rows(q_refs[i], 0, turned.at[i]), heads)
        spread_ref[i] = spread
        pieces = [page_pieces(own_ref, i, bits_ref, 0, i, steps, heads)]
        if i == 0:
            step_of = lax.broadcasted_iota(jnp.int32, (rows, 16), 0) % steps
            causal = lax.broadcasted_iota(jnp.int32, (rows, 16), 1) <= step_of
            pieces.append((new_ref[0], new_ref[1], causal))
        return attend(spread, pieces)

    def end(i, finish):
        top, total, weighted = finish()
        top_ref[i] = jnp.broadcast_to(top, (rows, 128))
        total_ref[i] = jnp.broadcast_to(total, (rows, 128))
        sum_ref[i] = own_heads(weighted, heads)

    staged(len(q_refs), 1, begin, end)


def second_kernel(
    steps, heads, bits_ref, spread_ref, sum_ref, top_ref, total_ref, other_ref, out_ref
):
    m, rows = spread_ref.shape[:2]
    me = lax.axis_index("ctx")
    columns = []

    def begin(i):
        pieces = [page_pieces(other_ref, me ^ (2 * i), bits_ref, 1, i, steps, heads)]
        return attend(spread_ref[i], pieces)

    def end(i, finish):
        first_top, first_total = top_ref[i], total_ref[i]
        top, total, weighted = finish()
        top = jnp.broadcast_to(top, (rows, 128))
        both = jnp.maximum(top, first_top)
        factor, first_factor = jnp.exp(top - both), jnp.exp(first_top - both)
        total = jnp.broadcast_to(total, (rows, 128)) * factor + first_total * first_factor
        total = jnp.where(total > 0.0, total, 1.0)
        share = 1.0 / total
        joined = own_heads(weighted, heads) * (factor * share)
        joined = joined + sum_ref[i] * (first_factor * share)
        out_ref[i * rows : (i + 1) * rows, :] = joined.astype(jnp.bfloat16)
        columns.append(both + jnp.log(total))

    staged(m, m if m <= 4 else 2, begin, end)
    out_ref[m * rows :, :] = stat_block(columns)


def partials(bits, new_pairs, own_kv, other_kv, queries, rows, heads):
    m, pages = own_kv.shape[:2]
    tokens, width = pages * PAGE, own_kv.shape[4]
    steps = queries[0].shape[1]
    options = dict(
        compiler_params=pltpu.CompilerParams(vmem_limit_bytes=VMEM_LIMIT),
        cost_estimate=pl.CostEstimate(
            flops=4 * m * rows * tokens * width,
            bytes_accessed=2**20,
            transcendentals=m * rows * tokens,
        ),
    )
    state = pl.pallas_call(
        functools.partial(first_kernel, heads),
        out_shape=[
            jax.ShapeDtypeStruct((m, rows, width), jnp.bfloat16),
            jax.ShapeDtypeStruct((m, rows, HD), jnp.float32),
            jax.ShapeDtypeStruct((m, rows, 128), jnp.float32),
            jax.ShapeDtypeStruct((m, rows, 128), jnp.float32),
        ],
        in_specs=[VMEM] * (3 + m),
        out_specs=[VMEM] * 4,
        scratch_shapes=[pltpu.VMEM((m, rows, HD), jnp.float32)],
        **options,
    )(bits, new_pairs, own_kv, *queries)
    return pl.pallas_call(
        functools.partial(second_kernel, steps, heads),
        out_shape=jax.ShapeDtypeStruct((m * rows + stat_rows(m), HD), jnp.bfloat16),
        in_specs=[VMEM] * 6,
        out_specs=VMEM,
        **options,
    )(bits, *state, other_kv)


def last_merge_kernel(rows, steps, *refs):
    *part_refs, _, out_ref = refs
    m = len(part_refs)
    logs = []
    for j, ref in enumerate(part_refs):
        stats = ref[m * rows :, :].astype(jnp.float32)
        log = stats[:m] + stats[m : 2 * m] + stats[2 * m : 3 * m]
        if j:
            log = jnp.concatenate([log[i ^ j : (i ^ j) + 1] for i in range(m)], axis=0)
        logs.append(log)
    top = functools.reduce(jnp.maximum, logs)
    factors = [jnp.exp(log - top) for log in logs]
    share = 1.0 / functools.reduce(jnp.add, factors)
    lane = lax.broadcasted_iota(jnp.int32, (m, 128), 1) // rows
    beside = 128 // rows
    packed = []
    for first in range(0, m, beside):
        wide = jnp.zeros((m, 128), jnp.float32)
        for p in range(min(beside, m - first)):
            weight = factors[first + p] * share
            if p:
                weight = jnp.concatenate(
                    [weight[:, 128 - p * rows :], weight[:, : 128 - p * rows]], axis=1
                )
            wide = jnp.where(lane == p, weight, wide)
        packed.append(wide)
    on_row = lax.broadcasted_iota(jnp.int32, (rows, 128), 0)
    diagonal = lax.broadcasted_iota(jnp.int32, (rows, 128), 1) % rows == on_row
    joined = []
    for i in range(m):
        weights = jnp.concatenate(
            [jnp.where(diagonal, wide[i : i + 1], 0.0) for wide in packed], axis=1
        )
        parts = jnp.concatenate(
            [ref[(i ^ j) * rows : ((i ^ j) + 1) * rows, :] for j, ref in enumerate(part_refs)],
            axis=0,
        )
        high = weights.astype(jnp.bfloat16)
        low = (weights - high.astype(jnp.float32)).astype(jnp.bfloat16)
        product = jnp.dot(high, parts, preferred_element_type=jnp.float32)
        product = product + jnp.dot(low, parts, preferred_element_type=jnp.float32)
        joined.append(product)
    for j in range(rows // steps):
        piece = jnp.concatenate([x[j * steps : (j + 1) * steps] for x in joined], axis=0)
        out_ref[:, j * HD : (j + 1) * HD] = piece.astype(jnp.bfloat16)


def last_merge(parts, weight, rows, steps):
    m = len(parts)
    return pl.pallas_call(
        functools.partial(last_merge_kernel, rows, steps),
        out_shape=jax.ShapeDtypeStruct((m * steps, rows // steps * HD), jnp.bfloat16),
        in_specs=[VMEM] * m + [ANY],
        out_specs=VMEM,
        compiler_params=pltpu.CompilerParams(vmem_limit_bytes=VMEM_LIMIT),
        cost_estimate=pl.CostEstimate(
            flops=2 * m * m * rows * HD, bytes_accessed=2**18, transcendentals=0
        ),
    )(*parts, weight)


def load_kernel(weight_ref, _, out_ref, sems):
    piece = out_ref.shape[0] // WEIGHT_PIECES
    copies = []
    for i in range(WEIGHT_PIECES):
        span = pl.ds(i * piece, piece)
        copy = pltpu.make_async_copy(weight_ref.at[span], out_ref.at[span], sems.at[i])
        copy.start()
        copies.append(copy)
    for copy in copies:
        copy.wait()


def load_weight(out_weight, after):
    return pl.pallas_call(
        load_kernel,
        out_shape=jax.ShapeDtypeStruct(out_weight.shape, out_weight.dtype),
        in_specs=[HBM, ANY],
        out_specs=VMEM,
        scratch_shapes=[pltpu.SemaphoreType.DMA((WEIGHT_PIECES,))],
        compiler_params=pltpu.CompilerParams(vmem_limit_bytes=VMEM_LIMIT),
        cost_estimate=pl.CostEstimate(
            flops=0, bytes_accessed=out_weight.size * 4, transcendentals=0
        ),
    )(pltpu.with_memory_space_constraint(out_weight, pltpu.HBM), after)


def half_kernel(att_ref, weight_ref, out_ref):
    out_ref[...] = jnp.dot(att_ref[...], weight_ref[...], preferred_element_type=jnp.float32)


def project_kernel(n_head, targets, att_ref, half_ref, weight_ref, *refs):
    *out_refs, rows_all = refs
    seqs, steps, _ = out_refs[0].shape
    me = lax.axis_index("ctx")
    mine = lax.axis_index("head")
    product = jnp.dot(att_ref[...], weight_ref[...], preferred_element_type=jnp.float32)
    for i in range(rows_all.shape[0] // 2):
        rows_all[2 * i, :steps, :] = product[i * steps : (i + 1) * steps]
        rows_all[2 * i + 1, :steps, :] = half_ref[i * steps : (i + 1) * steps, :]
    for k, ref in enumerate(out_refs):
        target = mine
        if k > 0:
            for core, row in enumerate(targets[k - 1]):
                for z, t in enumerate(row):
                    target = jnp.where((me % 2 == core) & (mine == z), t, target)
        for j in range(seqs):
            found = rows_all[(jnp.maximum(target, 0) * seqs + j) ^ me, :steps]
            if k > 0 and any(t < 0 for row in targets[k - 1] for t in row):
                found = jnp.where(target < 0, 0.0, found)
            ref[j] = found.astype(ref.dtype)


def project_options(att, weight):
    width, columns = weight.shape
    return dict(
        compiler_params=pltpu.CompilerParams(vmem_limit_bytes=VMEM_LIMIT),
        cost_estimate=pl.CostEstimate(
            flops=2 * att.size * columns, bytes_accessed=width * columns * 2, transcendentals=0
        ),
    )


def project_half(att, weight):
    return pl.pallas_call(
        half_kernel,
        out_shape=jax.ShapeDtypeStruct((att.shape[0], weight.shape[1]), jnp.float32),
        in_specs=[VMEM] * 2,
        out_specs=VMEM,
        **project_options(att, weight),
    )(att, weight)


def project(att, half, weight, steps, n_head, targets):
    n = 2 * att.shape[0] // steps
    columns = weight.shape[1]
    outs = [
        jax.ShapeDtypeStruct((n // n_head, steps, columns), jnp.bfloat16 if k else jnp.float32)
        for k in range(1 + len(targets))
    ]
    return pl.pallas_call(
        functools.partial(project_kernel, n_head, targets),
        out_shape=outs,
        in_specs=[VMEM] * 3,
        out_specs=[VMEM] * len(outs),
        scratch_shapes=[pltpu.VMEM((n, 8, columns), jnp.float32)],
        **project_options(att, weight),
    )(att, half, weight)


def head_plan(n_head):
    if n_head == 4:
        return [
            (((0, 1), (1, 1), (0, 3), (0, 0)), ((1, 2), (1, 3), (0, 2), (1, 0))),
            (((1, 0), (0, 2), (0, 0), (0, 1)), ((1, 1), (1, 2), (1, 3), (0, 3))),
            (((0, 3), (0, 0), (1, 2), (0, 2)), ((1, 3), (0, 1), (1, 0), (1, 1))),
            (((0, 2), (0, 3), (0, 1), (1, 3)), ((0, 0), (1, 0), (1, 1), (1, 2))),
        ]
    return [
        tuple(tuple((core, (z + t) % n_head) for z in range(n_head)) for core in range(2))
        for t in range(1, n_head)
    ]


def plan_targets(plan):
    seen = set()
    targets = []
    for permutation in plan:
        rows = []
        for core, row in enumerate(permutation):
            rows.append([])
            for z, (to_core, t) in enumerate(row):
                useful = to_core == core and (core, z, t) not in seen
                rows[core].append(t if useful else -1)
                if useful:
                    seen.add((core, z, t))
        targets.append(rows)
    return targets


def send_by(permutation, x):
    n, n_head = lax.axis_size("ctx"), lax.axis_size("head")
    pairs = []
    for c in range(n):
        for z in range(n_head):
            core, t = permutation[c % 2][z]
            pairs.append((c * n_head + z, (c - c % 2 + core) * n_head + t))
    return lax.ppermute(x, ("ctx", "head"), pairs)


def swap(x, axis, r):
    size = lax.axis_size(axis)
    return lax.ppermute(x, axis, [(i, i ^ r) for i in range(size)])


def swap_chips(x, n):
    return [swap(x, "ctx", r) for r in range(2, n, 2)]


def swap_other_cores(x, n):
    return [swap(x, "ctx", r) for r in range(1, n, 2)]


def local(queries, kv_cache, new_kv, selected, out_weight):
    steps, _, width = queries.shape
    heads = kv_cache.shape[4] // HD
    rows = steps * heads * GROUPS
    n = lax.axis_size("ctx")
    n_head = lax.axis_size("head")

    first_q = queries.reshape(1, steps, width)
    other_kv = swap(kv_cache, "ctx", 1)
    far_q = swap_chips(first_q, n)
    new_pairs = new_kv.reshape(steps, 2, heads * HD)
    own_q, own_kv, bits, new_pairs = own_side(first_q, kv_cache, selected, new_pairs)
    all_q = [own_q] + far_q
    sent = partials(bits, new_pairs, own_kv, other_kv, all_q, rows, heads)
    parts = swap_other_cores(sent, n)
    weight = load_weight(out_weight, sent)
    odd_att = last_merge(parts, weight, rows, steps)
    even_att = swap(odd_att, "ctx", 1)
    plan = head_plan(n_head)
    half = project_half(odd_att, weight)
    total, *rows_out = project(
        even_att, half, weight, steps, n_head, plan_targets(plan)
    )
    for chunk, permutation in zip(rows_out, plan):
        total = total + send_by(permutation, chunk).astype(jnp.float32)
    return total.astype(jnp.bfloat16)


def solution(mesh):
    return jax.shard_map(
        local,
        mesh=mesh,
        in_specs=(
            P(None, "ctx", "head"),
            P(None, "ctx", None, None, "head"),
            P(None, "ctx", None, "head"),
            P(None, None, "head", None),
            P("head", "ctx"),
        ),
        out_specs=P("head", None, "ctx"),
        check_vma=False,
    )
```

```python
import functools

import jax
import jax.numpy as jnp
from jax import lax
from jax.experimental import pallas as pl
from jax.experimental.pallas import tpu as pltpu
from jax.sharding import PartitionSpec as P

HQ = 64
KVH = 8
HD = 128
PAGE = 64
GROUPS = HQ // KVH
STAT_ROWS = 16
MASKED = -3e38
FLOOR = -1.5e38
WEIGHT_PIECES = 4
VMEM_LIMIT = 24 * 1024 * 1024

VMEM = pl.BlockSpec(memory_space=pltpu.VMEM)
ANY = pl.BlockSpec(memory_space=pl.ANY)
HBM = pl.BlockSpec(memory_space=pltpu.HBM)
NT = (((1,), (1,)), ((), ()))


def query_rows(q_ref, slot, turned):
    steps, width = q_ref.shape[1:]
    for j in range(width // HD):
        piece = q_ref[slot, :, j * HD : (j + 1) * HD]
        turned[j * steps : (j + 1) * steps, :] = piece.astype(jnp.float32)
    return turned[...].astype(jnp.bfloat16)


def three_parts(x):
    high = x.astype(jnp.bfloat16).astype(jnp.float32)
    rest = x - high
    middle = rest.astype(jnp.bfloat16).astype(jnp.float32)
    return high, middle, rest - middle


def stat_rows(slots):
    return -(-3 * slots // STAT_ROWS) * STAT_ROWS


def stat_block(columns):
    rows = columns[0].shape[0]
    lane = lax.broadcasted_iota(jnp.int32, (rows, 128), 1)
    sheet = jnp.zeros((rows, 128), jnp.float32)
    for i, column in enumerate(columns):
        sheet = jnp.where(lane == i, column, sheet)
    sheet = jnp.concatenate([sheet, jnp.zeros((128 - rows, 128), jnp.float32)], axis=0)
    count = len(columns)
    parts = list(three_parts(jnp.transpose(sheet)[:count]))
    spare = stat_rows(count) - 3 * count
    if spare:
        parts.append(jnp.zeros((spare, 128), jnp.float32))
    return jnp.concatenate(parts, axis=0).astype(jnp.bfloat16)


def own_kernel(
    q_in, kv_in, selected_in, new_in, q_out, kv_out, bits_out, new_out, selected_ref, new_ref, sems
):
    steps, _, heads, _ = selected_ref.shape
    m, pages = kv_out.shape[:2]
    me = lax.axis_index("ctx")
    pairs = [(selected_in, selected_ref), (new_in, new_ref), (q_in, q_out)]
    pairs += [(kv_in.at[me ^ (2 * i)], kv_out.at[i]) for i in range(m)]
    copies = [pltpu.make_async_copy(*pair, sems.at[i]) for i, pair in enumerate(pairs)]
    for copy in copies:
        copy.start()
    for copy in copies[:2]:
        copy.wait()
    by_step = []
    for s in range(steps):
        lists = jnp.concatenate([selected_ref[s, me ^ (2 * i)] for i in range(m)], axis=0)
        for core in range(2):
            page = lists - (me ^ core) * pages
            here = (page >= 0) & (page < pages)
            bit = jnp.where(here, jnp.left_shift(1, page & 31), 0).astype(jnp.float32)
            total = jnp.sum(bit, axis=1, keepdims=True).astype(jnp.int32)
            by_step.append(jnp.broadcast_to(total, (m * heads, 128)))
    step_of = lax.broadcasted_iota(jnp.int32, (8, 128), 0) % steps
    for core in range(2):
        for i in range(m):
            for h in range(heads):
                row = i * heads + h
                bits = jnp.zeros((8, 128), jnp.int32)
                for s in range(steps):
                    bits = jnp.where(step_of == s, by_step[2 * s + core][row : row + 1], bits)
                bits_out[core, i, h] = bits
    for part in range(2):
        tokens = [new_ref[s, part : part + 1].astype(jnp.float32) for s in range(steps)]
        blank = jnp.zeros((16 - steps, new_ref.shape[2]), jnp.float32)
        new_out[part] = jnp.concatenate(tokens + [blank], axis=0).astype(jnp.bfloat16)
    for copy in copies[2:]:
        copy.wait()


def own_side(queries, kv_cache, selected, new_kv):
    batch, heads = selected.shape[1:3]
    m = batch // 2
    operands = (queries, kv_cache, selected, new_kv)
    return pl.pallas_call(
        own_kernel,
        out_shape=[
            jax.ShapeDtypeStruct(queries.shape, queries.dtype),
            jax.ShapeDtypeStruct((m,) + kv_cache.shape[1:], kv_cache.dtype),
            jax.ShapeDtypeStruct((2, m, heads, 8, 128), jnp.int32),
            jax.ShapeDtypeStruct((2, 16, new_kv.shape[2]), jnp.bfloat16),
        ],
        in_specs=[HBM] * 4,
        out_specs=[VMEM] * 4,
        scratch_shapes=[
            pltpu.VMEM(selected.shape, selected.dtype),
            pltpu.VMEM(new_kv.shape, new_kv.dtype),
            pltpu.SemaphoreType.DMA((3 + m,)),
        ],
        compiler_params=pltpu.CompilerParams(vmem_limit_bytes=VMEM_LIMIT),
        cost_estimate=pl.CostEstimate(
            flops=2**20, bytes_accessed=kv_cache.size * 2, transcendentals=0
        ),
    )(*[pltpu.with_memory_space_constraint(x, pltpu.HBM) for x in operands])


def page_mask(bits_ref, core, i, h, steps, page_bit):
    bits = jnp.concatenate([bits_ref[core, i, h]] * (page_bit.shape[1] // 128), axis=1)
    return jnp.concatenate([(page_bit & bits) != 0] * steps, axis=0)


def attend(query, pieces):
    found = []
    for keys, values, allowed in pieces:
        scores = lax.dot_general(query, keys, NT, preferred_element_type=jnp.float32)
        found.append((jnp.where(allowed, scores * HD ** (-0.5), MASKED), values))

    def finish():
        tops = [jnp.max(scores, axis=1, keepdims=True) for scores, _ in found]
        top = jnp.maximum(functools.reduce(jnp.maximum, tops), FLOOR)
        total, weighted = 0.0, 0.0
        for scores, values in found:
            expo = jnp.exp(scores - top)
            total = total + jnp.sum(expo, axis=1, keepdims=True)
            weighted = weighted + jnp.dot(
                expo.astype(jnp.bfloat16), values, preferred_element_type=jnp.float32
            )
        return top, total, weighted

    return finish


def page_piece(kv_ref, where, bits_ref, core, i, h, steps):
    tokens = kv_ref.shape[1] * PAGE
    page_bit = jnp.left_shift(1, lax.broadcasted_iota(jnp.int32, (8, tokens), 1) // PAGE)
    lanes = slice(h * HD, (h + 1) * HD)
    keys = kv_ref[where, :, 0, :, lanes].reshape(tokens, HD)
    values = kv_ref[where, :, 1, :, lanes].reshape(tokens, HD)
    return keys, values, page_mask(bits_ref, core, i, h, steps, page_bit)


def staged(count, ahead, begin, end):
    begun = [begin(i) for i in range(min(ahead, count))]
    for i in range(count):
        if i + ahead < count:
            begun.append(begin(i + ahead))
        end(i, begun[i])


def first_kernel(heads, bits_ref, new_ref, own_ref, *refs):
    *q_refs, query_ref, sum_ref, top_ref, total_ref, turned = refs
    steps = q_refs[0].shape[1]
    m, span = len(q_refs), steps * GROUPS

    def begin(unit):
        i, h = divmod(unit, heads)
        rows = slice(h * span, (h + 1) * span)
        if h == 0:
            query_ref[i] = query_rows(q_refs[i], 0, turned.at[i])
        query = turned[i, rows].astype(jnp.bfloat16)
        pieces = [page_piece(own_ref, i, bits_ref, 0, i, h, steps)]
        if i == 0:
            step_of = lax.broadcasted_iota(jnp.int32, (span, 16), 0) % steps
            causal = lax.broadcasted_iota(jnp.int32, (span, 16), 1) <= step_of
            lanes = slice(h * HD, (h + 1) * HD)
            pieces.append((new_ref[0, :, lanes], new_ref[1, :, lanes], causal))
        return attend(query, pieces)

    def end(unit, finish):
        i, h = divmod(unit, heads)
        rows = slice(h * span, (h + 1) * span)
        top, total, weighted = finish()
        top_ref[i, rows] = jnp.broadcast_to(top, (span, 128))
        total_ref[i, rows] = jnp.broadcast_to(total, (span, 128))
        sum_ref[i, rows] = weighted

    staged(m * heads, heads, begin, end)


def second_kernel(
    steps, heads, bits_ref, query_ref, sum_ref, top_ref, total_ref, other_ref, out_ref
):
    m, rows = query_ref.shape[:2]
    span = steps * GROUPS
    me = lax.axis_index("ctx")
    logs = []

    def begin(unit):
        i, h = divmod(unit, heads)
        piece = page_piece(other_ref, me ^ (2 * i), bits_ref, 1, i, h, steps)
        return attend(query_ref[i, h * span : (h + 1) * span], [piece])

    def end(unit, finish):
        i, h = divmod(unit, heads)
        own = slice(h * span, (h + 1) * span)
        first_top, first_total = top_ref[i, own], total_ref[i, own]
        top, total, weighted = finish()
        top = jnp.broadcast_to(top, (span, 128))
        both = jnp.maximum(top, first_top)
        factor, first_factor = jnp.exp(top - both), jnp.exp(first_top - both)
        total = jnp.broadcast_to(total, (span, 128)) * factor + first_total * first_factor
        total = jnp.where(total > 0.0, total, 1.0)
        share = 1.0 / total
        joined = weighted * (factor * share) + sum_ref[i, own] * (first_factor * share)
        first = i * rows + h * span
        out_ref[first : first + span, :] = joined.astype(jnp.bfloat16)
        logs.append(both + jnp.log(total))

    count = m * heads
    staged(count, count if count <= 8 else heads, begin, end)
    columns = [jnp.concatenate(logs[i * heads : (i + 1) * heads], axis=0) for i in range(m)]
    out_ref[m * rows :, :] = stat_block(columns)


def partials(bits, new_pairs, own_kv, other_kv, queries, rows, heads):
    m, pages = own_kv.shape[:2]
    tokens, width = pages * PAGE, own_kv.shape[4]
    steps = queries[0].shape[1]
    options = dict(
        compiler_params=pltpu.CompilerParams(vmem_limit_bytes=VMEM_LIMIT),
        cost_estimate=pl.CostEstimate(
            flops=4 * m * rows * tokens * width,
            bytes_accessed=2**20,
            transcendentals=m * rows * tokens,
        ),
    )
    state = pl.pallas_call(
        functools.partial(first_kernel, heads),
        out_shape=[
            jax.ShapeDtypeStruct((m, rows, HD), jnp.bfloat16),
            jax.ShapeDtypeStruct((m, rows, HD), jnp.float32),
            jax.ShapeDtypeStruct((m, rows, 128), jnp.float32),
            jax.ShapeDtypeStruct((m, rows, 128), jnp.float32),
        ],
        in_specs=[VMEM] * (3 + m),
        out_specs=[VMEM] * 4,
        scratch_shapes=[pltpu.VMEM((m, rows, HD), jnp.float32)],
        **options,
    )(bits, new_pairs, own_kv, *queries)
    return pl.pallas_call(
        functools.partial(second_kernel, steps, heads),
        out_shape=jax.ShapeDtypeStruct((m * rows + stat_rows(m), HD), jnp.bfloat16),
        in_specs=[VMEM] * 6,
        out_specs=VMEM,
        **options,
    )(bits, *state, other_kv)


def last_merge_kernel(rows, steps, *refs):
    *part_refs, _, out_ref = refs
    m = len(part_refs)
    logs = []
    for j, ref in enumerate(part_refs):
        stats = ref[m * rows :, :].astype(jnp.float32)
        log = stats[:m] + stats[m : 2 * m] + stats[2 * m : 3 * m]
        if j:
            log = jnp.concatenate([log[i ^ j : (i ^ j) + 1] for i in range(m)], axis=0)
        logs.append(log)
    top = functools.reduce(jnp.maximum, logs)
    factors = [jnp.exp(log - top) for log in logs]
    share = 1.0 / functools.reduce(jnp.add, factors)
    lane = lax.broadcasted_iota(jnp.int32, (m, 128), 1) // rows
    beside = 128 // rows
    packed = []
    for first in range(0, m, beside):
        wide = jnp.zeros((m, 128), jnp.float32)
        for p in range(min(beside, m - first)):
            weight = factors[first + p] * share
            if p:
                weight = jnp.concatenate(
                    [weight[:, 128 - p * rows :], weight[:, : 128 - p * rows]], axis=1
                )
            wide = jnp.where(lane == p, weight, wide)
        packed.append(wide)
    on_row = lax.broadcasted_iota(jnp.int32, (rows, 128), 0)
    diagonal = lax.broadcasted_iota(jnp.int32, (rows, 128), 1) % rows == on_row
    joined = []
    for i in range(m):
        weights = jnp.concatenate(
            [jnp.where(diagonal, wide[i : i + 1], 0.0) for wide in packed], axis=1
        )
        parts = jnp.concatenate(
            [ref[(i ^ j) * rows : ((i ^ j) + 1) * rows, :] for j, ref in enumerate(part_refs)],
            axis=0,
        )
        high = weights.astype(jnp.bfloat16)
        low = (weights - high.astype(jnp.float32)).astype(jnp.bfloat16)
        both = jnp.concatenate([high, low], axis=0)
        product = jnp.dot(both, parts, preferred_element_type=jnp.float32)
        joined.append(product[:rows] + product[rows:])
    for j in range(rows // steps):
        piece = jnp.concatenate([x[j * steps : (j + 1) * steps] for x in joined], axis=0)
        out_ref[:, j * HD : (j + 1) * HD] = piece.astype(jnp.bfloat16)


def last_merge(parts, weight, rows, steps):
    m = len(parts)
    return pl.pallas_call(
        functools.partial(last_merge_kernel, rows, steps),
        out_shape=jax.ShapeDtypeStruct((m * steps, rows // steps * HD), jnp.bfloat16),
        in_specs=[VMEM] * m + [ANY],
        out_specs=VMEM,
        compiler_params=pltpu.CompilerParams(vmem_limit_bytes=VMEM_LIMIT),
        cost_estimate=pl.CostEstimate(
            flops=2 * m * m * rows * HD, bytes_accessed=2**18, transcendentals=0
        ),
    )(*parts, weight)


def load_kernel(weight_ref, _, out_ref, sems):
    piece = out_ref.shape[0] // WEIGHT_PIECES
    copies = []
    for i in range(WEIGHT_PIECES):
        span = pl.ds(i * piece, piece)
        copy = pltpu.make_async_copy(weight_ref.at[span], out_ref.at[span], sems.at[i])
        copy.start()
        copies.append(copy)
    for copy in copies:
        copy.wait()


def load_weight(out_weight, after):
    return pl.pallas_call(
        load_kernel,
        out_shape=jax.ShapeDtypeStruct(out_weight.shape, out_weight.dtype),
        in_specs=[HBM, ANY],
        out_specs=VMEM,
        scratch_shapes=[pltpu.SemaphoreType.DMA((WEIGHT_PIECES,))],
        compiler_params=pltpu.CompilerParams(vmem_limit_bytes=VMEM_LIMIT),
        cost_estimate=pl.CostEstimate(
            flops=0, bytes_accessed=out_weight.size * 4, transcendentals=0
        ),
    )(pltpu.with_memory_space_constraint(out_weight, pltpu.HBM), after)


def half_kernel(att_ref, weight_ref, out_ref):
    out_ref[...] = jnp.dot(att_ref[...], weight_ref[...], preferred_element_type=jnp.float32)


def project_kernel(n_head, targets, att_ref, half_ref, weight_ref, *refs):
    *out_refs, rows_all = refs
    seqs, steps, _ = out_refs[0].shape
    me = lax.axis_index("ctx")
    mine = lax.axis_index("head")
    product = jnp.dot(att_ref[...], weight_ref[...], preferred_element_type=jnp.float32)
    for i in range(rows_all.shape[0] // 2):
        rows_all[2 * i, :steps, :] = product[i * steps : (i + 1) * steps]
        rows_all[2 * i + 1, :steps, :] = half_ref[i * steps : (i + 1) * steps, :]
    for k, ref in enumerate(out_refs):
        target = mine
        if k > 0:
            for core, row in enumerate(targets[k - 1]):
                for z, t in enumerate(row):
                    target = jnp.where((me % 2 == core) & (mine == z), t, target)
        for j in range(seqs):
            found = rows_all[(jnp.maximum(target, 0) * seqs + j) ^ me, :steps]
            if k > 0 and any(t < 0 for row in targets[k - 1] for t in row):
                found = jnp.where(target < 0, 0.0, found)
            ref[j] = found.astype(ref.dtype)


def project_options(att, weight):
    width, columns = weight.shape
    return dict(
        compiler_params=pltpu.CompilerParams(vmem_limit_bytes=VMEM_LIMIT),
        cost_estimate=pl.CostEstimate(
            flops=2 * att.size * columns, bytes_accessed=width * columns * 2, transcendentals=0
        ),
    )


def project_half(att, weight):
    return pl.pallas_call(
        half_kernel,
        out_shape=jax.ShapeDtypeStruct((att.shape[0], weight.shape[1]), jnp.float32),
        in_specs=[VMEM] * 2,
        out_specs=VMEM,
        **project_options(att, weight),
    )(att, weight)


def project(att, half, weight, steps, n_head, targets):
    n = 2 * att.shape[0] // steps
    columns = weight.shape[1]
    outs = [
        jax.ShapeDtypeStruct((n // n_head, steps, columns), jnp.bfloat16 if k else jnp.float32)
        for k in range(1 + len(targets))
    ]
    return pl.pallas_call(
        functools.partial(project_kernel, n_head, targets),
        out_shape=outs,
        in_specs=[VMEM] * 3,
        out_specs=[VMEM] * len(outs),
        scratch_shapes=[pltpu.VMEM((n, 8, columns), jnp.float32)],
        **project_options(att, weight),
    )(att, half, weight)


def head_plan(n_head):
    if n_head == 4:
        return [
            (((0, 1), (1, 1), (0, 3), (0, 0)), ((1, 2), (1, 3), (0, 2), (1, 0))),
            (((1, 0), (0, 2), (0, 0), (0, 1)), ((1, 1), (1, 2), (1, 3), (0, 3))),
            (((0, 3), (0, 0), (1, 2), (0, 2)), ((1, 3), (0, 1), (1, 0), (1, 1))),
            (((0, 2), (0, 3), (0, 1), (1, 3)), ((0, 0), (1, 0), (1, 1), (1, 2))),
        ]
    return [
        tuple(tuple((core, (z + t) % n_head) for z in range(n_head)) for core in range(2))
        for t in range(1, n_head)
    ]


def plan_targets(plan):
    seen = set()
    targets = []
    for permutation in plan:
        rows = []
        for core, row in enumerate(permutation):
            rows.append([])
            for z, (to_core, t) in enumerate(row):
                useful = to_core == core and (core, z, t) not in seen
                rows[core].append(t if useful else -1)
                if useful:
                    seen.add((core, z, t))
        targets.append(rows)
    return targets


def send_by(permutation, x):
    n, n_head = lax.axis_size("ctx"), lax.axis_size("head")
    pairs = []
    for c in range(n):
        for z in range(n_head):
            core, t = permutation[c % 2][z]
            pairs.append((c * n_head + z, (c - c % 2 + core) * n_head + t))
    return lax.ppermute(x, ("ctx", "head"), pairs)


def swap(x, axis, r):
    size = lax.axis_size(axis)
    return lax.ppermute(x, axis, [(i, i ^ r) for i in range(size)])


def swap_chips(x, n):
    return [swap(x, "ctx", r) for r in range(2, n, 2)]


def swap_other_cores(x, n):
    return [swap(x, "ctx", r) for r in range(1, n, 2)]


def local(queries, kv_cache, new_kv, selected, out_weight):
    steps, _, width = queries.shape
    heads = kv_cache.shape[4] // HD
    rows = steps * heads * GROUPS
    n = lax.axis_size("ctx")
    n_head = lax.axis_size("head")

    first_q = queries.reshape(1, steps, width)
    other_kv = swap(kv_cache, "ctx", 1)
    far_q = swap_chips(first_q, n)
    new_pairs = new_kv.reshape(steps, 2, heads * HD)
    own_q, own_kv, bits, new_pairs = own_side(first_q, kv_cache, selected, new_pairs)
    all_q = [own_q] + far_q
    sent = partials(bits, new_pairs, own_kv, other_kv, all_q, rows, heads)
    parts = swap_other_cores(sent, n)
    weight = load_weight(out_weight, sent)
    odd_att = last_merge(parts, weight, rows, steps)
    even_att = swap(odd_att, "ctx", 1)
    plan = head_plan(n_head)
    half = project_half(odd_att, weight)
    total, *rows_out = project(
        even_att, half, weight, steps, n_head, plan_targets(plan)
    )
    for chunk, permutation in zip(rows_out, plan):
        total = total + send_by(permutation, chunk).astype(jnp.float32)
    return total.astype(jnp.bfloat16)


def solution(mesh):
    return jax.shard_map(
        local,
        mesh=mesh,
        in_specs=(
            P(None, "ctx", "head"),
            P(None, "ctx", None, None, "head"),
            P(None, "ctx", None, "head"),
            P(None, None, "head", None),
            P("head", "ctx"),
        ),
        out_specs=P("head", None, "ctx"),
        check_vma=False,
    )
```

```python
import functools

import jax
import jax.numpy as jnp
from jax import lax
from jax.experimental import pallas as pl
from jax.experimental.pallas import tpu as pltpu
from jax.sharding import PartitionSpec as P

HQ = 64
KVH = 8
HD = 128
PAGE = 64
GROUPS = HQ // KVH
STAT_ROWS = 16
MASKED = -3e38
FLOOR = -1.5e38
WEIGHT_PIECES = 4
VMEM_LIMIT = 24 * 1024 * 1024

VMEM = pl.BlockSpec(memory_space=pltpu.VMEM)
ANY = pl.BlockSpec(memory_space=pl.ANY)
HBM = pl.BlockSpec(memory_space=pltpu.HBM)
NT = (((1,), (1,)), ((), ()))


def query_rows(q_ref, slot, turned):
    steps, width = q_ref.shape[1:]
    for j in range(width // HD):
        piece = q_ref[slot, :, j * HD : (j + 1) * HD]
        turned[j * steps : (j + 1) * steps, :] = piece.astype(jnp.float32)
    return turned[...].astype(jnp.bfloat16)


def spread_heads(query, heads):
    rows = query.shape[0]
    row_head = lax.broadcasted_iota(jnp.int32, (rows, heads * HD), 0) // (rows // heads)
    lane_head = lax.broadcasted_iota(jnp.int32, (rows, heads * HD), 1) // HD
    wide = jnp.concatenate([query] * heads, axis=1)
    return jnp.where(row_head == lane_head, wide, jnp.zeros_like(wide))


def own_heads(weighted, heads):
    span = weighted.shape[0] // heads
    return jnp.concatenate(
        [weighted[h * span : (h + 1) * span, h * HD : (h + 1) * HD] for h in range(heads)], axis=0
    )


def three_parts(x):
    high = x.astype(jnp.bfloat16).astype(jnp.float32)
    rest = x - high
    middle = rest.astype(jnp.bfloat16).astype(jnp.float32)
    return high, middle, rest - middle


def stat_rows(slots):
    return -(-3 * slots // STAT_ROWS) * STAT_ROWS


def stat_block(columns):
    rows = columns[0].shape[0]
    lane = lax.broadcasted_iota(jnp.int32, (rows, 128), 1)
    sheet = jnp.zeros((rows, 128), jnp.float32)
    for i, column in enumerate(columns):
        sheet = jnp.where(lane == i, column, sheet)
    sheet = jnp.concatenate([sheet, jnp.zeros((128 - rows, 128), jnp.float32)], axis=0)
    count = len(columns)
    parts = list(three_parts(jnp.transpose(sheet)[:count]))
    spare = stat_rows(count) - 3 * count
    if spare:
        parts.append(jnp.zeros((spare, 128), jnp.float32))
    return jnp.concatenate(parts, axis=0).astype(jnp.bfloat16)


def own_kernel(
    q_in, kv_in, selected_in, new_in, q_out, kv_out, bits_out, new_out, selected_ref, new_ref, sems
):
    steps, _, heads, _ = selected_ref.shape
    m, pages = kv_out.shape[:2]
    me = lax.axis_index("ctx")
    pairs = [(selected_in, selected_ref), (new_in, new_ref), (q_in, q_out)]
    pairs += [(kv_in.at[me ^ (2 * i)], kv_out.at[i]) for i in range(m)]
    copies = [pltpu.make_async_copy(*pair, sems.at[i]) for i, pair in enumerate(pairs)]
    for copy in copies:
        copy.start()
    for copy in copies[:2]:
        copy.wait()
    by_step = []
    for s in range(steps):
        lists = jnp.concatenate([selected_ref[s, me ^ (2 * i)] for i in range(m)], axis=0)
        for core in range(2):
            page = lists - (me ^ core) * pages
            here = (page >= 0) & (page < pages)
            bit = jnp.where(here, jnp.left_shift(1, page & 31), 0).astype(jnp.float32)
            total = jnp.sum(bit, axis=1, keepdims=True).astype(jnp.int32)
            by_step.append(jnp.broadcast_to(total, (m * heads, 128)))
    step_of = lax.broadcasted_iota(jnp.int32, (8, 128), 0) % steps
    for core in range(2):
        for i in range(m):
            for h in range(heads):
                row = i * heads + h
                bits = jnp.zeros((8, 128), jnp.int32)
                for s in range(steps):
                    bits = jnp.where(step_of == s, by_step[2 * s + core][row : row + 1], bits)
                bits_out[core, i, h] = bits
    for part in range(2):
        tokens = [new_ref[s, part : part + 1].astype(jnp.float32) for s in range(steps)]
        blank = jnp.zeros((16 - steps, new_ref.shape[2]), jnp.float32)
        new_out[part] = jnp.concatenate(tokens + [blank], axis=0).astype(jnp.bfloat16)
    for copy in copies[2:]:
        copy.wait()


def own_side(queries, kv_cache, selected, new_kv):
    batch, heads = selected.shape[1:3]
    m = batch // 2
    operands = (queries, kv_cache, selected, new_kv)
    return pl.pallas_call(
        own_kernel,
        out_shape=[
            jax.ShapeDtypeStruct(queries.shape, queries.dtype),
            jax.ShapeDtypeStruct((m,) + kv_cache.shape[1:], kv_cache.dtype),
            jax.ShapeDtypeStruct((2, m, heads, 8, 128), jnp.int32),
            jax.ShapeDtypeStruct((2, 16, new_kv.shape[2]), jnp.bfloat16),
        ],
        in_specs=[HBM] * 4,
        out_specs=[VMEM] * 4,
        scratch_shapes=[
            pltpu.VMEM(selected.shape, selected.dtype),
            pltpu.VMEM(new_kv.shape, new_kv.dtype),
            pltpu.SemaphoreType.DMA((3 + m,)),
        ],
        compiler_params=pltpu.CompilerParams(vmem_limit_bytes=VMEM_LIMIT),
        cost_estimate=pl.CostEstimate(
            flops=2**20, bytes_accessed=kv_cache.size * 2, transcendentals=0
        ),
    )(*[pltpu.with_memory_space_constraint(x, pltpu.HBM) for x in operands])


def page_masks(bits_ref, core, i, steps, page_bit):
    masks = []
    for h in range(bits_ref.shape[2]):
        bits = jnp.concatenate([bits_ref[core, i, h]] * (page_bit.shape[1] // 128), axis=1)
        masks += [(page_bit & bits) != 0] * steps
    return jnp.concatenate(masks, axis=0)


def attend(spread, pieces):
    found = []
    for keys, values, allowed in pieces:
        scores = lax.dot_general(spread, keys, NT, preferred_element_type=jnp.float32)
        found.append((jnp.where(allowed, scores * HD ** (-0.5), MASKED), values))

    def finish():
        tops = [jnp.max(scores, axis=1, keepdims=True) for scores, _ in found]
        top = jnp.maximum(functools.reduce(jnp.maximum, tops), FLOOR)
        total, weighted = 0.0, 0.0
        for scores, values in found:
            expo = jnp.exp(scores - top)
            total = total + jnp.sum(expo, axis=1, keepdims=True)
            weighted = weighted + jnp.dot(
                expo.astype(jnp.bfloat16), values, preferred_element_type=jnp.float32
            )
        return top, total, weighted

    return finish


def page_pieces(kv_ref, where, bits_ref, core, i, steps, heads):
    tokens = kv_ref.shape[1] * PAGE
    page_bit = jnp.left_shift(1, lax.broadcasted_iota(jnp.int32, (8, tokens), 1) // PAGE)
    keys = kv_ref[where, :, 0].reshape(tokens, heads * HD)
    values = kv_ref[where, :, 1].reshape(tokens, heads * HD)
    return keys, values, page_masks(bits_ref, core, i, steps, page_bit)


def staged(count, ahead, begin, end):
    begun = [begin(i) for i in range(min(ahead, count))]
    for i in range(count):
        if i + ahead < count:
            begun.append(begin(i + ahead))
        end(i, begun[i])


def first_kernel(heads, bits_ref, new_ref, own_ref, *refs):
    *q_refs, spread_ref, sum_ref, top_ref, total_ref, turned = refs
    steps = q_refs[0].shape[1]
    rows = turned.shape[1]

    def begin(i):
        spread = spread_heads(query_rows(q_refs[i], 0, turned.at[i]), heads)
        spread_ref[i] = spread
        pieces = [page_pieces(own_ref, i, bits_ref, 0, i, steps, heads)]
        if i == 0:
            step_of = lax.broadcasted_iota(jnp.int32, (rows, 16), 0) % steps
            causal = lax.broadcasted_iota(jnp.int32, (rows, 16), 1) <= step_of
            pieces.append((new_ref[0], new_ref[1], causal))
        return attend(spread, pieces)

    def end(i, finish):
        top, total, weighted = finish()
        top_ref[i] = jnp.broadcast_to(top, (rows, 128))
        total_ref[i] = jnp.broadcast_to(total, (rows, 128))
        sum_ref[i] = own_heads(weighted, heads)

    staged(len(q_refs), 1, begin, end)


def second_kernel(
    steps, heads, bits_ref, spread_ref, sum_ref, top_ref, total_ref, other_ref, out_ref
):
    m, rows = spread_ref.shape[:2]
    me = lax.axis_index("ctx")
    columns = []

    def begin(i):
        pieces = [page_pieces(other_ref, me ^ (2 * i), bits_ref, 1, i, steps, heads)]
        return attend(spread_ref[i], pieces)

    def end(i, finish):
        first_top, first_total = top_ref[i], total_ref[i]
        top, total, weighted = finish()
        top = jnp.broadcast_to(top, (rows, 128))
        both = jnp.maximum(top, first_top)
        factor, first_factor = jnp.exp(top - both), jnp.exp(first_top - both)
        total = jnp.broadcast_to(total, (rows, 128)) * factor + first_total * first_factor
        total = jnp.where(total > 0.0, total, 1.0)
        share = 1.0 / total
        joined = own_heads(weighted, heads) * (factor * share)
        joined = joined + sum_ref[i] * (first_factor * share)
        out_ref[i * rows : (i + 1) * rows, :] = joined.astype(jnp.bfloat16)
        columns.append(both + jnp.log(total))

    staged(m, m if m <= 4 else 2, begin, end)
    out_ref[m * rows :, :] = stat_block(columns)


def partials(bits, new_pairs, own_kv, other_kv, queries, rows, heads):
    m, pages = own_kv.shape[:2]
    tokens, width = pages * PAGE, own_kv.shape[4]
    steps = queries[0].shape[1]
    options = dict(
        compiler_params=pltpu.CompilerParams(vmem_limit_bytes=VMEM_LIMIT),
        cost_estimate=pl.CostEstimate(
            flops=4 * m * rows * tokens * width,
            bytes_accessed=2**20,
            transcendentals=m * rows * tokens,
        ),
    )
    state = pl.pallas_call(
        functools.partial(first_kernel, heads),
        out_shape=[
            jax.ShapeDtypeStruct((m, rows, width), jnp.bfloat16),
            jax.ShapeDtypeStruct((m, rows, HD), jnp.float32),
            jax.ShapeDtypeStruct((m, rows, 128), jnp.float32),
            jax.ShapeDtypeStruct((m, rows, 128), jnp.float32),
        ],
        in_specs=[VMEM] * (3 + m),
        out_specs=[VMEM] * 4,
        scratch_shapes=[pltpu.VMEM((m, rows, HD), jnp.float32)],
        **options,
    )(bits, new_pairs, own_kv, *queries)
    return pl.pallas_call(
        functools.partial(second_kernel, steps, heads),
        out_shape=jax.ShapeDtypeStruct((m * rows + stat_rows(m), HD), jnp.bfloat16),
        in_specs=[VMEM] * 6,
        out_specs=VMEM,
        **options,
    )(bits, *state, other_kv)


def last_merge_kernel(rows, steps, *refs):
    *part_refs, _, out_ref = refs
    m = len(part_refs)
    logs = []
    for j, ref in enumerate(part_refs):
        stats = ref[m * rows :, :].astype(jnp.float32)
        log = stats[:m] + stats[m : 2 * m] + stats[2 * m : 3 * m]
        if j:
            log = jnp.concatenate([log[i ^ j : (i ^ j) + 1] for i in range(m)], axis=0)
        logs.append(log)
    top = functools.reduce(jnp.maximum, logs)
    factors = [jnp.exp(log - top) for log in logs]
    share = 1.0 / functools.reduce(jnp.add, factors)
    lane = lax.broadcasted_iota(jnp.int32, (m, 128), 1) // rows
    beside = 128 // rows
    packed = []
    for first in range(0, m, beside):
        wide = jnp.zeros((m, 128), jnp.float32)
        for p in range(min(beside, m - first)):
            weight = factors[first + p] * share
            if p:
                weight = jnp.concatenate(
                    [weight[:, 128 - p * rows :], weight[:, : 128 - p * rows]], axis=1
                )
            wide = jnp.where(lane == p, weight, wide)
        packed.append(wide)
    on_row = lax.broadcasted_iota(jnp.int32, (rows, 128), 0)
    diagonal = lax.broadcasted_iota(jnp.int32, (rows, 128), 1) % rows == on_row
    joined = []
    for i in range(m):
        weights = jnp.concatenate(
            [jnp.where(diagonal, wide[i : i + 1], 0.0) for wide in packed], axis=1
        )
        parts = jnp.concatenate(
            [ref[(i ^ j) * rows : ((i ^ j) + 1) * rows, :] for j, ref in enumerate(part_refs)],
            axis=0,
        )
        high = weights.astype(jnp.bfloat16)
        low = (weights - high.astype(jnp.float32)).astype(jnp.bfloat16)
        both = jnp.concatenate([high, low], axis=0)
        product = jnp.dot(both, parts, preferred_element_type=jnp.float32)
        joined.append(product[:rows] + product[rows:])
    for j in range(rows // steps):
        piece = jnp.concatenate([x[j * steps : (j + 1) * steps] for x in joined], axis=0)
        out_ref[:, j * HD : (j + 1) * HD] = piece.astype(jnp.bfloat16)


def last_merge(parts, weight, rows, steps):
    m = len(parts)
    return pl.pallas_call(
        functools.partial(last_merge_kernel, rows, steps),
        out_shape=jax.ShapeDtypeStruct((m * steps, rows // steps * HD), jnp.bfloat16),
        in_specs=[VMEM] * m + [ANY],
        out_specs=VMEM,
        compiler_params=pltpu.CompilerParams(vmem_limit_bytes=VMEM_LIMIT),
        cost_estimate=pl.CostEstimate(
            flops=2 * m * m * rows * HD, bytes_accessed=2**18, transcendentals=0
        ),
    )(*parts, weight)


def load_kernel(weight_ref, _, out_ref, sems):
    piece = out_ref.shape[0] // WEIGHT_PIECES
    copies = []
    for i in range(WEIGHT_PIECES):
        span = pl.ds(i * piece, piece)
        copy = pltpu.make_async_copy(weight_ref.at[span], out_ref.at[span], sems.at[i])
        copy.start()
        copies.append(copy)
    for copy in copies:
        copy.wait()


def load_weight(out_weight, after):
    return pl.pallas_call(
        load_kernel,
        out_shape=jax.ShapeDtypeStruct(out_weight.shape, out_weight.dtype),
        in_specs=[HBM, ANY],
        out_specs=VMEM,
        scratch_shapes=[pltpu.SemaphoreType.DMA((WEIGHT_PIECES,))],
        compiler_params=pltpu.CompilerParams(vmem_limit_bytes=VMEM_LIMIT),
        cost_estimate=pl.CostEstimate(
            flops=0, bytes_accessed=out_weight.size * 4, transcendentals=0
        ),
    )(pltpu.with_memory_space_constraint(out_weight, pltpu.HBM), after)


def half_kernel(att_ref, weight_ref, out_ref):
    out_ref[...] = jnp.dot(att_ref[...], weight_ref[...], preferred_element_type=jnp.float32)


def project_kernel(n_head, targets, att_ref, half_ref, weight_ref, *refs):
    *out_refs, rows_all = refs
    seqs, steps, _ = out_refs[0].shape
    me = lax.axis_index("ctx")
    mine = lax.axis_index("head")
    product = jnp.dot(att_ref[...], weight_ref[...], preferred_element_type=jnp.float32)
    for i in range(rows_all.shape[0] // 2):
        rows_all[2 * i, :steps, :] = product[i * steps : (i + 1) * steps]
        rows_all[2 * i + 1, :steps, :] = half_ref[i * steps : (i + 1) * steps, :]
    for k, ref in enumerate(out_refs):
        target = mine
        if k > 0:
            for core, row in enumerate(targets[k - 1]):
                for z, t in enumerate(row):
                    target = jnp.where((me % 2 == core) & (mine == z), t, target)
        for j in range(seqs):
            found = rows_all[(jnp.maximum(target, 0) * seqs + j) ^ me, :steps]
            if k > 0 and any(t < 0 for row in targets[k - 1] for t in row):
                found = jnp.where(target < 0, 0.0, found)
            ref[j] = found.astype(ref.dtype)


def project_options(att, weight):
    width, columns = weight.shape
    return dict(
        compiler_params=pltpu.CompilerParams(vmem_limit_bytes=VMEM_LIMIT),
        cost_estimate=pl.CostEstimate(
            flops=2 * att.size * columns, bytes_accessed=width * columns * 2, transcendentals=0
        ),
    )


def project_half(att, weight):
    return pl.pallas_call(
        half_kernel,
        out_shape=jax.ShapeDtypeStruct((att.shape[0], weight.shape[1]), jnp.float32),
        in_specs=[VMEM] * 2,
        out_specs=VMEM,
        **project_options(att, weight),
    )(att, weight)


def project(att, half, weight, steps, n_head, targets):
    n = 2 * att.shape[0] // steps
    columns = weight.shape[1]
    outs = [
        jax.ShapeDtypeStruct((n // n_head, steps, columns), jnp.bfloat16 if k else jnp.float32)
        for k in range(1 + len(targets))
    ]
    return pl.pallas_call(
        functools.partial(project_kernel, n_head, targets),
        out_shape=outs,
        in_specs=[VMEM] * 3,
        out_specs=[VMEM] * len(outs),
        scratch_shapes=[pltpu.VMEM((n, 8, columns), jnp.float32)],
        **project_options(att, weight),
    )(att, half, weight)


def head_plan(n_head):
    if n_head == 4:
        return [
            (((1, 0), (1, 1), (0, 0), (1, 3)), ((1, 2), (0, 1), (0, 2), (0, 3))),
            (((0, 1), (0, 2), (0, 3), (0, 0)), ((1, 1), (1, 3), (1, 0), (1, 2))),
            (((0, 3), (0, 0), (0, 1), (0, 2)), ((1, 3), (1, 2), (1, 1), (1, 0))),
            (((0, 2), (0, 3), (1, 2), (0, 1)), ((0, 0), (1, 0), (1, 3), (1, 1))),
        ]
    return [
        tuple(tuple((core, (z + t) % n_head) for z in range(n_head)) for core in range(2))
        for t in range(1, n_head)
    ]


def plan_targets(plan):
    seen = set()
    targets = []
    for permutation in plan:
        rows = []
        for core, row in enumerate(permutation):
            rows.append([])
            for z, (to_core, t) in enumerate(row):
                useful = to_core == core and (core, z, t) not in seen
                rows[core].append(t if useful else -1)
                if useful:
                    seen.add((core, z, t))
        targets.append(rows)
    return targets


def send_by(permutation, x):
    n, n_head = lax.axis_size("ctx"), lax.axis_size("head")
    pairs = []
    for c in range(n):
        for z in range(n_head):
            core, t = permutation[c % 2][z]
            pairs.append((c * n_head + z, (c - c % 2 + core) * n_head + t))
    return lax.ppermute(x, ("ctx", "head"), pairs)


def swap(x, axis, r):
    size = lax.axis_size(axis)
    return lax.ppermute(x, axis, [(i, i ^ r) for i in range(size)])


def swap_chips(x, n):
    return [swap(x, "ctx", r) for r in range(2, n, 2)]


def swap_other_cores(x, n):
    return [swap(x, "ctx", r) for r in range(1, n, 2)]


def local(queries, kv_cache, new_kv, selected, out_weight):
    steps, _, width = queries.shape
    heads = kv_cache.shape[4] // HD
    rows = steps * heads * GROUPS
    n = lax.axis_size("ctx")
    n_head = lax.axis_size("head")

    first_q = queries.reshape(1, steps, width)
    other_kv = swap(kv_cache, "ctx", 1)
    far_q = swap_chips(first_q, n)
    new_pairs = new_kv.reshape(steps, 2, heads * HD)
    own_q, own_kv, bits, new_pairs = own_side(first_q, kv_cache, selected, new_pairs)
    all_q = [own_q] + far_q
    sent = partials(bits, new_pairs, own_kv, other_kv, all_q, rows, heads)
    parts = swap_other_cores(sent, n)
    weight = load_weight(out_weight, sent)
    odd_att = last_merge(parts, weight, rows, steps)
    even_att = swap(odd_att, "ctx", 1)
    plan = head_plan(n_head)
    half = project_half(odd_att, weight)
    total, *rows_out = project(
        even_att, half, weight, steps, n_head, plan_targets(plan)
    )
    for chunk, permutation in zip(rows_out, plan):
        total = total + send_by(permutation, chunk).astype(jnp.float32)
    return total.astype(jnp.bfloat16)


def solution(mesh):
    return jax.shard_map(
        local,
        mesh=mesh,
        in_specs=(
            P(None, "ctx", "head"),
            P(None, "ctx", None, None, "head"),
            P(None, "ctx", None, "head"),
            P(None, None, "head", None),
            P("head", "ctx"),
        ),
        out_specs=P("head", None, "ctx"),
        check_vma=False,
    )
```

```python
import functools

import jax
import jax.numpy as jnp
from jax import lax
from jax.experimental import pallas as pl
from jax.experimental.pallas import tpu as pltpu
from jax.sharding import PartitionSpec as P

HQ = 64
KVH = 8
HD = 128
PAGE = 64
GROUPS = HQ // KVH
STAT_ROWS = 16
MASKED = -3e38
FLOOR = -1.5e38
WEIGHT_PIECES = 4
VMEM_LIMIT = 24 * 1024 * 1024

VMEM = pl.BlockSpec(memory_space=pltpu.VMEM)
ANY = pl.BlockSpec(memory_space=pl.ANY)
HBM = pl.BlockSpec(memory_space=pltpu.HBM)
NT = (((1,), (1,)), ((), ()))


def query_rows(q_ref, slot, turned):
    steps, width = q_ref.shape[1:]
    for j in range(width // HD):
        piece = q_ref[slot, :, j * HD : (j + 1) * HD]
        turned[j * steps : (j + 1) * steps, :] = piece.astype(jnp.float32)
    return turned[...].astype(jnp.bfloat16)


def spread_heads(query, heads):
    rows = query.shape[0]
    row_head = lax.broadcasted_iota(jnp.int32, (rows, heads * HD), 0) // (rows // heads)
    lane_head = lax.broadcasted_iota(jnp.int32, (rows, heads * HD), 1) // HD
    wide = jnp.concatenate([query] * heads, axis=1)
    return jnp.where(row_head == lane_head, wide, jnp.zeros_like(wide))


def own_heads(weighted, heads):
    span = weighted.shape[0] // heads
    return jnp.concatenate(
        [weighted[h * span : (h + 1) * span, h * HD : (h + 1) * HD] for h in range(heads)], axis=0
    )


def three_parts(x):
    high = x.astype(jnp.bfloat16).astype(jnp.float32)
    rest = x - high
    middle = rest.astype(jnp.bfloat16).astype(jnp.float32)
    return high, middle, rest - middle


def stat_rows(slots):
    return -(-3 * slots // STAT_ROWS) * STAT_ROWS


def stat_block(columns):
    rows = columns[0].shape[0]
    lane = lax.broadcasted_iota(jnp.int32, (rows, 128), 1)
    sheet = jnp.zeros((rows, 128), jnp.float32)
    for i, column in enumerate(columns):
        sheet = jnp.where(lane == i, column, sheet)
    sheet = jnp.concatenate([sheet, jnp.zeros((128 - rows, 128), jnp.float32)], axis=0)
    count = len(columns)
    parts = list(three_parts(jnp.transpose(sheet)[:count]))
    spare = stat_rows(count) - 3 * count
    if spare:
        parts.append(jnp.zeros((spare, 128), jnp.float32))
    return jnp.concatenate(parts, axis=0).astype(jnp.bfloat16)


def own_kernel(
    q_in, kv_in, selected_in, new_in, q_out, kv_out, bits_out, new_out, selected_ref, new_ref, sems
):
    steps, _, heads, _ = selected_ref.shape
    m, pages = kv_out.shape[:2]
    me = lax.axis_index("ctx")
    pairs = [(selected_in, selected_ref), (new_in, new_ref), (q_in, q_out)]
    pairs += [(kv_in.at[me ^ (2 * i)], kv_out.at[i]) for i in range(m)]
    copies = [pltpu.make_async_copy(*pair, sems.at[i]) for i, pair in enumerate(pairs)]
    for copy in copies:
        copy.start()
    for copy in copies[:2]:
        copy.wait()
    by_step = []
    for s in range(steps):
        lists = jnp.concatenate([selected_ref[s, me ^ (2 * i)] for i in range(m)], axis=0)
        for core in range(2):
            page = lists - (me ^ core) * pages
            here = (page >= 0) & (page < pages)
            bit = jnp.where(here, jnp.left_shift(1, page & 31), 0).astype(jnp.float32)
            total = jnp.sum(bit, axis=1, keepdims=True).astype(jnp.int32)
            by_step.append(jnp.broadcast_to(total, (m * heads, 128)))
    step_of = lax.broadcasted_iota(jnp.int32, (8, 128), 0) % steps
    for core in range(2):
        for i in range(m):
            for h in range(heads):
                row = i * heads + h
                bits = jnp.zeros((8, 128), jnp.int32)
                for s in range(steps):
                    bits = jnp.where(step_of == s, by_step[2 * s + core][row : row + 1], bits)
                bits_out[core, i, h] = bits
    for part in range(2):
        tokens = [new_ref[s, part : part + 1].astype(jnp.float32) for s in range(steps)]
        blank = jnp.zeros((16 - steps, new_ref.shape[2]), jnp.float32)
        new_out[part] = jnp.concatenate(tokens + [blank], axis=0).astype(jnp.bfloat16)
    for copy in copies[2:]:
        copy.wait()


def own_side(queries, kv_cache, selected, new_kv):
    batch, heads = selected.shape[1:3]
    m = batch // 2
    operands = (queries, kv_cache, selected, new_kv)
    return pl.pallas_call(
        own_kernel,
        out_shape=[
            jax.ShapeDtypeStruct(queries.shape, queries.dtype),
            jax.ShapeDtypeStruct((m,) + kv_cache.shape[1:], kv_cache.dtype),
            jax.ShapeDtypeStruct((2, m, heads, 8, 128), jnp.int32),
            jax.ShapeDtypeStruct((2, 16, new_kv.shape[2]), jnp.bfloat16),
        ],
        in_specs=[HBM] * 4,
        out_specs=[VMEM] * 4,
        scratch_shapes=[
            pltpu.VMEM(selected.shape, selected.dtype),
            pltpu.VMEM(new_kv.shape, new_kv.dtype),
            pltpu.SemaphoreType.DMA((3 + m,)),
        ],
        compiler_params=pltpu.CompilerParams(vmem_limit_bytes=VMEM_LIMIT),
        cost_estimate=pl.CostEstimate(
            flops=2**20, bytes_accessed=kv_cache.size * 2, transcendentals=0
        ),
    )(*[pltpu.with_memory_space_constraint(x, pltpu.HBM) for x in operands])


def page_masks(bits_ref, core, i, steps, page_bit):
    masks = []
    for h in range(bits_ref.shape[2]):
        bits = jnp.concatenate([bits_ref[core, i, h]] * (page_bit.shape[1] // 128), axis=1)
        masks += [(page_bit & bits) != 0] * steps
    return jnp.concatenate(masks, axis=0)


def attend(spread, pieces):
    found = []
    for keys, values, allowed in pieces:
        scores = lax.dot_general(spread, keys, NT, preferred_element_type=jnp.float32)
        found.append((jnp.where(allowed, scores * HD ** (-0.5), MASKED), values))

    def finish():
        tops = [jnp.max(scores, axis=1, keepdims=True) for scores, _ in found]
        top = jnp.maximum(functools.reduce(jnp.maximum, tops), FLOOR)
        total, weighted = 0.0, 0.0
        for scores, values in found:
            expo = jnp.exp(scores - top)
            total = total + jnp.sum(expo, axis=1, keepdims=True)
            weighted = weighted + jnp.dot(
                expo.astype(jnp.bfloat16), values, preferred_element_type=jnp.float32
            )
        return top, total, weighted

    return finish


def page_pieces(kv_ref, where, bits_ref, core, i, steps, heads):
    tokens = kv_ref.shape[1] * PAGE
    page_bit = jnp.left_shift(1, lax.broadcasted_iota(jnp.int32, (8, tokens), 1) // PAGE)
    keys = kv_ref[where, :, 0].reshape(tokens, heads * HD)
    values = kv_ref[where, :, 1].reshape(tokens, heads * HD)
    return keys, values, page_masks(bits_ref, core, i, steps, page_bit)


def staged(count, ahead, begin, end):
    begun = [begin(i) for i in range(min(ahead, count))]
    for i in range(count):
        if i + ahead < count:
            begun.append(begin(i + ahead))
        end(i, begun[i])


def first_kernel(heads, bits_ref, new_ref, own_ref, *refs):
    *q_refs, spread_ref, sum_ref, top_ref, total_ref, turned = refs
    steps = q_refs[0].shape[1]
    rows = turned.shape[1]

    def begin(i):
        spread = spread_heads(query_rows(q_refs[i], 0, turned.at[i]), heads)
        spread_ref[i] = spread
        pieces = [page_pieces(own_ref, i, bits_ref, 0, i, steps, heads)]
        if i == 0:
            step_of = lax.broadcasted_iota(jnp.int32, (rows, 16), 0) % steps
            causal = lax.broadcasted_iota(jnp.int32, (rows, 16), 1) <= step_of
            pieces.append((new_ref[0], new_ref[1], causal))
        return attend(spread, pieces)

    def end(i, finish):
        top, total, weighted = finish()
        top_ref[i] = jnp.broadcast_to(top, (rows, 128))
        total_ref[i] = jnp.broadcast_to(total, (rows, 128))
        sum_ref[i] = own_heads(weighted, heads)

    staged(len(q_refs), 1, begin, end)


def second_kernel(
    steps, heads, bits_ref, spread_ref, sum_ref, top_ref, total_ref, other_ref, out_ref
):
    m, rows = spread_ref.shape[:2]
    me = lax.axis_index("ctx")
    columns = []

    def begin(i):
        pieces = [page_pieces(other_ref, me ^ (2 * i), bits_ref, 1, i, steps, heads)]
        return attend(spread_ref[i], pieces)

    def end(i, finish):
        first_top, first_total = top_ref[i], total_ref[i]
        top, total, weighted = finish()
        top = jnp.broadcast_to(top, (rows, 128))
        both = jnp.maximum(top, first_top)
        factor, first_factor = jnp.exp(top - both), jnp.exp(first_top - both)
        total = jnp.broadcast_to(total, (rows, 128)) * factor + first_total * first_factor
        total = jnp.where(total > 0.0, total, 1.0)
        share = 1.0 / total
        joined = own_heads(weighted, heads) * (factor * share)
        joined = joined + sum_ref[i] * (first_factor * share)
        out_ref[i * rows : (i + 1) * rows, :] = joined.astype(jnp.bfloat16)
        columns.append(both + jnp.log(total))

    staged(m, m if m <= 4 else 2, begin, end)
    out_ref[m * rows :, :] = stat_block(columns)


def partials(bits, new_pairs, own_kv, other_kv, queries, rows, heads):
    m, pages = own_kv.shape[:2]
    tokens, width = pages * PAGE, own_kv.shape[4]
    steps = queries[0].shape[1]
    options = dict(
        compiler_params=pltpu.CompilerParams(vmem_limit_bytes=VMEM_LIMIT),
        cost_estimate=pl.CostEstimate(
            flops=4 * m * rows * tokens * width,
            bytes_accessed=2**20,
            transcendentals=m * rows * tokens,
        ),
    )
    state = pl.pallas_call(
        functools.partial(first_kernel, heads),
        out_shape=[
            jax.ShapeDtypeStruct((m, rows, width), jnp.bfloat16),
            jax.ShapeDtypeStruct((m, rows, HD), jnp.float32),
            jax.ShapeDtypeStruct((m, rows, 128), jnp.float32),
            jax.ShapeDtypeStruct((m, rows, 128), jnp.float32),
        ],
        in_specs=[VMEM] * (3 + m),
        out_specs=[VMEM] * 4,
        scratch_shapes=[pltpu.VMEM((m, rows, HD), jnp.float32)],
        **options,
    )(bits, new_pairs, own_kv, *queries)
    return pl.pallas_call(
        functools.partial(second_kernel, steps, heads),
        out_shape=jax.ShapeDtypeStruct((m * rows + stat_rows(m), HD), jnp.bfloat16),
        in_specs=[VMEM] * 6,
        out_specs=VMEM,
        **options,
    )(bits, *state, other_kv)


def last_merge_kernel(rows, steps, *refs):
    *part_refs, _, out_ref = refs
    m = len(part_refs)
    logs = []
    for j, ref in enumerate(part_refs):
        stats = ref[m * rows :, :].astype(jnp.float32)
        log = stats[:m] + stats[m : 2 * m] + stats[2 * m : 3 * m]
        if j:
            log = jnp.concatenate([log[i ^ j : (i ^ j) + 1] for i in range(m)], axis=0)
        logs.append(log)
    top = functools.reduce(jnp.maximum, logs)
    factors = [jnp.exp(log - top) for log in logs]
    share = 1.0 / functools.reduce(jnp.add, factors)
    lane = lax.broadcasted_iota(jnp.int32, (m, 128), 1) // rows
    beside = 128 // rows
    packed = []
    for first in range(0, m, beside):
        wide = jnp.zeros((m, 128), jnp.float32)
        for p in range(min(beside, m - first)):
            weight = factors[first + p] * share
            if p:
                weight = jnp.concatenate(
                    [weight[:, 128 - p * rows :], weight[:, : 128 - p * rows]], axis=1
                )
            wide = jnp.where(lane == p, weight, wide)
        packed.append(wide)
    on_row = lax.broadcasted_iota(jnp.int32, (rows, 128), 0)
    diagonal = lax.broadcasted_iota(jnp.int32, (rows, 128), 1) % rows == on_row
    joined = []
    for i in range(m):
        weights = jnp.concatenate(
            [jnp.where(diagonal, wide[i : i + 1], 0.0) for wide in packed], axis=1
        )
        parts = jnp.concatenate(
            [ref[(i ^ j) * rows : ((i ^ j) + 1) * rows, :] for j, ref in enumerate(part_refs)],
            axis=0,
        )
        high = weights.astype(jnp.bfloat16)
        low = (weights - high.astype(jnp.float32)).astype(jnp.bfloat16)
        both = jnp.concatenate([high, low], axis=0)
        product = jnp.dot(both, parts, preferred_element_type=jnp.float32)
        joined.append(product[:rows] + product[rows:])
    for j in range(rows // steps):
        piece = jnp.concatenate([x[j * steps : (j + 1) * steps] for x in joined], axis=0)
        out_ref[:, j * HD : (j + 1) * HD] = piece.astype(jnp.bfloat16)


def last_merge(parts, weight, rows, steps):
    m = len(parts)
    return pl.pallas_call(
        functools.partial(last_merge_kernel, rows, steps),
        out_shape=jax.ShapeDtypeStruct((m * steps, rows // steps * HD), jnp.bfloat16),
        in_specs=[VMEM] * m + [ANY],
        out_specs=VMEM,
        compiler_params=pltpu.CompilerParams(vmem_limit_bytes=VMEM_LIMIT),
        cost_estimate=pl.CostEstimate(
            flops=2 * m * m * rows * HD, bytes_accessed=2**18, transcendentals=0
        ),
    )(*parts, weight)


def load_kernel(weight_ref, _, out_ref, sems):
    piece = out_ref.shape[0] // WEIGHT_PIECES
    copies = []
    for i in range(WEIGHT_PIECES):
        span = pl.ds(i * piece, piece)
        copy = pltpu.make_async_copy(weight_ref.at[span], out_ref.at[span], sems.at[i])
        copy.start()
        copies.append(copy)
    for copy in copies:
        copy.wait()


def load_weight(out_weight, after):
    return pl.pallas_call(
        load_kernel,
        out_shape=jax.ShapeDtypeStruct(out_weight.shape, out_weight.dtype),
        in_specs=[HBM, ANY],
        out_specs=VMEM,
        scratch_shapes=[pltpu.SemaphoreType.DMA((WEIGHT_PIECES,))],
        compiler_params=pltpu.CompilerParams(vmem_limit_bytes=VMEM_LIMIT),
        cost_estimate=pl.CostEstimate(
            flops=0, bytes_accessed=out_weight.size * 4, transcendentals=0
        ),
    )(pltpu.with_memory_space_constraint(out_weight, pltpu.HBM), after)


def half_kernel(att_ref, weight_ref, out_ref):
    out_ref[...] = jnp.dot(att_ref[...], weight_ref[...], preferred_element_type=jnp.float32)


def project_kernel(n_head, targets, att_ref, half_ref, weight_ref, *refs):
    *out_refs, rows_all = refs
    seqs, steps, _ = out_refs[0].shape
    me = lax.axis_index("ctx")
    mine = lax.axis_index("head")
    product = jnp.dot(att_ref[...], weight_ref[...], preferred_element_type=jnp.float32)
    for i in range(rows_all.shape[0] // 2):
        rows_all[2 * i, :steps, :] = product[i * steps : (i + 1) * steps]
        rows_all[2 * i + 1, :steps, :] = half_ref[i * steps : (i + 1) * steps, :]
    for k, ref in enumerate(out_refs):
        target = mine
        if k > 0:
            for core, row in enumerate(targets[k - 1]):
                for z, t in enumerate(row):
                    target = jnp.where((me % 2 == core) & (mine == z), t, target)
        for j in range(seqs):
            found = rows_all[(jnp.maximum(target, 0) * seqs + j) ^ me, :steps]
            if k > 0 and any(t < 0 for row in targets[k - 1] for t in row):
                found = jnp.where(target < 0, 0.0, found)
            ref[j] = found.astype(ref.dtype)


def project_options(att, weight):
    width, columns = weight.shape
    return dict(
        compiler_params=pltpu.CompilerParams(vmem_limit_bytes=VMEM_LIMIT),
        cost_estimate=pl.CostEstimate(
            flops=2 * att.size * columns, bytes_accessed=width * columns * 2, transcendentals=0
        ),
    )


def project_half(att, weight):
    return pl.pallas_call(
        half_kernel,
        out_shape=jax.ShapeDtypeStruct((att.shape[0], weight.shape[1]), jnp.float32),
        in_specs=[VMEM] * 2,
        out_specs=VMEM,
        **project_options(att, weight),
    )(att, weight)


def project(att, half, weight, steps, n_head, targets):
    n = 2 * att.shape[0] // steps
    columns = weight.shape[1]
    outs = [
        jax.ShapeDtypeStruct((n // n_head, steps, columns), jnp.bfloat16 if k else jnp.float32)
        for k in range(1 + len(targets))
    ]
    return pl.pallas_call(
        functools.partial(project_kernel, n_head, targets),
        out_shape=outs,
        in_specs=[VMEM] * 3,
        out_specs=[VMEM] * len(outs),
        scratch_shapes=[pltpu.VMEM((n, 8, columns), jnp.float32)],
        **project_options(att, weight),
    )(att, half, weight)


def sum_kernel(own_ref, *refs):
    *part_refs, out_ref, held, sems = refs
    copies = []
    for j in range(own_ref.shape[0]):
        total = own_ref[j]
        for ref in part_refs:
            total = total + ref[j].astype(jnp.float32)
        held[j] = total.astype(jnp.bfloat16)
        copy = pltpu.make_async_copy(held.at[j], out_ref.at[j], sems.at[j])
        copy.start()
        copies.append(copy)
    for copy in copies:
        copy.wait()


def sum_parts(own, parts):
    return pl.pallas_call(
        sum_kernel,
        out_shape=jax.ShapeDtypeStruct(own.shape, jnp.bfloat16),
        in_specs=[VMEM] * (1 + len(parts)),
        out_specs=HBM,
        scratch_shapes=[
            pltpu.VMEM(own.shape, jnp.bfloat16),
            pltpu.SemaphoreType.DMA((own.shape[0],)),
        ],
        compiler_params=pltpu.CompilerParams(vmem_limit_bytes=VMEM_LIMIT),
        cost_estimate=pl.CostEstimate(
            flops=own.size * len(parts), bytes_accessed=own.size * 8, transcendentals=0
        ),
    )(own, *parts)


def head_plan(n_head):
    if n_head == 4:
        return [
            (((1, 0), (1, 1), (0, 0), (1, 3)), ((1, 2), (0, 1), (0, 2), (0, 3))),
            (((0, 1), (0, 2), (0, 3), (0, 0)), ((1, 1), (1, 3), (1, 0), (1, 2))),
            (((0, 3), (0, 0), (0, 1), (0, 2)), ((1, 3), (1, 2), (1, 1), (1, 0))),
            (((0, 2), (0, 3), (1, 2), (0, 1)), ((0, 0), (1, 0), (1, 3), (1, 1))),
        ]
    return [
        tuple(tuple((core, (z + t) % n_head) for z in range(n_head)) for core in range(2))
        for t in range(1, n_head)
    ]


def plan_targets(plan):
    seen = set()
    targets = []
    for permutation in plan:
        rows = []
        for core, row in enumerate(permutation):
            rows.append([])
            for z, (to_core, t) in enumerate(row):
                useful = to_core == core and (core, z, t) not in seen
                rows[core].append(t if useful else -1)
                if useful:
                    seen.add((core, z, t))
        targets.append(rows)
    return targets


def send_by(permutation, x):
    n, n_head = lax.axis_size("ctx"), lax.axis_size("head")
    pairs = []
    for c in range(n):
        for z in range(n_head):
            core, t = permutation[c % 2][z]
            pairs.append((c * n_head + z, (c - c % 2 + core) * n_head + t))
    return lax.ppermute(x, ("ctx", "head"), pairs)


def swap(x, axis, r):
    size = lax.axis_size(axis)
    return lax.ppermute(x, axis, [(i, i ^ r) for i in range(size)])


def swap_chips(x, n):
    return [swap(x, "ctx", r) for r in range(2, n, 2)]


def swap_other_cores(x, n):
    return [swap(x, "ctx", r) for r in range(1, n, 2)]


def local(queries, kv_cache, new_kv, selected, out_weight):
    steps, _, width = queries.shape
    heads = kv_cache.shape[4] // HD
    rows = steps * heads * GROUPS
    n = lax.axis_size("ctx")
    n_head = lax.axis_size("head")

    first_q = queries.reshape(1, steps, width)
    other_kv = swap(kv_cache, "ctx", 1)
    far_q = swap_chips(first_q, n)
    new_pairs = new_kv.reshape(steps, 2, heads * HD)
    own_q, own_kv, bits, new_pairs = own_side(first_q, kv_cache, selected, new_pairs)
    all_q = [own_q] + far_q
    sent = partials(bits, new_pairs, own_kv, other_kv, all_q, rows, heads)
    parts = swap_other_cores(sent, n)
    weight = load_weight(out_weight, sent)
    odd_att = last_merge(parts, weight, rows, steps)
    even_att = swap(odd_att, "ctx", 1)
    plan = head_plan(n_head)
    half = project_half(odd_att, weight)
    own_rows, *rows_out = project(
        even_att, half, weight, steps, n_head, plan_targets(plan)
    )
    got = [send_by(permutation, chunk) for chunk, permutation in zip(rows_out, plan)]
    return sum_parts(own_rows, got)


def solution(mesh):
    return jax.shard_map(
        local,
        mesh=mesh,
        in_specs=(
            P(None, "ctx", "head"),
            P(None, "ctx", None, None, "head"),
            P(None, "ctx", None, "head"),
            P(None, None, "head", None),
            P("head", "ctx"),
        ),
        out_specs=P("head", None, "ctx"),
        check_vma=False,
    )
```

```python
import functools

import jax
import jax.numpy as jnp
from jax import lax
from jax.experimental import pallas as pl
from jax.experimental.pallas import tpu as pltpu
from jax.sharding import PartitionSpec as P

HQ = 64
KVH = 8
HD = 128
PAGE = 64
GROUPS = HQ // KVH
STAT_ROWS = 16
MASKED = -3e38
FLOOR = -1.5e38
WEIGHT_PIECES = 4
VMEM_LIMIT = 24 * 1024 * 1024

VMEM = pl.BlockSpec(memory_space=pltpu.VMEM)
ANY = pl.BlockSpec(memory_space=pl.ANY)
HBM = pl.BlockSpec(memory_space=pltpu.HBM)
NT = (((1,), (1,)), ((), ()))


def query_rows(q_ref, slot, turned):
    steps, width = q_ref.shape[1:]
    for j in range(width // HD):
        piece = q_ref[slot, :, j * HD : (j + 1) * HD]
        turned[j * steps : (j + 1) * steps, :] = piece.astype(jnp.float32)
    return turned[...].astype(jnp.bfloat16)


def spread_heads(query, heads):
    rows = query.shape[0]
    row_head = lax.broadcasted_iota(jnp.int32, (rows, heads * HD), 0) // (rows // heads)
    lane_head = lax.broadcasted_iota(jnp.int32, (rows, heads * HD), 1) // HD
    wide = jnp.concatenate([query] * heads, axis=1)
    return jnp.where(row_head == lane_head, wide, jnp.zeros_like(wide))


def own_heads(weighted, heads):
    span = weighted.shape[0] // heads
    return jnp.concatenate(
        [weighted[h * span : (h + 1) * span, h * HD : (h + 1) * HD] for h in range(heads)], axis=0
    )


def three_parts(x):
    high = x.astype(jnp.bfloat16).astype(jnp.float32)
    rest = x - high
    middle = rest.astype(jnp.bfloat16).astype(jnp.float32)
    return high, middle, rest - middle


def stat_rows(slots):
    return -(-3 * slots // STAT_ROWS) * STAT_ROWS


def stat_block(columns):
    rows = columns[0].shape[0]
    lane = lax.broadcasted_iota(jnp.int32, (rows, 128), 1)
    sheet = jnp.zeros((rows, 128), jnp.float32)
    for i, column in enumerate(columns):
        sheet = jnp.where(lane == i, column, sheet)
    sheet = jnp.concatenate([sheet, jnp.zeros((128 - rows, 128), jnp.float32)], axis=0)
    count = len(columns)
    parts = list(three_parts(jnp.transpose(sheet)[:count]))
    spare = stat_rows(count) - 3 * count
    if spare:
        parts.append(jnp.zeros((spare, 128), jnp.float32))
    return jnp.concatenate(parts, axis=0).astype(jnp.bfloat16)


def own_kernel(
    kv_in, selected_in, new_ref, kv_out, bits_out, new_out, selected_ref, sems
):
    steps, _, heads, _ = selected_ref.shape
    m, pages = kv_out.shape[:2]
    me = lax.axis_index("ctx")
    pairs = [(selected_in, selected_ref)]
    pairs += [(kv_in.at[me ^ (2 * i)], kv_out.at[i]) for i in range(m)]
    copies = [pltpu.make_async_copy(*pair, sems.at[i]) for i, pair in enumerate(pairs)]
    for copy in copies:
        copy.start()
    copies[0].wait()
    by_step = []
    for s in range(steps):
        lists = jnp.concatenate([selected_ref[s, me ^ (2 * i)] for i in range(m)], axis=0)
        for core in range(2):
            page = lists - (me ^ core) * pages
            here = (page >= 0) & (page < pages)
            bit = jnp.where(here, jnp.left_shift(1, page & 31), 0).astype(jnp.float32)
            total = jnp.sum(bit, axis=1, keepdims=True).astype(jnp.int32)
            by_step.append(jnp.broadcast_to(total, (m * heads, 128)))
    step_of = lax.broadcasted_iota(jnp.int32, (8, 128), 0) % steps
    for core in range(2):
        for i in range(m):
            for h in range(heads):
                row = i * heads + h
                bits = jnp.zeros((8, 128), jnp.int32)
                for s in range(steps):
                    bits = jnp.where(step_of == s, by_step[2 * s + core][row : row + 1], bits)
                bits_out[core, i, h] = bits
    for part in range(2):
        tokens = [new_ref[s, part : part + 1].astype(jnp.float32) for s in range(steps)]
        blank = jnp.zeros((16 - steps, new_ref.shape[2]), jnp.float32)
        new_out[part] = jnp.concatenate(tokens + [blank], axis=0).astype(jnp.bfloat16)
    for copy in copies[1:]:
        copy.wait()


def own_side(kv_cache, selected, new_kv):
    batch, heads = selected.shape[1:3]
    m = batch // 2
    operands = (kv_cache, selected)
    return pl.pallas_call(
        own_kernel,
        out_shape=[
            jax.ShapeDtypeStruct((m,) + kv_cache.shape[1:], kv_cache.dtype),
            jax.ShapeDtypeStruct((2, m, heads, 8, 128), jnp.int32),
            jax.ShapeDtypeStruct((2, 16, new_kv.shape[2]), jnp.bfloat16),
        ],
        in_specs=[HBM, HBM, VMEM],
        out_specs=[VMEM] * 3,
        scratch_shapes=[
            pltpu.VMEM(selected.shape, selected.dtype),
            pltpu.SemaphoreType.DMA((1 + m,)),
        ],
        compiler_params=pltpu.CompilerParams(vmem_limit_bytes=VMEM_LIMIT),
        cost_estimate=pl.CostEstimate(
            flops=2**20, bytes_accessed=kv_cache.size * 2, transcendentals=0
        ),
    )(*[pltpu.with_memory_space_constraint(x, pltpu.HBM) for x in operands], new_kv)


def page_masks(bits_ref, core, i, steps, page_bit):
    masks = []
    for h in range(bits_ref.shape[2]):
        bits = jnp.concatenate([bits_ref[core, i, h]] * (page_bit.shape[1] // 128), axis=1)
        masks += [(page_bit & bits) != 0] * steps
    return jnp.concatenate(masks, axis=0)


def attend(spread, pieces):
    found = []
    for keys, values, allowed in pieces:
        scores = lax.dot_general(spread, keys, NT, preferred_element_type=jnp.float32)
        found.append((jnp.where(allowed, scores * HD ** (-0.5), MASKED), values))

    def finish():
        tops = [jnp.max(scores, axis=1, keepdims=True) for scores, _ in found]
        top = jnp.maximum(functools.reduce(jnp.maximum, tops), FLOOR)
        total, weighted = 0.0, 0.0
        for scores, values in found:
            expo = jnp.exp(scores - top)
            total = total + jnp.sum(expo, axis=1, keepdims=True)
            weighted = weighted + jnp.dot(
                expo.astype(jnp.bfloat16), values, preferred_element_type=jnp.float32
            )
        return top, total, weighted

    return finish


def page_pieces(kv_ref, where, bits_ref, core, i, steps, heads):
    tokens = kv_ref.shape[1] * PAGE
    page_bit = jnp.left_shift(1, lax.broadcasted_iota(jnp.int32, (8, tokens), 1) // PAGE)
    keys = kv_ref[where, :, 0].reshape(tokens, heads * HD)
    values = kv_ref[where, :, 1].reshape(tokens, heads * HD)
    return keys, values, page_masks(bits_ref, core, i, steps, page_bit)


def staged(count, ahead, begin, end):
    begun = [begin(i) for i in range(min(ahead, count))]
    for i in range(count):
        if i + ahead < count:
            begun.append(begin(i + ahead))
        end(i, begun[i])


def first_kernel(heads, bits_ref, new_ref, own_ref, *refs):
    *q_refs, spread_ref, sum_ref, top_ref, total_ref, turned = refs
    steps = q_refs[0].shape[1]
    rows = turned.shape[1]

    def begin(i):
        spread = spread_heads(query_rows(q_refs[i], 0, turned.at[i]), heads)
        spread_ref[i] = spread
        pieces = [page_pieces(own_ref, i, bits_ref, 0, i, steps, heads)]
        if i == 0:
            step_of = lax.broadcasted_iota(jnp.int32, (rows, 16), 0) % steps
            causal = lax.broadcasted_iota(jnp.int32, (rows, 16), 1) <= step_of
            pieces.append((new_ref[0], new_ref[1], causal))
        return attend(spread, pieces)

    def end(i, finish):
        top, total, weighted = finish()
        top_ref[i] = jnp.broadcast_to(top, (rows, 128))
        total_ref[i] = jnp.broadcast_to(total, (rows, 128))
        sum_ref[i] = own_heads(weighted, heads)

    staged(len(q_refs), 1, begin, end)


def second_kernel(
    steps, heads, bits_ref, spread_ref, sum_ref, top_ref, total_ref, other_ref, out_ref
):
    m, rows = spread_ref.shape[:2]
    me = lax.axis_index("ctx")
    columns = []

    def begin(i):
        pieces = [page_pieces(other_ref, me ^ (2 * i), bits_ref, 1, i, steps, heads)]
        return attend(spread_ref[i], pieces)

    def end(i, finish):
        first_top, first_total = top_ref[i], total_ref[i]
        top, total, weighted = finish()
        top = jnp.broadcast_to(top, (rows, 128))
        both = jnp.maximum(top, first_top)
        factor, first_factor = jnp.exp(top - both), jnp.exp(first_top - both)
        total = jnp.broadcast_to(total, (rows, 128)) * factor + first_total * first_factor
        total = jnp.where(total > 0.0, total, 1.0)
        share = 1.0 / total
        joined = own_heads(weighted, heads) * (factor * share)
        joined = joined + sum_ref[i] * (first_factor * share)
        out_ref[i * rows : (i + 1) * rows, :] = joined.astype(jnp.bfloat16)
        columns.append(both + jnp.log(total))

    staged(m, m if m <= 4 else 2, begin, end)
    out_ref[m * rows :, :] = stat_block(columns)


def partials(bits, new_pairs, own_kv, other_kv, queries, rows, heads):
    m, pages = own_kv.shape[:2]
    tokens, width = pages * PAGE, own_kv.shape[4]
    steps = queries[0].shape[1]
    options = dict(
        compiler_params=pltpu.CompilerParams(vmem_limit_bytes=VMEM_LIMIT),
        cost_estimate=pl.CostEstimate(
            flops=4 * m * rows * tokens * width,
            bytes_accessed=2**20,
            transcendentals=m * rows * tokens,
        ),
    )
    state = pl.pallas_call(
        functools.partial(first_kernel, heads),
        out_shape=[
            jax.ShapeDtypeStruct((m, rows, width), jnp.bfloat16),
            jax.ShapeDtypeStruct((m, rows, HD), jnp.float32),
            jax.ShapeDtypeStruct((m, rows, 128), jnp.float32),
            jax.ShapeDtypeStruct((m, rows, 128), jnp.float32),
        ],
        in_specs=[VMEM] * (3 + m),
        out_specs=[VMEM] * 4,
        scratch_shapes=[pltpu.VMEM((m, rows, HD), jnp.float32)],
        **options,
    )(bits, new_pairs, own_kv, *queries)
    return pl.pallas_call(
        functools.partial(second_kernel, steps, heads),
        out_shape=jax.ShapeDtypeStruct((m * rows + stat_rows(m), HD), jnp.bfloat16),
        in_specs=[VMEM] * 6,
        out_specs=VMEM,
        **options,
    )(bits, *state, other_kv)


def last_merge_kernel(rows, steps, *refs):
    *part_refs, _, out_ref = refs
    m = len(part_refs)
    logs = []
    for j, ref in enumerate(part_refs):
        stats = ref[m * rows :, :].astype(jnp.float32)
        log = stats[:m] + stats[m : 2 * m] + stats[2 * m : 3 * m]
        if j:
            log = jnp.concatenate([log[i ^ j : (i ^ j) + 1] for i in range(m)], axis=0)
        logs.append(log)
    top = functools.reduce(jnp.maximum, logs)
    factors = [jnp.exp(log - top) for log in logs]
    share = 1.0 / functools.reduce(jnp.add, factors)
    lane = lax.broadcasted_iota(jnp.int32, (m, 128), 1) // rows
    beside = 128 // rows
    packed = []
    for first in range(0, m, beside):
        wide = jnp.zeros((m, 128), jnp.float32)
        for p in range(min(beside, m - first)):
            weight = factors[first + p] * share
            if p:
                weight = jnp.concatenate(
                    [weight[:, 128 - p * rows :], weight[:, : 128 - p * rows]], axis=1
                )
            wide = jnp.where(lane == p, weight, wide)
        packed.append(wide)
    on_row = lax.broadcasted_iota(jnp.int32, (rows, 128), 0)
    diagonal = lax.broadcasted_iota(jnp.int32, (rows, 128), 1) % rows == on_row
    joined = []
    for i in range(m):
        weights = jnp.concatenate(
            [jnp.where(diagonal, wide[i : i + 1], 0.0) for wide in packed], axis=1
        )
        parts = jnp.concatenate(
            [ref[(i ^ j) * rows : ((i ^ j) + 1) * rows, :] for j, ref in enumerate(part_refs)],
            axis=0,
        )
        high = weights.astype(jnp.bfloat16)
        low = (weights - high.astype(jnp.float32)).astype(jnp.bfloat16)
        both = jnp.concatenate([high, low], axis=0)
        product = jnp.dot(both, parts, preferred_element_type=jnp.float32)
        joined.append(product[:rows] + product[rows:])
    for j in range(rows // steps):
        piece = jnp.concatenate([x[j * steps : (j + 1) * steps] for x in joined], axis=0)
        out_ref[:, j * HD : (j + 1) * HD] = piece.astype(jnp.bfloat16)


def last_merge(parts, weight, rows, steps):
    m = len(parts)
    return pl.pallas_call(
        functools.partial(last_merge_kernel, rows, steps),
        out_shape=jax.ShapeDtypeStruct((m * steps, rows // steps * HD), jnp.bfloat16),
        in_specs=[VMEM] * m + [ANY],
        out_specs=VMEM,
        compiler_params=pltpu.CompilerParams(vmem_limit_bytes=VMEM_LIMIT),
        cost_estimate=pl.CostEstimate(
            flops=2 * m * m * rows * HD, bytes_accessed=2**18, transcendentals=0
        ),
    )(*parts, weight)


def load_kernel(weight_ref, _, out_ref, sems):
    piece = out_ref.shape[0] // WEIGHT_PIECES
    copies = []
    for i in range(WEIGHT_PIECES):
        span = pl.ds(i * piece, piece)
        copy = pltpu.make_async_copy(weight_ref.at[span], out_ref.at[span], sems.at[i])
        copy.start()
        copies.append(copy)
    for copy in copies:
        copy.wait()


def load_weight(out_weight, after):
    return pl.pallas_call(
        load_kernel,
        out_shape=jax.ShapeDtypeStruct(out_weight.shape, out_weight.dtype),
        in_specs=[HBM, ANY],
        out_specs=VMEM,
        scratch_shapes=[pltpu.SemaphoreType.DMA((WEIGHT_PIECES,))],
        compiler_params=pltpu.CompilerParams(vmem_limit_bytes=VMEM_LIMIT),
        cost_estimate=pl.CostEstimate(
            flops=0, bytes_accessed=out_weight.size * 4, transcendentals=0
        ),
    )(pltpu.with_memory_space_constraint(out_weight, pltpu.HBM), after)


def half_kernel(att_ref, weight_ref, out_ref):
    out_ref[...] = jnp.dot(att_ref[...], weight_ref[...], preferred_element_type=jnp.float32)


def project_kernel(n_head, targets, att_ref, half_ref, weight_ref, *refs):
    *out_refs, rows_all = refs
    seqs, steps, _ = out_refs[0].shape
    me = lax.axis_index("ctx")
    mine = lax.axis_index("head")
    product = jnp.dot(att_ref[...], weight_ref[...], preferred_element_type=jnp.float32)
    for i in range(rows_all.shape[0] // 2):
        rows_all[2 * i, :steps, :] = product[i * steps : (i + 1) * steps]
        rows_all[2 * i + 1, :steps, :] = half_ref[i * steps : (i + 1) * steps, :]
    for k, ref in enumerate(out_refs):
        target = mine
        if k > 0:
            for core, row in enumerate(targets[k - 1]):
                for z, t in enumerate(row):
                    target = jnp.where((me % 2 == core) & (mine == z), t, target)
        for j in range(seqs):
            found = rows_all[(jnp.maximum(target, 0) * seqs + j) ^ me, :steps]
            if k > 0 and any(t < 0 for row in targets[k - 1] for t in row):
                found = jnp.where(target < 0, 0.0, found)
            ref[j] = found.astype(ref.dtype)


def project_options(att, weight):
    width, columns = weight.shape
    return dict(
        compiler_params=pltpu.CompilerParams(vmem_limit_bytes=VMEM_LIMIT),
        cost_estimate=pl.CostEstimate(
            flops=2 * att.size * columns, bytes_accessed=width * columns * 2, transcendentals=0
        ),
    )


def project_half(att, weight):
    return pl.pallas_call(
        half_kernel,
        out_shape=jax.ShapeDtypeStruct((att.shape[0], weight.shape[1]), jnp.float32),
        in_specs=[VMEM] * 2,
        out_specs=VMEM,
        **project_options(att, weight),
    )(att, weight)


def project(att, half, weight, steps, n_head, targets):
    n = 2 * att.shape[0] // steps
    columns = weight.shape[1]
    outs = [
        jax.ShapeDtypeStruct((n // n_head, steps, columns), jnp.bfloat16 if k else jnp.float32)
        for k in range(1 + len(targets))
    ]
    return pl.pallas_call(
        functools.partial(project_kernel, n_head, targets),
        out_shape=outs,
        in_specs=[VMEM] * 3,
        out_specs=[VMEM] * len(outs),
        scratch_shapes=[pltpu.VMEM((n, 8, columns), jnp.float32)],
        **project_options(att, weight),
    )(att, half, weight)


def head_plan(n_head):
    if n_head == 4:
        return [
            (((1, 0), (1, 1), (0, 0), (1, 3)), ((1, 2), (0, 1), (0, 2), (0, 3))),
            (((0, 1), (0, 2), (0, 3), (0, 0)), ((1, 1), (1, 3), (1, 0), (1, 2))),
            (((0, 3), (0, 0), (0, 1), (0, 2)), ((1, 3), (1, 2), (1, 1), (1, 0))),
            (((0, 2), (0, 3), (1, 2), (0, 1)), ((0, 0), (1, 0), (1, 3), (1, 1))),
        ]
    return [
        tuple(tuple((core, (z + t) % n_head) for z in range(n_head)) for core in range(2))
        for t in range(1, n_head)
    ]


def plan_targets(plan):
    seen = set()
    targets = []
    for permutation in plan:
        rows = []
        for core, row in enumerate(permutation):
            rows.append([])
            for z, (to_core, t) in enumerate(row):
                useful = to_core == core and (core, z, t) not in seen
                rows[core].append(t if useful else -1)
                if useful:
                    seen.add((core, z, t))
        targets.append(rows)
    return targets


def send_by(permutation, x):
    n, n_head = lax.axis_size("ctx"), lax.axis_size("head")
    pairs = []
    for c in range(n):
        for z in range(n_head):
            core, t = permutation[c % 2][z]
            pairs.append((c * n_head + z, (c - c % 2 + core) * n_head + t))
    return lax.ppermute(x, ("ctx", "head"), pairs)


def swap(x, axis, r):
    size = lax.axis_size(axis)
    return lax.ppermute(x, axis, [(i, i ^ r) for i in range(size)])


def swap_chips(x, n):
    return [swap(x, "ctx", r) for r in range(2, n, 2)]


def swap_other_cores(x, n):
    return [swap(x, "ctx", r) for r in range(1, n, 2)]


def local(queries, kv_cache, new_kv, selected, out_weight):
    steps, _, width = queries.shape
    heads = kv_cache.shape[4] // HD
    rows = steps * heads * GROUPS
    n = lax.axis_size("ctx")
    n_head = lax.axis_size("head")

    first_q = queries.reshape(1, steps, width)
    other_kv = swap(kv_cache, "ctx", 1)
    far_q = swap_chips(first_q, n)
    new_pairs = new_kv.reshape(steps, 2, heads * HD)
    own_kv, bits, new_pairs = own_side(kv_cache, selected, new_pairs)
    all_q = [first_q] + far_q
    sent = partials(bits, new_pairs, own_kv, other_kv, all_q, rows, heads)
    parts = swap_other_cores(sent, n)
    weight = load_weight(out_weight, sent)
    odd_att = last_merge(parts, weight, rows, steps)
    even_att = swap(odd_att, "ctx", 1)
    plan = head_plan(n_head)
    half = project_half(odd_att, weight)
    total, *rows_out = project(
        even_att, half, weight, steps, n_head, plan_targets(plan)
    )
    for chunk, permutation in zip(rows_out, plan):
        total = total + send_by(permutation, chunk).astype(jnp.float32)
    return total.astype(jnp.bfloat16)


def solution(mesh):
    return jax.shard_map(
        local,
        mesh=mesh,
        in_specs=(
            P(None, "ctx", "head"),
            P(None, "ctx", None, None, "head"),
            P(None, "ctx", None, "head"),
            P(None, None, "head", None),
            P("head", "ctx"),
        ),
        out_specs=P("head", None, "ctx"),
        check_vma=False,
    )
```

```python
import functools

import jax
import jax.numpy as jnp
from jax import lax
from jax.experimental import pallas as pl
from jax.experimental.pallas import tpu as pltpu
from jax.sharding import PartitionSpec as P

HQ = 64
KVH = 8
HD = 128
PAGE = 64
GROUPS = HQ // KVH
STAT_ROWS = 16
MASKED = -3e38
FLOOR = -1.5e38
WEIGHT_PIECES = 4
VMEM_LIMIT = 24 * 1024 * 1024

VMEM = pl.BlockSpec(memory_space=pltpu.VMEM)
ANY = pl.BlockSpec(memory_space=pl.ANY)
HBM = pl.BlockSpec(memory_space=pltpu.HBM)
NT = (((1,), (1,)), ((), ()))


def query_rows(q_ref, slot, turned):
    steps, width = q_ref.shape[1:]
    for j in range(width // HD):
        piece = q_ref[slot, :, j * HD : (j + 1) * HD]
        turned[j * steps : (j + 1) * steps, :] = piece.astype(jnp.float32)
    return turned[...].astype(jnp.bfloat16)


def spread_heads(query, heads):
    rows = query.shape[0]
    row_head = lax.broadcasted_iota(jnp.int32, (rows, heads * HD), 0) // (rows // heads)
    lane_head = lax.broadcasted_iota(jnp.int32, (rows, heads * HD), 1) // HD
    wide = jnp.concatenate([query] * heads, axis=1)
    return jnp.where(row_head == lane_head, wide, jnp.zeros_like(wide))


def own_heads(weighted, heads):
    span = weighted.shape[0] // heads
    return jnp.concatenate(
        [weighted[h * span : (h + 1) * span, h * HD : (h + 1) * HD] for h in range(heads)], axis=0
    )


def three_parts(x):
    high = x.astype(jnp.bfloat16).astype(jnp.float32)
    rest = x - high
    middle = rest.astype(jnp.bfloat16).astype(jnp.float32)
    return high, middle, rest - middle


def stat_rows(slots):
    return -(-3 * slots // STAT_ROWS) * STAT_ROWS


def stat_block(columns):
    rows = columns[0].shape[0]
    lane = lax.broadcasted_iota(jnp.int32, (rows, 128), 1)
    sheet = jnp.zeros((rows, 128), jnp.float32)
    for i, column in enumerate(columns):
        sheet = jnp.where(lane == i, column, sheet)
    sheet = jnp.concatenate([sheet, jnp.zeros((128 - rows, 128), jnp.float32)], axis=0)
    count = len(columns)
    parts = list(three_parts(jnp.transpose(sheet)[:count]))
    spare = stat_rows(count) - 3 * count
    if spare:
        parts.append(jnp.zeros((spare, 128), jnp.float32))
    return jnp.concatenate(parts, axis=0).astype(jnp.bfloat16)


def own_kernel(
    kv_in, selected_in, new_ref, kv_out, bits_out, new_out, selected_ref, sems
):
    steps, _, heads, _ = selected_ref.shape
    m, pages = kv_out.shape[:2]
    me = lax.axis_index("ctx")
    pairs = [(selected_in, selected_ref)]
    pairs += [(kv_in.at[me ^ (2 * i)], kv_out.at[i]) for i in range(m)]
    copies = [pltpu.make_async_copy(*pair, sems.at[i]) for i, pair in enumerate(pairs)]
    for copy in copies:
        copy.start()
    copies[0].wait()
    by_step = []
    for s in range(steps):
        lists = jnp.concatenate([selected_ref[s, me ^ (2 * i)] for i in range(m)], axis=0)
        for core in range(2):
            page = lists - (me ^ core) * pages
            here = (page >= 0) & (page < pages)
            bit = jnp.where(here, jnp.left_shift(1, page & 31), 0).astype(jnp.float32)
            total = jnp.sum(bit, axis=1, keepdims=True).astype(jnp.int32)
            by_step.append(jnp.broadcast_to(total, (m * heads, 128)))
    step_of = lax.broadcasted_iota(jnp.int32, (8, 128), 0) % steps
    for core in range(2):
        for i in range(m):
            for h in range(heads):
                row = i * heads + h
                bits = jnp.zeros((8, 128), jnp.int32)
                for s in range(steps):
                    bits = jnp.where(step_of == s, by_step[2 * s + core][row : row + 1], bits)
                bits_out[core, i, h] = bits
    for part in range(2):
        tokens = [new_ref[s].astype(jnp.float32)[part : part + 1] for s in range(steps)]
        blank = jnp.zeros((16 - steps, new_ref.shape[2]), jnp.float32)
        new_out[part] = jnp.concatenate(tokens + [blank], axis=0).astype(jnp.bfloat16)
    for copy in copies[1:]:
        copy.wait()


def own_side(kv_cache, selected, new_kv):
    batch, heads = selected.shape[1:3]
    m = batch // 2
    operands = (kv_cache, selected)
    return pl.pallas_call(
        own_kernel,
        out_shape=[
            jax.ShapeDtypeStruct((m,) + kv_cache.shape[1:], kv_cache.dtype),
            jax.ShapeDtypeStruct((2, m, heads, 8, 128), jnp.int32),
            jax.ShapeDtypeStruct((2, 16, new_kv.shape[2]), jnp.bfloat16),
        ],
        in_specs=[HBM, HBM, VMEM],
        out_specs=[VMEM] * 3,
        scratch_shapes=[
            pltpu.VMEM(selected.shape, selected.dtype),
            pltpu.SemaphoreType.DMA((1 + m,)),
        ],
        compiler_params=pltpu.CompilerParams(vmem_limit_bytes=VMEM_LIMIT),
        cost_estimate=pl.CostEstimate(
            flops=2**20, bytes_accessed=kv_cache.size * 2, transcendentals=0
        ),
    )(*[pltpu.with_memory_space_constraint(x, pltpu.HBM) for x in operands], new_kv)


def page_masks(bits_ref, core, i, steps, page_bit):
    masks = []
    for h in range(bits_ref.shape[2]):
        bits = jnp.concatenate([bits_ref[core, i, h]] * (page_bit.shape[1] // 128), axis=1)
        masks += [(page_bit & bits) != 0] * steps
    return jnp.concatenate(masks, axis=0)


def attend(spread, pieces):
    found = []
    for keys, values, allowed in pieces:
        scores = lax.dot_general(spread, keys, NT, preferred_element_type=jnp.float32)
        found.append((jnp.where(allowed, scores * HD ** (-0.5), MASKED), values))

    def finish():
        tops = [jnp.max(scores, axis=1, keepdims=True) for scores, _ in found]
        top = jnp.maximum(functools.reduce(jnp.maximum, tops), FLOOR)
        total, weighted = 0.0, 0.0
        for scores, values in found:
            expo = jnp.exp(scores - top)
            total = total + jnp.sum(expo, axis=1, keepdims=True)
            weighted = weighted + jnp.dot(
                expo.astype(jnp.bfloat16), values, preferred_element_type=jnp.float32
            )
        return top, total, weighted

    return finish


def page_pieces(kv_ref, where, bits_ref, core, i, steps, heads):
    tokens = kv_ref.shape[1] * PAGE
    page_bit = jnp.left_shift(1, lax.broadcasted_iota(jnp.int32, (8, tokens), 1) // PAGE)
    keys = kv_ref[where, :, 0].reshape(tokens, heads * HD)
    values = kv_ref[where, :, 1].reshape(tokens, heads * HD)
    return keys, values, page_masks(bits_ref, core, i, steps, page_bit)


def staged(count, ahead, begin, end):
    begun = [begin(i) for i in range(min(ahead, count))]
    for i in range(count):
        if i + ahead < count:
            begun.append(begin(i + ahead))
        end(i, begun[i])


def first_kernel(heads, bits_ref, new_ref, own_ref, *refs):
    *q_refs, spread_ref, sum_ref, top_ref, total_ref, turned = refs
    steps = q_refs[0].shape[1]
    rows = turned.shape[1]

    def begin(i):
        spread = spread_heads(query_rows(q_refs[i], 0, turned.at[i]), heads)
        spread_ref[i] = spread
        pieces = [page_pieces(own_ref, i, bits_ref, 0, i, steps, heads)]
        if i == 0:
            step_of = lax.broadcasted_iota(jnp.int32, (rows, 16), 0) % steps
            causal = lax.broadcasted_iota(jnp.int32, (rows, 16), 1) <= step_of
            pieces.append((new_ref[0], new_ref[1], causal))
        return attend(spread, pieces)

    def end(i, finish):
        top, total, weighted = finish()
        top_ref[i] = jnp.broadcast_to(top, (rows, 128))
        total_ref[i] = jnp.broadcast_to(total, (rows, 128))
        sum_ref[i] = own_heads(weighted, heads)

    staged(len(q_refs), 1, begin, end)


def second_kernel(
    steps, heads, bits_ref, spread_ref, sum_ref, top_ref, total_ref, other_ref, out_ref
):
    m, rows = spread_ref.shape[:2]
    me = lax.axis_index("ctx")
    columns = []

    def begin(i):
        pieces = [page_pieces(other_ref, me ^ (2 * i), bits_ref, 1, i, steps, heads)]
        return attend(spread_ref[i], pieces)

    def end(i, finish):
        first_top, first_total = top_ref[i], total_ref[i]
        top, total, weighted = finish()
        top = jnp.broadcast_to(top, (rows, 128))
        both = jnp.maximum(top, first_top)
        factor, first_factor = jnp.exp(top - both), jnp.exp(first_top - both)
        total = jnp.broadcast_to(total, (rows, 128)) * factor + first_total * first_factor
        total = jnp.where(total > 0.0, total, 1.0)
        share = 1.0 / total
        joined = own_heads(weighted, heads) * (factor * share)
        joined = joined + sum_ref[i] * (first_factor * share)
        out_ref[i * rows : (i + 1) * rows, :] = joined.astype(jnp.bfloat16)
        columns.append(both + jnp.log(total))

    staged(m, m if m <= 4 else 2, begin, end)
    out_ref[m * rows :, :] = stat_block(columns)


def partials(bits, new_pairs, own_kv, other_kv, queries, rows, heads):
    m, pages = own_kv.shape[:2]
    tokens, width = pages * PAGE, own_kv.shape[4]
    steps = queries[0].shape[1]
    options = dict(
        compiler_params=pltpu.CompilerParams(vmem_limit_bytes=VMEM_LIMIT),
        cost_estimate=pl.CostEstimate(
            flops=4 * m * rows * tokens * width,
            bytes_accessed=2**20,
            transcendentals=m * rows * tokens,
        ),
    )
    state = pl.pallas_call(
        functools.partial(first_kernel, heads),
        out_shape=[
            jax.ShapeDtypeStruct((m, rows, width), jnp.bfloat16),
            jax.ShapeDtypeStruct((m, rows, HD), jnp.float32),
            jax.ShapeDtypeStruct((m, rows, 128), jnp.float32),
            jax.ShapeDtypeStruct((m, rows, 128), jnp.float32),
        ],
        in_specs=[VMEM] * (3 + m),
        out_specs=[VMEM] * 4,
        scratch_shapes=[pltpu.VMEM((m, rows, HD), jnp.float32)],
        **options,
    )(bits, new_pairs, own_kv, *queries)
    return pl.pallas_call(
        functools.partial(second_kernel, steps, heads),
        out_shape=jax.ShapeDtypeStruct((m * rows + stat_rows(m), HD), jnp.bfloat16),
        in_specs=[VMEM] * 6,
        out_specs=VMEM,
        **options,
    )(bits, *state, other_kv)


def last_merge_kernel(rows, steps, *refs):
    *part_refs, _, out_ref = refs
    m = len(part_refs)
    logs = []
    for j, ref in enumerate(part_refs):
        stats = ref[m * rows :, :].astype(jnp.float32)
        log = stats[:m] + stats[m : 2 * m] + stats[2 * m : 3 * m]
        if j:
            log = jnp.concatenate([log[i ^ j : (i ^ j) + 1] for i in range(m)], axis=0)
        logs.append(log)
    top = functools.reduce(jnp.maximum, logs)
    factors = [jnp.exp(log - top) for log in logs]
    share = 1.0 / functools.reduce(jnp.add, factors)
    lane = lax.broadcasted_iota(jnp.int32, (m, 128), 1) // rows
    beside = 128 // rows
    packed = []
    for first in range(0, m, beside):
        wide = jnp.zeros((m, 128), jnp.float32)
        for p in range(min(beside, m - first)):
            weight = factors[first + p] * share
            if p:
                weight = jnp.concatenate(
                    [weight[:, 128 - p * rows :], weight[:, : 128 - p * rows]], axis=1
                )
            wide = jnp.where(lane == p, weight, wide)
        packed.append(wide)
    on_row = lax.broadcasted_iota(jnp.int32, (rows, 128), 0)
    diagonal = lax.broadcasted_iota(jnp.int32, (rows, 128), 1) % rows == on_row
    joined = []
    for i in range(m):
        weights = jnp.concatenate(
            [jnp.where(diagonal, wide[i : i + 1], 0.0) for wide in packed], axis=1
        )
        parts = jnp.concatenate(
            [ref[(i ^ j) * rows : ((i ^ j) + 1) * rows, :] for j, ref in enumerate(part_refs)],
            axis=0,
        )
        high = weights.astype(jnp.bfloat16)
        low = (weights - high.astype(jnp.float32)).astype(jnp.bfloat16)
        both = jnp.concatenate([high, low], axis=0)
        product = jnp.dot(both, parts, preferred_element_type=jnp.float32)
        joined.append(product[:rows] + product[rows:])
    for j in range(rows // steps):
        piece = jnp.concatenate([x[j * steps : (j + 1) * steps] for x in joined], axis=0)
        out_ref[:, j * HD : (j + 1) * HD] = piece.astype(jnp.bfloat16)


def last_merge(parts, weight, rows, steps):
    m = len(parts)
    return pl.pallas_call(
        functools.partial(last_merge_kernel, rows, steps),
        out_shape=jax.ShapeDtypeStruct((m * steps, rows // steps * HD), jnp.bfloat16),
        in_specs=[VMEM] * m + [ANY],
        out_specs=VMEM,
        compiler_params=pltpu.CompilerParams(vmem_limit_bytes=VMEM_LIMIT),
        cost_estimate=pl.CostEstimate(
            flops=2 * m * m * rows * HD, bytes_accessed=2**18, transcendentals=0
        ),
    )(*parts, weight)


def load_kernel(weight_ref, _, out_ref, sems):
    piece = out_ref.shape[0] // WEIGHT_PIECES
    copies = []
    for i in range(WEIGHT_PIECES):
        span = pl.ds(i * piece, piece)
        copy = pltpu.make_async_copy(weight_ref.at[span], out_ref.at[span], sems.at[i])
        copy.start()
        copies.append(copy)
    for copy in copies:
        copy.wait()


def load_weight(out_weight, after):
    return pl.pallas_call(
        load_kernel,
        out_shape=jax.ShapeDtypeStruct(out_weight.shape, out_weight.dtype),
        in_specs=[HBM, ANY],
        out_specs=VMEM,
        scratch_shapes=[pltpu.SemaphoreType.DMA((WEIGHT_PIECES,))],
        compiler_params=pltpu.CompilerParams(vmem_limit_bytes=VMEM_LIMIT),
        cost_estimate=pl.CostEstimate(
            flops=0, bytes_accessed=out_weight.size * 4, transcendentals=0
        ),
    )(pltpu.with_memory_space_constraint(out_weight, pltpu.HBM), after)


def half_kernel(att_ref, weight_ref, out_ref):
    out_ref[...] = jnp.dot(att_ref[...], weight_ref[...], preferred_element_type=jnp.float32)


def project_kernel(n_head, targets, att_ref, half_ref, weight_ref, *refs):
    *out_refs, rows_all = refs
    seqs, steps, _ = out_refs[0].shape
    me = lax.axis_index("ctx")
    mine = lax.axis_index("head")
    product = jnp.dot(att_ref[...], weight_ref[...], preferred_element_type=jnp.float32)
    for i in range(rows_all.shape[0] // 2):
        rows_all[2 * i, :steps, :] = product[i * steps : (i + 1) * steps]
        rows_all[2 * i + 1, :steps, :] = half_ref[i * steps : (i + 1) * steps, :]
    for k, ref in enumerate(out_refs):
        target = mine
        if k > 0:
            for core, row in enumerate(targets[k - 1]):
                for z, t in enumerate(row):
                    target = jnp.where((me % 2 == core) & (mine == z), t, target)
        for j in range(seqs):
            found = rows_all[(jnp.maximum(target, 0) * seqs + j) ^ me, :steps]
            if k > 0 and any(t < 0 for row in targets[k - 1] for t in row):
                found = jnp.where(target < 0, 0.0, found)
            ref[j] = found.astype(ref.dtype)


def project_options(att, weight):
    width, columns = weight.shape
    return dict(
        compiler_params=pltpu.CompilerParams(vmem_limit_bytes=VMEM_LIMIT),
        cost_estimate=pl.CostEstimate(
            flops=2 * att.size * columns, bytes_accessed=width * columns * 2, transcendentals=0
        ),
    )


def project_half(att, weight):
    return pl.pallas_call(
        half_kernel,
        out_shape=jax.ShapeDtypeStruct((att.shape[0], weight.shape[1]), jnp.float32),
        in_specs=[VMEM] * 2,
        out_specs=VMEM,
        **project_options(att, weight),
    )(att, weight)


def project(att, half, weight, steps, n_head, targets):
    n = 2 * att.shape[0] // steps
    columns = weight.shape[1]
    outs = [
        jax.ShapeDtypeStruct((n // n_head, steps, columns), jnp.bfloat16 if k else jnp.float32)
        for k in range(1 + len(targets))
    ]
    return pl.pallas_call(
        functools.partial(project_kernel, n_head, targets),
        out_shape=outs,
        in_specs=[VMEM] * 3,
        out_specs=[VMEM] * len(outs),
        scratch_shapes=[pltpu.VMEM((n, 8, columns), jnp.float32)],
        **project_options(att, weight),
    )(att, half, weight)


def head_plan(n_head):
    if n_head == 4:
        return [
            (((1, 0), (1, 1), (0, 0), (1, 3)), ((1, 2), (0, 1), (0, 2), (0, 3))),
            (((0, 1), (0, 2), (0, 3), (0, 0)), ((1, 1), (1, 3), (1, 0), (1, 2))),
            (((0, 3), (0, 0), (0, 1), (0, 2)), ((1, 3), (1, 2), (1, 1), (1, 0))),
            (((0, 2), (0, 3), (1, 2), (0, 1)), ((0, 0), (1, 0), (1, 3), (1, 1))),
        ]
    return [
        tuple(tuple((core, (z + t) % n_head) for z in range(n_head)) for core in range(2))
        for t in range(1, n_head)
    ]


def plan_targets(plan):
    seen = set()
    targets = []
    for permutation in plan:
        rows = []
        for core, row in enumerate(permutation):
            rows.append([])
            for z, (to_core, t) in enumerate(row):
                useful = to_core == core and (core, z, t) not in seen
                rows[core].append(t if useful else -1)
                if useful:
                    seen.add((core, z, t))
        targets.append(rows)
    return targets


def send_by(permutation, x):
    n, n_head = lax.axis_size("ctx"), lax.axis_size("head")
    pairs = []
    for c in range(n):
        for z in range(n_head):
            core, t = permutation[c % 2][z]
            pairs.append((c * n_head + z, (c - c % 2 + core) * n_head + t))
    return lax.ppermute(x, ("ctx", "head"), pairs)


def swap(x, axis, r):
    size = lax.axis_size(axis)
    return lax.ppermute(x, axis, [(i, i ^ r) for i in range(size)])


def swap_chips(x, n):
    return [swap(x, "ctx", r) for r in range(2, n, 2)]


def swap_other_cores(x, n):
    return [swap(x, "ctx", r) for r in range(1, n, 2)]


def local(queries, kv_cache, new_kv, selected, out_weight):
    steps, _, width = queries.shape
    heads = kv_cache.shape[4] // HD
    rows = steps * heads * GROUPS
    n = lax.axis_size("ctx")
    n_head = lax.axis_size("head")

    first_q = queries.reshape(1, steps, width)
    other_kv = swap(kv_cache, "ctx", 1)
    far_q = swap_chips(first_q, n)
    new_pairs = new_kv.reshape(steps, 2, heads * HD)
    own_kv, bits, new_pairs = own_side(kv_cache, selected, new_pairs)
    all_q = [first_q] + far_q
    sent = partials(bits, new_pairs, own_kv, other_kv, all_q, rows, heads)
    parts = swap_other_cores(sent, n)
    weight = load_weight(out_weight, sent)
    odd_att = last_merge(parts, weight, rows, steps)
    even_att = swap(odd_att, "ctx", 1)
    plan = head_plan(n_head)
    half = project_half(odd_att, weight)
    total, *rows_out = project(
        even_att, half, weight, steps, n_head, plan_targets(plan)
    )
    for chunk, permutation in zip(rows_out, plan):
        total = total + send_by(permutation, chunk).astype(jnp.float32)
    return total.astype(jnp.bfloat16)


def solution(mesh):
    return jax.shard_map(
        local,
        mesh=mesh,
        in_specs=(
            P(None, "ctx", "head"),
            P(None, "ctx", None, None, "head"),
            P(None, "ctx", None, "head"),
            P(None, None, "head", None),
            P("head", "ctx"),
        ),
        out_specs=P("head", None, "ctx"),
        check_vma=False,
    )
```

```python
import functools

import jax
import jax.numpy as jnp
from jax import lax
from jax.experimental import pallas as pl
from jax.experimental.pallas import tpu as pltpu
from jax.sharding import PartitionSpec as P

HQ = 64
KVH = 8
HD = 128
PAGE = 64
GROUPS = HQ // KVH
STAT_ROWS = 16
MASKED = -3e38
FLOOR = -1.5e38
WEIGHT_PIECES = 4
VMEM_LIMIT = 24 * 1024 * 1024

VMEM = pl.BlockSpec(memory_space=pltpu.VMEM)
ANY = pl.BlockSpec(memory_space=pl.ANY)
HBM = pl.BlockSpec(memory_space=pltpu.HBM)
NT = (((1,), (1,)), ((), ()))


def query_rows(q_ref, slot, turned):
    steps, width = q_ref.shape[1:]
    for j in range(width // HD):
        piece = q_ref[slot, :, j * HD : (j + 1) * HD]
        turned[j * steps : (j + 1) * steps, :] = piece.astype(jnp.float32)
    return turned[...].astype(jnp.bfloat16)


def spread_heads(query, heads):
    rows = query.shape[0]
    row_head = lax.broadcasted_iota(jnp.int32, (rows, heads * HD), 0) // (rows // heads)
    lane_head = lax.broadcasted_iota(jnp.int32, (rows, heads * HD), 1) // HD
    wide = jnp.concatenate([query] * heads, axis=1)
    return jnp.where(row_head == lane_head, wide, jnp.zeros_like(wide))


def own_heads(weighted, heads):
    span = weighted.shape[0] // heads
    return jnp.concatenate(
        [weighted[h * span : (h + 1) * span, h * HD : (h + 1) * HD] for h in range(heads)], axis=0
    )


def three_parts(x):
    high = x.astype(jnp.bfloat16).astype(jnp.float32)
    rest = x - high
    middle = rest.astype(jnp.bfloat16).astype(jnp.float32)
    return high, middle, rest - middle


def stat_rows(slots):
    return -(-3 * slots // STAT_ROWS) * STAT_ROWS


def stat_block(columns):
    rows = columns[0].shape[0]
    lane = lax.broadcasted_iota(jnp.int32, (rows, 128), 1)
    sheet = jnp.zeros((rows, 128), jnp.float32)
    for i, column in enumerate(columns):
        sheet = jnp.where(lane == i, column, sheet)
    sheet = jnp.concatenate([sheet, jnp.zeros((128 - rows, 128), jnp.float32)], axis=0)
    count = len(columns)
    parts = list(three_parts(jnp.transpose(sheet)[:count]))
    spare = stat_rows(count) - 3 * count
    if spare:
        parts.append(jnp.zeros((spare, 128), jnp.float32))
    return jnp.concatenate(parts, axis=0).astype(jnp.bfloat16)


def own_kernel(
    kv_in, selected_in, new_ref, kv_out, bits_out, new_out, selected_ref, sems
):
    steps, _, heads, _ = selected_ref.shape
    m, pages = kv_out.shape[:2]
    me = lax.axis_index("ctx")
    pairs = [(selected_in, selected_ref)]
    pairs += [(kv_in.at[me ^ (2 * i)], kv_out.at[i]) for i in range(m)]
    copies = [pltpu.make_async_copy(*pair, sems.at[i]) for i, pair in enumerate(pairs)]
    for copy in copies:
        copy.start()
    copies[0].wait()
    by_step = []
    for s in range(steps):
        lists = jnp.concatenate([selected_ref[s, me ^ (2 * i)] for i in range(m)], axis=0)
        for core in range(2):
            page = lists - (me ^ core) * pages
            here = (page >= 0) & (page < pages)
            bit = jnp.where(here, jnp.left_shift(1, page & 31), 0).astype(jnp.float32)
            total = jnp.sum(bit, axis=1, keepdims=True).astype(jnp.int32)
            by_step.append(jnp.broadcast_to(total, (m * heads, 128)))
    step_of = lax.broadcasted_iota(jnp.int32, (8, 128), 0) % steps
    for core in range(2):
        for i in range(m):
            for h in range(heads):
                row = i * heads + h
                bits = jnp.zeros((8, 128), jnp.int32)
                for s in range(steps):
                    bits = jnp.where(step_of == s, by_step[2 * s + core][row : row + 1], bits)
                bits_out[core, i, h] = bits
    for part in range(2):
        tokens = [new_ref[s].astype(jnp.float32)[part : part + 1] for s in range(steps)]
        blank = jnp.zeros((16 - steps, new_ref.shape[2]), jnp.float32)
        new_out[part] = jnp.concatenate(tokens + [blank], axis=0).astype(jnp.bfloat16)
    for copy in copies[1:]:
        copy.wait()


def own_side(kv_cache, selected, new_kv):
    batch, heads = selected.shape[1:3]
    m = batch // 2
    operands = (kv_cache, selected)
    return pl.pallas_call(
        own_kernel,
        out_shape=[
            jax.ShapeDtypeStruct((m,) + kv_cache.shape[1:], kv_cache.dtype),
            jax.ShapeDtypeStruct((2, m, heads, 8, 128), jnp.int32),
            jax.ShapeDtypeStruct((2, 16, new_kv.shape[2]), jnp.bfloat16),
        ],
        in_specs=[HBM, HBM, VMEM],
        out_specs=[VMEM] * 3,
        scratch_shapes=[
            pltpu.VMEM(selected.shape, selected.dtype),
            pltpu.SemaphoreType.DMA((1 + m,)),
        ],
        compiler_params=pltpu.CompilerParams(vmem_limit_bytes=VMEM_LIMIT),
        cost_estimate=pl.CostEstimate(
            flops=2**20, bytes_accessed=kv_cache.size * 2, transcendentals=0
        ),
    )(*[pltpu.with_memory_space_constraint(x, pltpu.HBM) for x in operands], new_kv)


def page_masks(bits_ref, core, i, steps, page_bit):
    masks = []
    for h in range(bits_ref.shape[2]):
        bits = jnp.concatenate([bits_ref[core, i, h]] * (page_bit.shape[1] // 128), axis=1)
        masks += [(page_bit & bits) != 0] * steps
    return jnp.concatenate(masks, axis=0)


def attend(spread, pieces):
    found = []
    for keys, values, allowed in pieces:
        scores = lax.dot_general(spread, keys, NT, preferred_element_type=jnp.float32)
        found.append((jnp.where(allowed, scores * HD ** (-0.5), MASKED), values))

    def finish():
        tops = [jnp.max(scores, axis=1, keepdims=True) for scores, _ in found]
        top = jnp.maximum(functools.reduce(jnp.maximum, tops), FLOOR)
        total, weighted = 0.0, 0.0
        for scores, values in found:
            expo = jnp.exp(scores - top)
            total = total + jnp.sum(expo, axis=1, keepdims=True)
            weighted = weighted + jnp.dot(
                expo.astype(jnp.bfloat16), values, preferred_element_type=jnp.float32
            )
        return top, total, weighted

    return finish


def page_pieces(kv_ref, where, bits_ref, core, i, steps, heads):
    tokens = kv_ref.shape[1] * PAGE
    page_bit = jnp.left_shift(1, lax.broadcasted_iota(jnp.int32, (8, tokens), 1) // PAGE)
    keys = kv_ref[where, :, 0].reshape(tokens, heads * HD)
    values = kv_ref[where, :, 1].reshape(tokens, heads * HD)
    return keys, values, page_masks(bits_ref, core, i, steps, page_bit)


def staged(count, ahead, begin, end):
    begun = [begin(i) for i in range(min(ahead, count))]
    for i in range(count):
        if i + ahead < count:
            begun.append(begin(i + ahead))
        end(i, begun[i])


def first_kernel(heads, bits_ref, new_ref, own_ref, *refs):
    *q_refs, spread_ref, sum_ref, top_ref, total_ref, turned = refs
    steps = q_refs[0].shape[1]
    rows = turned.shape[1]

    def begin(i):
        spread = spread_heads(query_rows(q_refs[i], 0, turned.at[i]), heads)
        spread_ref[i] = spread
        pieces = [page_pieces(own_ref, i, bits_ref, 0, i, steps, heads)]
        if i == 0:
            step_of = lax.broadcasted_iota(jnp.int32, (rows, 16), 0) % steps
            causal = lax.broadcasted_iota(jnp.int32, (rows, 16), 1) <= step_of
            pieces.append((new_ref[0], new_ref[1], causal))
        return attend(spread, pieces)

    def end(i, finish):
        top, total, weighted = finish()
        top_ref[i] = jnp.broadcast_to(top, (rows, 128))
        total_ref[i] = jnp.broadcast_to(total, (rows, 128))
        sum_ref[i] = own_heads(weighted, heads)

    staged(len(q_refs), 1, begin, end)


def second_kernel(
    steps, heads, bits_ref, spread_ref, sum_ref, top_ref, total_ref, other_ref, out_ref
):
    m, rows = spread_ref.shape[:2]
    me = lax.axis_index("ctx")
    columns = []

    def begin(i):
        pieces = [page_pieces(other_ref, me ^ (2 * i), bits_ref, 1, i, steps, heads)]
        return attend(spread_ref[i], pieces)

    def end(i, finish):
        first_top, first_total = top_ref[i], total_ref[i]
        top, total, weighted = finish()
        top = jnp.broadcast_to(top, (rows, 128))
        both = jnp.maximum(top, first_top)
        factor, first_factor = jnp.exp(top - both), jnp.exp(first_top - both)
        total = jnp.broadcast_to(total, (rows, 128)) * factor + first_total * first_factor
        total = jnp.where(total > 0.0, total, 1.0)
        share = 1.0 / total
        joined = own_heads(weighted, heads) * (factor * share)
        joined = joined + sum_ref[i] * (first_factor * share)
        out_ref[i * rows : (i + 1) * rows, :] = joined.astype(jnp.bfloat16)
        columns.append(both + jnp.log(total))

    staged(m, m if m <= 4 else 2, begin, end)
    out_ref[m * rows :, :] = stat_block(columns)


def partials(bits, new_pairs, own_kv, other_kv, queries, rows, heads):
    m, pages = own_kv.shape[:2]
    tokens, width = pages * PAGE, own_kv.shape[4]
    steps = queries[0].shape[1]
    options = dict(
        compiler_params=pltpu.CompilerParams(vmem_limit_bytes=VMEM_LIMIT),
        cost_estimate=pl.CostEstimate(
            flops=4 * m * rows * tokens * width,
            bytes_accessed=2**20,
            transcendentals=m * rows * tokens,
        ),
    )
    state = pl.pallas_call(
        functools.partial(first_kernel, heads),
        out_shape=[
            jax.ShapeDtypeStruct((m, rows, width), jnp.bfloat16),
            jax.ShapeDtypeStruct((m, rows, HD), jnp.float32),
            jax.ShapeDtypeStruct((m, rows, 128), jnp.float32),
            jax.ShapeDtypeStruct((m, rows, 128), jnp.float32),
        ],
        in_specs=[VMEM] * (3 + m),
        out_specs=[VMEM] * 4,
        scratch_shapes=[pltpu.VMEM((m, rows, HD), jnp.float32)],
        **options,
    )(bits, new_pairs, own_kv, *queries)
    return pl.pallas_call(
        functools.partial(second_kernel, steps, heads),
        out_shape=jax.ShapeDtypeStruct((m * rows + stat_rows(m), HD), jnp.bfloat16),
        in_specs=[VMEM] * 6,
        out_specs=VMEM,
        **options,
    )(bits, *state, other_kv)


def last_merge_kernel(rows, steps, *refs):
    *part_refs, _, out_ref = refs
    m = len(part_refs)
    logs = []
    for j, ref in enumerate(part_refs):
        stats = ref[m * rows :, :].astype(jnp.float32)
        log = stats[:m] + stats[m : 2 * m] + stats[2 * m : 3 * m]
        if j:
            log = jnp.concatenate([log[i ^ j : (i ^ j) + 1] for i in range(m)], axis=0)
        logs.append(log)
    top = functools.reduce(jnp.maximum, logs)
    factors = [jnp.exp(log - top) for log in logs]
    share = 1.0 / functools.reduce(jnp.add, factors)
    lane = lax.broadcasted_iota(jnp.int32, (m, 128), 1) // rows
    beside = 128 // rows
    packed = []
    for first in range(0, m, beside):
        wide = jnp.zeros((m, 128), jnp.float32)
        for p in range(min(beside, m - first)):
            weight = factors[first + p] * share
            if p:
                weight = jnp.concatenate(
                    [weight[:, 128 - p * rows :], weight[:, : 128 - p * rows]], axis=1
                )
            wide = jnp.where(lane == p, weight, wide)
        packed.append(wide)
    on_row = lax.broadcasted_iota(jnp.int32, (rows, 128), 0)
    diagonal = lax.broadcasted_iota(jnp.int32, (rows, 128), 1) % rows == on_row
    joined = []
    for i in range(m):
        weights = jnp.concatenate(
            [jnp.where(diagonal, wide[i : i + 1], 0.0) for wide in packed], axis=1
        )
        parts = jnp.concatenate(
            [ref[(i ^ j) * rows : ((i ^ j) + 1) * rows, :] for j, ref in enumerate(part_refs)],
            axis=0,
        )
        high = weights.astype(jnp.bfloat16)
        low = (weights - high.astype(jnp.float32)).astype(jnp.bfloat16)
        both = jnp.concatenate([high, low], axis=0)
        product = jnp.dot(both, parts, preferred_element_type=jnp.float32)
        joined.append(product[:rows] + product[rows:])
    for j in range(rows // steps):
        piece = jnp.concatenate([x[j * steps : (j + 1) * steps] for x in joined], axis=0)
        out_ref[:, j * HD : (j + 1) * HD] = piece.astype(jnp.bfloat16)


def last_merge(parts, weight, rows, steps):
    m = len(parts)
    return pl.pallas_call(
        functools.partial(last_merge_kernel, rows, steps),
        out_shape=jax.ShapeDtypeStruct((m * steps, rows // steps * HD), jnp.bfloat16),
        in_specs=[VMEM] * m + [ANY],
        out_specs=VMEM,
        compiler_params=pltpu.CompilerParams(vmem_limit_bytes=VMEM_LIMIT),
        cost_estimate=pl.CostEstimate(
            flops=2 * m * m * rows * HD, bytes_accessed=2**18, transcendentals=0
        ),
    )(*parts, weight)


def load_kernel(weight_ref, _, out_ref, sems):
    piece = out_ref.shape[0] // WEIGHT_PIECES
    copies = []
    for i in range(WEIGHT_PIECES):
        span = pl.ds(i * piece, piece)
        copy = pltpu.make_async_copy(weight_ref.at[span], out_ref.at[span], sems.at[i])
        copy.start()
        copies.append(copy)
    for copy in copies:
        copy.wait()


def load_weight(out_weight, after):
    return pl.pallas_call(
        load_kernel,
        out_shape=jax.ShapeDtypeStruct(out_weight.shape, out_weight.dtype),
        in_specs=[HBM, ANY],
        out_specs=VMEM,
        scratch_shapes=[pltpu.SemaphoreType.DMA((WEIGHT_PIECES,))],
        compiler_params=pltpu.CompilerParams(vmem_limit_bytes=VMEM_LIMIT),
        cost_estimate=pl.CostEstimate(
            flops=0, bytes_accessed=out_weight.size * 4, transcendentals=0
        ),
    )(pltpu.with_memory_space_constraint(out_weight, pltpu.HBM), after)


def half_kernel(att_ref, weight_ref, out_ref):
    out_ref[...] = jnp.dot(att_ref[...], weight_ref[...], preferred_element_type=jnp.float32)


def project_kernel(n_head, targets, att_ref, half_ref, weight_ref, *refs):
    *out_refs, rows_all = refs
    seqs, steps, _ = out_refs[0].shape
    me = lax.axis_index("ctx")
    mine = lax.axis_index("head")
    for i in range(rows_all.shape[0] // 2):
        rows_all[2 * i + 1, :steps, :] = half_ref[i * steps : (i + 1) * steps, :]
    picks = []
    for k in range(len(out_refs)):
        target = mine
        if k > 0:
            for core, row in enumerate(targets[k - 1]):
                for z, t in enumerate(row):
                    target = jnp.where((me % 2 == core) & (mine == z), t, target)
        picks.append(target)
    product = jnp.dot(att_ref[...], weight_ref[...], preferred_element_type=jnp.float32)
    for i in range(rows_all.shape[0] // 2):
        rows_all[2 * i, :steps, :] = product[i * steps : (i + 1) * steps]
    for k, (ref, target) in enumerate(zip(out_refs, picks)):
        for j in range(seqs):
            found = rows_all[(jnp.maximum(target, 0) * seqs + j) ^ me, :steps]
            if k > 0 and any(t < 0 for row in targets[k - 1] for t in row):
                found = jnp.where(target < 0, 0.0, found)
            ref[j] = found.astype(ref.dtype)


def project_options(att, weight):
    width, columns = weight.shape
    return dict(
        compiler_params=pltpu.CompilerParams(vmem_limit_bytes=VMEM_LIMIT),
        cost_estimate=pl.CostEstimate(
            flops=2 * att.size * columns, bytes_accessed=width * columns * 2, transcendentals=0
        ),
    )


def project_half(att, weight):
    return pl.pallas_call(
        half_kernel,
        out_shape=jax.ShapeDtypeStruct((att.shape[0], weight.shape[1]), jnp.float32),
        in_specs=[VMEM] * 2,
        out_specs=VMEM,
        **project_options(att, weight),
    )(att, weight)


def project(att, half, weight, steps, n_head, targets):
    n = 2 * att.shape[0] // steps
    columns = weight.shape[1]
    outs = [
        jax.ShapeDtypeStruct((n // n_head, steps, columns), jnp.bfloat16 if k else jnp.float32)
        for k in range(1 + len(targets))
    ]
    return pl.pallas_call(
        functools.partial(project_kernel, n_head, targets),
        out_shape=outs,
        in_specs=[VMEM] * 3,
        out_specs=[VMEM] * len(outs),
        scratch_shapes=[pltpu.VMEM((n, 8, columns), jnp.float32)],
        **project_options(att, weight),
    )(att, half, weight)


def head_plan(n_head):
    if n_head == 4:
        return [
            (((1, 0), (1, 1), (0, 0), (1, 3)), ((1, 2), (0, 1), (0, 2), (0, 3))),
            (((0, 1), (0, 2), (0, 3), (0, 0)), ((1, 1), (1, 3), (1, 0), (1, 2))),
            (((0, 3), (0, 0), (0, 1), (0, 2)), ((1, 3), (1, 2), (1, 1), (1, 0))),
            (((0, 2), (0, 3), (1, 2), (0, 1)), ((0, 0), (1, 0), (1, 3), (1, 1))),
        ]
    return [
        tuple(tuple((core, (z + t) % n_head) for z in range(n_head)) for core in range(2))
        for t in range(1, n_head)
    ]


def plan_targets(plan):
    seen = set()
    targets = []
    for permutation in plan:
        rows = []
        for core, row in enumerate(permutation):
            rows.append([])
            for z, (to_core, t) in enumerate(row):
                useful = to_core == core and (core, z, t) not in seen
                rows[core].append(t if useful else -1)
                if useful:
                    seen.add((core, z, t))
        targets.append(rows)
    return targets


def send_by(permutation, x):
    n, n_head = lax.axis_size("ctx"), lax.axis_size("head")
    pairs = []
    for c in range(n):
        for z in range(n_head):
            core, t = permutation[c % 2][z]
            pairs.append((c * n_head + z, (c - c % 2 + core) * n_head + t))
    return lax.ppermute(x, ("ctx", "head"), pairs)


def swap(x, axis, r):
    size = lax.axis_size(axis)
    return lax.ppermute(x, axis, [(i, i ^ r) for i in range(size)])


def swap_chips(x, n):
    return [swap(x, "ctx", r) for r in range(2, n, 2)]


def swap_other_cores(x, n):
    return [swap(x, "ctx", r) for r in range(1, n, 2)]


def local(queries, kv_cache, new_kv, selected, out_weight):
    steps, _, width = queries.shape
    heads = kv_cache.shape[4] // HD
    rows = steps * heads * GROUPS
    n = lax.axis_size("ctx")
    n_head = lax.axis_size("head")

    first_q = queries.reshape(1, steps, width)
    other_kv = swap(kv_cache, "ctx", 1)
    far_q = swap_chips(first_q, n)
    new_pairs = new_kv.reshape(steps, 2, heads * HD)
    own_kv, bits, new_pairs = own_side(kv_cache, selected, new_pairs)
    all_q = [first_q] + far_q
    sent = partials(bits, new_pairs, own_kv, other_kv, all_q, rows, heads)
    parts = swap_other_cores(sent, n)
    weight = load_weight(out_weight, sent)
    odd_att = last_merge(parts, weight, rows, steps)
    even_att = swap(odd_att, "ctx", 1)
    plan = head_plan(n_head)
    half = project_half(odd_att, weight)
    total, *rows_out = project(
        even_att, half, weight, steps, n_head, plan_targets(plan)
    )
    for chunk, permutation in zip(rows_out, plan):
        total = total + send_by(permutation, chunk).astype(jnp.float32)
    return total.astype(jnp.bfloat16)


def solution(mesh):
    return jax.shard_map(
        local,
        mesh=mesh,
        in_specs=(
            P(None, "ctx", "head"),
            P(None, "ctx", None, None, "head"),
            P(None, "ctx", None, "head"),
            P(None, None, "head", None),
            P("head", "ctx"),
        ),
        out_specs=P("head", None, "ctx"),
        check_vma=False,
    )
```

```python
import functools

import jax
import jax.numpy as jnp
from jax import lax
from jax.experimental import pallas as pl
from jax.experimental.pallas import tpu as pltpu
from jax.sharding import PartitionSpec as P

HQ = 64
KVH = 8
HD = 128
PAGE = 64
GROUPS = HQ // KVH
STAT_ROWS = 16
MASKED = -3e38
FLOOR = -1.5e38
WEIGHT_PIECES = 4
VMEM_LIMIT = 24 * 1024 * 1024

VMEM = pl.BlockSpec(memory_space=pltpu.VMEM)
ANY = pl.BlockSpec(memory_space=pl.ANY)
HBM = pl.BlockSpec(memory_space=pltpu.HBM)
NT = (((1,), (1,)), ((), ()))


def query_rows(q_ref, slot, turned):
    steps, width = q_ref.shape[1:]
    for j in range(width // HD):
        piece = q_ref[slot, :, j * HD : (j + 1) * HD]
        turned[j * steps : (j + 1) * steps, :] = piece.astype(jnp.float32)
    return turned[...].astype(jnp.bfloat16)


def spread_heads(query, heads):
    rows = query.shape[0]
    row_head = lax.broadcasted_iota(jnp.int32, (rows, heads * HD), 0) // (rows // heads)
    lane_head = lax.broadcasted_iota(jnp.int32, (rows, heads * HD), 1) // HD
    wide = jnp.concatenate([query] * heads, axis=1)
    return jnp.where(row_head == lane_head, wide, jnp.zeros_like(wide))


def own_heads(weighted, heads):
    span = weighted.shape[0] // heads
    return jnp.concatenate(
        [weighted[h * span : (h + 1) * span, h * HD : (h + 1) * HD] for h in range(heads)], axis=0
    )


def three_parts(x):
    high = x.astype(jnp.bfloat16).astype(jnp.float32)
    rest = x - high
    middle = rest.astype(jnp.bfloat16).astype(jnp.float32)
    return high, middle, rest - middle


def stat_rows(slots):
    return -(-3 * slots // STAT_ROWS) * STAT_ROWS


def stat_block(columns):
    rows = columns[0].shape[0]
    lane = lax.broadcasted_iota(jnp.int32, (rows, 128), 1)
    sheet = jnp.zeros((rows, 128), jnp.float32)
    for i, column in enumerate(columns):
        sheet = jnp.where(lane == i, column, sheet)
    sheet = jnp.concatenate([sheet, jnp.zeros((128 - rows, 128), jnp.float32)], axis=0)
    count = len(columns)
    parts = list(three_parts(jnp.transpose(sheet)[:count]))
    spare = stat_rows(count) - 3 * count
    if spare:
        parts.append(jnp.zeros((spare, 128), jnp.float32))
    return jnp.concatenate(parts, axis=0).astype(jnp.bfloat16)


def own_kernel(
    kv_in, selected_in, new_ref, kv_out, bits_out, new_out, selected_ref, sems
):
    steps, _, heads, _ = selected_ref.shape
    m, pages = kv_out.shape[:2]
    me = lax.axis_index("ctx")
    pairs = [(selected_in, selected_ref)]
    pairs += [(kv_in.at[me ^ (2 * i)], kv_out.at[i]) for i in range(m)]
    copies = [pltpu.make_async_copy(*pair, sems.at[i]) for i, pair in enumerate(pairs)]
    for copy in copies:
        copy.start()
    copies[0].wait()
    by_step = []
    for s in range(steps):
        lists = jnp.concatenate([selected_ref[s, me ^ (2 * i)] for i in range(m)], axis=0)
        for core in range(2):
            page = lists - (me ^ core) * pages
            here = (page >= 0) & (page < pages)
            bit = jnp.where(here, jnp.left_shift(1, page & 31), 0).astype(jnp.float32)
            total = jnp.sum(bit, axis=1, keepdims=True).astype(jnp.int32)
            by_step.append(jnp.broadcast_to(total, (m * heads, 128)))
    step_of = lax.broadcasted_iota(jnp.int32, (8, 128), 0) % steps
    for core in range(2):
        for i in range(m):
            for h in range(heads):
                row = i * heads + h
                bits = jnp.zeros((8, 128), jnp.int32)
                for s in range(steps):
                    bits = jnp.where(step_of == s, by_step[2 * s + core][row : row + 1], bits)
                bits_out[core, i, h] = bits
    for part in range(2):
        tokens = [new_ref[s].astype(jnp.float32)[part : part + 1] for s in range(steps)]
        blank = jnp.zeros((16 - steps, new_ref.shape[2]), jnp.float32)
        new_out[part] = jnp.concatenate(tokens + [blank], axis=0).astype(jnp.bfloat16)
    for copy in copies[1:]:
        copy.wait()


def own_side(kv_cache, selected, new_kv):
    batch, heads = selected.shape[1:3]
    m = batch // 2
    operands = (kv_cache, selected)
    return pl.pallas_call(
        own_kernel,
        out_shape=[
            jax.ShapeDtypeStruct((m,) + kv_cache.shape[1:], kv_cache.dtype),
            jax.ShapeDtypeStruct((2, m, heads, 8, 128), jnp.int32),
            jax.ShapeDtypeStruct((2, 16, new_kv.shape[2]), jnp.bfloat16),
        ],
        in_specs=[HBM, HBM, VMEM],
        out_specs=[VMEM] * 3,
        scratch_shapes=[
            pltpu.VMEM(selected.shape, selected.dtype),
            pltpu.SemaphoreType.DMA((1 + m,)),
        ],
        compiler_params=pltpu.CompilerParams(vmem_limit_bytes=VMEM_LIMIT),
        cost_estimate=pl.CostEstimate(
            flops=2**20, bytes_accessed=kv_cache.size * 2, transcendentals=0
        ),
    )(*[pltpu.with_memory_space_constraint(x, pltpu.HBM) for x in operands], new_kv)


def page_masks(bits_ref, core, i, steps, page_bit):
    masks = []
    for h in range(bits_ref.shape[2]):
        bits = jnp.concatenate([bits_ref[core, i, h]] * (page_bit.shape[1] // 128), axis=1)
        masks += [(page_bit & bits) != 0] * steps
    return jnp.concatenate(masks, axis=0)


def attend(spread, pieces):
    found = []
    for keys, values, allowed in pieces:
        scores = lax.dot_general(spread, keys, NT, preferred_element_type=jnp.float32)
        found.append((jnp.where(allowed, scores * HD ** (-0.5), MASKED), values))

    def finish():
        tops = [jnp.max(scores, axis=1, keepdims=True) for scores, _ in found]
        top = jnp.maximum(functools.reduce(jnp.maximum, tops), FLOOR)
        total, weighted = 0.0, 0.0
        for scores, values in found:
            expo = jnp.exp(scores - top)
            total = total + jnp.sum(expo, axis=1, keepdims=True)
            weighted = weighted + jnp.dot(
                expo.astype(jnp.bfloat16), values, preferred_element_type=jnp.float32
            )
        return top, total, weighted

    return finish


def page_pieces(kv_ref, where, bits_ref, core, i, steps, heads):
    tokens = kv_ref.shape[1] * PAGE
    page_bit = jnp.left_shift(1, lax.broadcasted_iota(jnp.int32, (8, tokens), 1) // PAGE)
    keys = kv_ref[where, :, 0].reshape(tokens, heads * HD)
    values = kv_ref[where, :, 1].reshape(tokens, heads * HD)
    return keys, values, page_masks(bits_ref, core, i, steps, page_bit)


def staged(count, ahead, begin, end):
    begun = [begin(i) for i in range(min(ahead, count))]
    for i in range(count):
        if i + ahead < count:
            begun.append(begin(i + ahead))
        end(i, begun[i])


def first_kernel(heads, bits_ref, new_ref, own_ref, *refs):
    *q_refs, spread_ref, sum_ref, top_ref, total_ref, turned = refs
    steps = q_refs[0].shape[1]
    rows = turned.shape[1]

    def begin(i):
        spread = spread_heads(query_rows(q_refs[i], 0, turned.at[i]), heads)
        spread_ref[i] = spread
        pieces = [page_pieces(own_ref, i, bits_ref, 0, i, steps, heads)]
        if i == 0:
            step_of = lax.broadcasted_iota(jnp.int32, (rows, 16), 0) % steps
            causal = lax.broadcasted_iota(jnp.int32, (rows, 16), 1) <= step_of
            pieces.append((new_ref[0], new_ref[1], causal))
        return attend(spread, pieces)

    def end(i, finish):
        top, total, weighted = finish()
        top_ref[i] = jnp.broadcast_to(top, (rows, 128))
        total_ref[i] = jnp.broadcast_to(total, (rows, 128))
        sum_ref[i] = own_heads(weighted, heads)

    staged(len(q_refs), len(q_refs) if len(q_refs) <= 4 else 2, begin, end)


def second_kernel(
    steps, heads, bits_ref, spread_ref, sum_ref, top_ref, total_ref, other_ref, out_ref
):
    m, rows = spread_ref.shape[:2]
    me = lax.axis_index("ctx")
    columns = []

    def begin(i):
        pieces = [page_pieces(other_ref, me ^ (2 * i), bits_ref, 1, i, steps, heads)]
        return attend(spread_ref[i], pieces)

    def end(i, finish):
        first_top, first_total = top_ref[i], total_ref[i]
        top, total, weighted = finish()
        top = jnp.broadcast_to(top, (rows, 128))
        both = jnp.maximum(top, first_top)
        factor, first_factor = jnp.exp(top - both), jnp.exp(first_top - both)
        total = jnp.broadcast_to(total, (rows, 128)) * factor + first_total * first_factor
        total = jnp.where(total > 0.0, total, 1.0)
        share = 1.0 / total
        joined = own_heads(weighted, heads) * (factor * share)
        joined = joined + sum_ref[i] * (first_factor * share)
        out_ref[i * rows : (i + 1) * rows, :] = joined.astype(jnp.bfloat16)
        columns.append(both + jnp.log(total))

    staged(m, m if m <= 4 else 2, begin, end)
    out_ref[m * rows :, :] = stat_block(columns)


def partials(bits, new_pairs, own_kv, other_kv, queries, rows, heads):
    m, pages = own_kv.shape[:2]
    tokens, width = pages * PAGE, own_kv.shape[4]
    steps = queries[0].shape[1]
    options = dict(
        compiler_params=pltpu.CompilerParams(vmem_limit_bytes=VMEM_LIMIT),
        cost_estimate=pl.CostEstimate(
            flops=4 * m * rows * tokens * width,
            bytes_accessed=2**20,
            transcendentals=m * rows * tokens,
        ),
    )
    state = pl.pallas_call(
        functools.partial(first_kernel, heads),
        out_shape=[
            jax.ShapeDtypeStruct((m, rows, width), jnp.bfloat16),
            jax.ShapeDtypeStruct((m, rows, HD), jnp.float32),
            jax.ShapeDtypeStruct((m, rows, 128), jnp.float32),
            jax.ShapeDtypeStruct((m, rows, 128), jnp.float32),
        ],
        in_specs=[VMEM] * (3 + m),
        out_specs=[VMEM] * 4,
        scratch_shapes=[pltpu.VMEM((m, rows, HD), jnp.float32)],
        **options,
    )(bits, new_pairs, own_kv, *queries)
    return pl.pallas_call(
        functools.partial(second_kernel, steps, heads),
        out_shape=jax.ShapeDtypeStruct((m * rows + stat_rows(m), HD), jnp.bfloat16),
        in_specs=[VMEM] * 6,
        out_specs=VMEM,
        **options,
    )(bits, *state, other_kv)


def last_merge_kernel(rows, steps, *refs):
    *part_refs, _, out_ref = refs
    m = len(part_refs)
    logs = []
    for j, ref in enumerate(part_refs):
        stats = ref[m * rows :, :].astype(jnp.float32)
        log = stats[:m] + stats[m : 2 * m] + stats[2 * m : 3 * m]
        if j:
            log = jnp.concatenate([log[i ^ j : (i ^ j) + 1] for i in range(m)], axis=0)
        logs.append(log)
    top = functools.reduce(jnp.maximum, logs)
    factors = [jnp.exp(log - top) for log in logs]
    share = 1.0 / functools.reduce(jnp.add, factors)
    lane = lax.broadcasted_iota(jnp.int32, (m, 128), 1) // rows
    beside = 128 // rows
    packed = []
    for first in range(0, m, beside):
        wide = jnp.zeros((m, 128), jnp.float32)
        for p in range(min(beside, m - first)):
            weight = factors[first + p] * share
            if p:
                weight = jnp.concatenate(
                    [weight[:, 128 - p * rows :], weight[:, : 128 - p * rows]], axis=1
                )
            wide = jnp.where(lane == p, weight, wide)
        packed.append(wide)
    on_row = lax.broadcasted_iota(jnp.int32, (rows, 128), 0)
    diagonal = lax.broadcasted_iota(jnp.int32, (rows, 128), 1) % rows == on_row
    joined = []
    for i in range(m):
        weights = jnp.concatenate(
            [jnp.where(diagonal, wide[i : i + 1], 0.0) for wide in packed], axis=1
        )
        parts = jnp.concatenate(
            [ref[(i ^ j) * rows : ((i ^ j) + 1) * rows, :] for j, ref in enumerate(part_refs)],
            axis=0,
        )
        high = weights.astype(jnp.bfloat16)
        low = (weights - high.astype(jnp.float32)).astype(jnp.bfloat16)
        both = jnp.concatenate([high, low], axis=0)
        product = jnp.dot(both, parts, preferred_element_type=jnp.float32)
        joined.append(product[:rows] + product[rows:])
    for j in range(rows // steps):
        piece = jnp.concatenate([x[j * steps : (j + 1) * steps] for x in joined], axis=0)
        out_ref[:, j * HD : (j + 1) * HD] = piece.astype(jnp.bfloat16)


def last_merge(parts, weight, rows, steps):
    m = len(parts)
    return pl.pallas_call(
        functools.partial(last_merge_kernel, rows, steps),
        out_shape=jax.ShapeDtypeStruct((m * steps, rows // steps * HD), jnp.bfloat16),
        in_specs=[VMEM] * m + [ANY],
        out_specs=VMEM,
        compiler_params=pltpu.CompilerParams(vmem_limit_bytes=VMEM_LIMIT),
        cost_estimate=pl.CostEstimate(
            flops=2 * m * m * rows * HD, bytes_accessed=2**18, transcendentals=0
        ),
    )(*parts, weight)


def load_kernel(weight_ref, _, out_ref, sems):
    piece = out_ref.shape[0] // WEIGHT_PIECES
    copies = []
    for i in range(WEIGHT_PIECES):
        span = pl.ds(i * piece, piece)
        copy = pltpu.make_async_copy(weight_ref.at[span], out_ref.at[span], sems.at[i])
        copy.start()
        copies.append(copy)
    for copy in copies:
        copy.wait()


def load_weight(out_weight, after):
    return pl.pallas_call(
        load_kernel,
        out_shape=jax.ShapeDtypeStruct(out_weight.shape, out_weight.dtype),
        in_specs=[HBM, ANY],
        out_specs=VMEM,
        scratch_shapes=[pltpu.SemaphoreType.DMA((WEIGHT_PIECES,))],
        compiler_params=pltpu.CompilerParams(vmem_limit_bytes=VMEM_LIMIT),
        cost_estimate=pl.CostEstimate(
            flops=0, bytes_accessed=out_weight.size * 4, transcendentals=0
        ),
    )(pltpu.with_memory_space_constraint(out_weight, pltpu.HBM), after)


def half_kernel(att_ref, weight_ref, out_ref):
    out_ref[...] = jnp.dot(att_ref[...], weight_ref[...], preferred_element_type=jnp.float32)


def project_kernel(n_head, targets, att_ref, half_ref, weight_ref, *refs):
    *out_refs, rows_all = refs
    seqs, steps, _ = out_refs[0].shape
    me = lax.axis_index("ctx")
    mine = lax.axis_index("head")
    for i in range(rows_all.shape[0] // 2):
        rows_all[2 * i + 1, :steps, :] = half_ref[i * steps : (i + 1) * steps, :]
    picks = []
    for k in range(len(out_refs)):
        target = mine
        if k > 0:
            for core, row in enumerate(targets[k - 1]):
                for z, t in enumerate(row):
                    target = jnp.where((me % 2 == core) & (mine == z), t, target)
        picks.append(target)
    product = jnp.dot(att_ref[...], weight_ref[...], preferred_element_type=jnp.float32)
    for i in range(rows_all.shape[0] // 2):
        rows_all[2 * i, :steps, :] = product[i * steps : (i + 1) * steps]
    for k, (ref, target) in enumerate(zip(out_refs, picks)):
        for j in range(seqs):
            found = rows_all[(jnp.maximum(target, 0) * seqs + j) ^ me, :steps]
            if k > 0 and any(t < 0 for row in targets[k - 1] for t in row):
                found = jnp.where(target < 0, 0.0, found)
            ref[j] = found.astype(ref.dtype)


def project_options(att, weight):
    width, columns = weight.shape
    return dict(
        compiler_params=pltpu.CompilerParams(vmem_limit_bytes=VMEM_LIMIT),
        cost_estimate=pl.CostEstimate(
            flops=2 * att.size * columns, bytes_accessed=width * columns * 2, transcendentals=0
        ),
    )


def project_half(att, weight):
    return pl.pallas_call(
        half_kernel,
        out_shape=jax.ShapeDtypeStruct((att.shape[0], weight.shape[1]), jnp.float32),
        in_specs=[VMEM] * 2,
        out_specs=VMEM,
        **project_options(att, weight),
    )(att, weight)


def project(att, half, weight, steps, n_head, targets):
    n = 2 * att.shape[0] // steps
    columns = weight.shape[1]
    outs = [
        jax.ShapeDtypeStruct((n // n_head, steps, columns), jnp.bfloat16 if k else jnp.float32)
        for k in range(1 + len(targets))
    ]
    return pl.pallas_call(
        functools.partial(project_kernel, n_head, targets),
        out_shape=outs,
        in_specs=[VMEM] * 3,
        out_specs=[VMEM] * len(outs),
        scratch_shapes=[pltpu.VMEM((n, 8, columns), jnp.float32)],
        **project_options(att, weight),
    )(att, half, weight)


def head_plan(n_head):
    if n_head == 4:
        return [
            (((1, 0), (1, 1), (0, 0), (1, 3)), ((1, 2), (0, 1), (0, 2), (0, 3))),
            (((0, 1), (0, 2), (0, 3), (0, 0)), ((1, 1), (1, 3), (1, 0), (1, 2))),
            (((0, 3), (0, 0), (0, 1), (0, 2)), ((1, 3), (1, 2), (1, 1), (1, 0))),
            (((0, 2), (0, 3), (1, 2), (0, 1)), ((0, 0), (1, 0), (1, 3), (1, 1))),
        ]
    return [
        tuple(tuple((core, (z + t) % n_head) for z in range(n_head)) for core in range(2))
        for t in range(1, n_head)
    ]


def plan_targets(plan):
    seen = set()
    targets = []
    for permutation in plan:
        rows = []
        for core, row in enumerate(permutation):
            rows.append([])
            for z, (to_core, t) in enumerate(row):
                useful = to_core == core and (core, z, t) not in seen
                rows[core].append(t if useful else -1)
                if useful:
                    seen.add((core, z, t))
        targets.append(rows)
    return targets


def send_by(permutation, x):
    n, n_head = lax.axis_size("ctx"), lax.axis_size("head")
    pairs = []
    for c in range(n):
        for z in range(n_head):
            core, t = permutation[c % 2][z]
            pairs.append((c * n_head + z, (c - c % 2 + core) * n_head + t))
    return lax.ppermute(x, ("ctx", "head"), pairs)


def swap(x, axis, r):
    size = lax.axis_size(axis)
    return lax.ppermute(x, axis, [(i, i ^ r) for i in range(size)])


def swap_chips(x, n):
    return [swap(x, "ctx", r) for r in range(2, n, 2)]


def swap_other_cores(x, n):
    return [swap(x, "ctx", r) for r in range(1, n, 2)]


def local(queries, kv_cache, new_kv, selected, out_weight):
    steps, _, width = queries.shape
    heads = kv_cache.shape[4] // HD
    rows = steps * heads * GROUPS
    n = lax.axis_size("ctx")
    n_head = lax.axis_size("head")

    first_q = queries.reshape(1, steps, width)
    other_kv = swap(kv_cache, "ctx", 1)
    far_q = swap_chips(first_q, n)
    new_pairs = new_kv.reshape(steps, 2, heads * HD)
    own_kv, bits, new_pairs = own_side(kv_cache, selected, new_pairs)
    all_q = [first_q] + far_q
    sent = partials(bits, new_pairs, own_kv, other_kv, all_q, rows, heads)
    parts = swap_other_cores(sent, n)
    weight = load_weight(out_weight, sent)
    odd_att = last_merge(parts, weight, rows, steps)
    even_att = swap(odd_att, "ctx", 1)
    plan = head_plan(n_head)
    half = project_half(odd_att, weight)
    total, *rows_out = project(
        even_att, half, weight, steps, n_head, plan_targets(plan)
    )
    for chunk, permutation in zip(rows_out, plan):
        total = total + send_by(permutation, chunk).astype(jnp.float32)
    return total.astype(jnp.bfloat16)


def solution(mesh):
    return jax.shard_map(
        local,
        mesh=mesh,
        in_specs=(
            P(None, "ctx", "head"),
            P(None, "ctx", None, None, "head"),
            P(None, "ctx", None, "head"),
            P(None, None, "head", None),
            P("head", "ctx"),
        ),
        out_specs=P("head", None, "ctx"),
        check_vma=False,
    )
```
